128 devices in a mesh: row: 8 (over z, core), col: 8 (over x, y_hi), dp: 2 (over y_lo).
Axes of the slice: x: 4, y: 4 (y_hi: 2, y_lo: 2; y = y_hi * 2 + y_lo), z: 4, core: 2. Of those that a mesh axis runs over, the one named last changes fastest.
Arguments:
- tokens: bfloat16 [2048, 8192], P(('col', 'dp'), 'row'), may hold values from -6 to 6
- out_grad: bfloat16 [2048, 8192], P(('col', 'dp'), 'row'), may hold values from -6 to 6
- weight_in: bfloat16 [8192, 16384], P('row', 'col'), may hold values from -0.0625 to 0.0625
- weight_out: bfloat16 [16384, 8192], P('col', 'row'), may hold values from -0.046875 to 0.046875
Outputs:
- mixed: bfloat16 [2048, 8192], P(('col', 'dp'), 'row')
- token_grad: bfloat16 [2048, 8192], P(('col', 'dp'), 'row')
- grad_in: float32 [8192, 16384], P('row', ('col', 'dp'))
- grad_out: float32 [16384, 8192], P(('col', 'dp'), 'row')
The draws below stay inside these ranges and needn't reach their ends.
All inputs are finite; a program needn't handle non-finite values.
Results may differ from the reference program's by a relative error of at most 0.035.
Values may be sent and summed in bfloat16 or wider, within the bound.
No kernel may reach another device: no remote copies, remote signals or barrier semaphores. Data moves between devices by JAX's collectives and lax.ppermute only.
A program may use at most 128 MiB of HBM per device.

```python
import math
import jax
import jax.numpy as jnp
from jax import lax

D = 8192
FF = 16384
TOKENS = 2048
D_PART = 1024
FF_PART = 2048


def steps_of(key, shape, split, least, high):
    def one(position, blocks):
        draws = jax.random.uniform(jax.random.fold_in(jax.random.fold_in(key, 6), position), (blocks,), jnp.float32, least / len(split), high / len(split))
        return jnp.repeat(jnp.exp(draws), shape[position] // blocks).reshape((-1,) + (1,) * (len(shape) - position - 1))

    loudness = one(*split[0])
    for cut in split[1:]:
        loudness = loudness * one(*cut)
    return loudness


def bell_draw(rng, shape, spread, reach, shards=(), dtype=jnp.bfloat16):
    values = spread * jax.random.normal(rng, shape, jnp.float32)
    if shards:
        values = values * steps_of(rng, shape, shards, -0.22, 0.18)
    return jnp.clip(values, -reach, reach).astype(dtype)


def setup_inputs(seed: int = 0) -> dict:
    splits = jax.random.split(jax.random.key(seed), 5)
    tokens = bell_draw(splits[0], (TOKENS, D), 1.0, 6.0, ((0, 16), (1, 8)))
    out_grad = bell_draw(splits[1], (TOKENS, D), 1.0, 6.0, ((0, 16), (1, 8)))
    weight_in = bell_draw(splits[2], (D, FF), D ** -0.5, 0.0625, ((0, 8), (1, 8)))
    weight_out = bell_draw(splits[3], (FF, D), FF ** -0.5, 0.046875, ((0, 8), (1, 8)))
    return {"tokens": tokens, "out_grad": out_grad, "weight_in": weight_in, "weight_out": weight_out}


def gelu_parts(pre):
    cdf = 0.5 * (1.0 + jax.scipy.special.erf(pre * (1.0 / math.sqrt(2.0))))
    activated = pre * cdf
    slope = cdf + pre * jnp.exp(-0.5 * pre * pre) * (1.0 / math.sqrt(2.0 * math.pi))
    return (activated, slope)

def summed_blocks(left, right, width):
    parts = left.shape[1] // width
    total = jnp.zeros((left.shape[0], right.shape[1]), jnp.float32)
    for index in range(parts):
        term = jnp.dot(left[:, index * width:(index + 1) * width], right[index * width:(index + 1) * width], preferred_element_type=jnp.float32)
        rounded = lax.optimization_barrier(term.astype(jnp.bfloat16))
        total = total + rounded.astype(jnp.float32)
    return total

def reference(tokens, out_grad, weight_in, weight_out):
    pre = summed_blocks(tokens, weight_in, D_PART)
    activated, slope = gelu_parts(pre)
    act = activated.astype(jnp.bfloat16)
    mixed = summed_blocks(act, weight_out, FF_PART).astype(jnp.bfloat16)
    back = summed_blocks(out_grad, weight_out.T, D_PART)
    dpre = (back * slope).astype(jnp.bfloat16)
    token_grad = summed_blocks(dpre, weight_in.T, FF_PART).astype(jnp.bfloat16)
    factor = 1.0 / math.sqrt(TOKENS)
    grad_in = jnp.dot(tokens.T, dpre, preferred_element_type=jnp.float32) * factor
    grad_out = jnp.dot(act.T, out_grad, preferred_element_type=jnp.float32) * factor
    return (mixed, token_grad, grad_in, grad_out)
```

```python
import functools
import math

import jax
import jax.numpy as jnp
from jax import lax
from jax.experimental import pallas as pl
from jax.experimental.pallas import tpu as pltpu
from jax.sharding import PartitionSpec as P

AXES = ("row", "col", "dp")
RING = 4
BF = jnp.bfloat16
F32 = jnp.float32
NN = (((1,), (0,)), ((), ()))
NT = (((1,), (1,)), ((), ()))
TN = (((0,), (0,)), ((), ()))


def gelu_parts(pre):
    cdf = 0.5 * (1.0 + jax.scipy.special.erf(pre * (1.0 / math.sqrt(2.0))))
    activated = pre * cdf
    slope = cdf + pre * jnp.exp(-0.5 * pre * pre) * (1.0 / math.sqrt(2.0 * math.pi))
    return (activated, slope)


def flat(z, c, x, y):
    return ((z % RING * 2 + c) * RING + x % RING) * RING + y % RING


def receive(array, source):
    pairs = []
    for z in range(RING):
        for c in range(2):
            for x in range(RING):
                for y in range(RING):
                    pairs.append((flat(*source(z, c, x, y)), flat(z, c, x, y)))
    return lax.ppermute(array, AXES, pairs)


def turn(c, k):
    return k if c == 0 else -k


def along(half, first, step, z, c, x, y):
    if (half == 0) == first:
        return (z, c, x + step, y)
    return (z, c, x, y + step)


def own(c, keep):
    return c if keep else 1 - c


def first_from(array, keep, k):
    def source(z, c, x, y):
        half = own(c, keep)
        return along(half, True, (z + turn(half, k)) % RING, z, c, x, y)

    return receive(array, source)


def first_to(array, keep, k):
    def source(z, c, x, y):
        half = own(c, keep)
        return along(half, True, -((z + turn(half, k)) % RING), z, c, x, y)

    return receive(array, source)


def second_from(array, keep, step):
    return receive(array, lambda z, c, x, y: along(own(c, keep), False, step, z, c, x, y))


def z_from(array, k):
    return receive(array, lambda z, c, x, y: (z + turn(c, k), c, x, y))


def swap(array):
    return receive(array, lambda z, c, x, y: (z, 1 - c, x, y))


def pair_kernel(added, *refs):
    if added:
        a_ref, left_ref, right_ref, more_ref, out_ref = refs
    else:
        a_ref, left_ref, right_ref, out_ref = refs

    def finish(total):
        if added:
            total = total + more_ref[...].astype(F32)
        out_ref[...] = total.astype(BF)

    @pl.when(pl.program_id(0) == 0)
    def _():
        finish(lax.dot_general(a_ref[...], left_ref[...], NN, preferred_element_type=F32))

    @pl.when(pl.program_id(0) == 1)
    def _():
        finish(lax.dot_general(a_ref[...], right_ref[...], NT, preferred_element_type=F32))


def pair_dot(a, left, right, more=None, tile=512):
    rows, depth = a.shape[0], left.shape[0]
    wide = left.shape[1]
    tiles = wide // tile
    in_specs = [
        pl.BlockSpec((rows, depth), lambda h, n: (0, h)),
        pl.BlockSpec((depth, tile), lambda h, n: (0, n * (1 - h) + (tiles - 1) * h)),
        pl.BlockSpec((tile, depth), lambda h, n: (n * h, 0)),
    ]
    args = [a, left, right]
    if more is not None:
        in_specs.append(pl.BlockSpec((rows, tile), lambda h, n: (0, h * tiles + n)))
        args.append(more)
    return pl.pallas_call(
        functools.partial(pair_kernel, more is not None),
        grid=(2, tiles),
        in_specs=in_specs,
        out_specs=pl.BlockSpec((rows, tile), lambda h, n: (0, h * tiles + n)),
        out_shape=jax.ShapeDtypeStruct((rows, 2 * wide), BF),
        compiler_params=pltpu.CompilerParams(vmem_limit_bytes=24 * 2**20),
        cost_estimate=pl.CostEstimate(
            flops=4 * rows * depth * wide,
            bytes_accessed=4 * depth * wide + 8 * rows * wide,
            transcendentals=0,
        ),
    )(*args)


def grad_kernel(count, factor, *refs):
    out_ref = refs[-1]
    total = None
    for i in range(count):
        term = lax.dot_general(
            refs[i][...], refs[count + i][...], TN, preferred_element_type=F32
        )
        total = term if total is None else total + term
    out_ref[...] = total * factor


def grad_dot(lefts, left_part, rights, right_part, factor, tile=256):
    count = len(lefts)
    rows = lefts[0].shape[0]
    wide = lefts[0].shape[1] // 2
    tiles = wide // tile
    return pl.pallas_call(
        functools.partial(grad_kernel, count, factor),
        grid=(tiles,),
        in_specs=[pl.BlockSpec((rows, wide), lambda n: (0, left_part))] * count
        + [pl.BlockSpec((rows, tile), lambda n: (0, right_part * tiles + n))] * count,
        out_specs=pl.BlockSpec((wide, tile), lambda n: (0, n)),
        out_shape=jax.ShapeDtypeStruct((wide, wide), F32),
        compiler_params=pltpu.CompilerParams(vmem_limit_bytes=40 * 2**20),
        cost_estimate=pl.CostEstimate(
            flops=2 * count * rows * wide * wide,
            bytes_accessed=4 * count * rows * wide + 4 * wide * wide,
            transcendentals=0,
        ),
    )(*lefts, *rights)


def total_of(parts):
    total = parts[0].astype(F32)
    for part in parts[1:]:
        total = total + part.astype(F32)
    return total


def shards(tokens, out_grad, weight_in, weight_out):
    core = lax.axis_index("row") % 2
    dp = lax.axis_index("dp")
    block, width = tokens.shape
    half = block // 2
    inner = weight_in.shape[1] // 2
    factor = 1.0 / math.sqrt(block * 16)

    both = jnp.concatenate([tokens, out_grad], axis=1)
    start = {
        True: lax.dynamic_slice_in_dim(both, core * half, half, 0),
        False: lax.dynamic_slice_in_dim(both, (1 - core) * half, half, 0),
    }
    w_in = lax.dynamic_slice_in_dim(weight_in, dp * inner, inner, 1)
    w_out = lax.dynamic_slice_in_dim(weight_out, dp * inner, inner, 0)

    panel = {}
    for keep in (True, False):
        panel[keep, 0] = jnp.concatenate(
            [first_from(start[keep], keep, k) for k in range(RING)], axis=0
        )
    for step in (1, 3, 2):
        for keep in (True, False):
            panel[keep, step] = second_from(panel[keep, 0], keep, step)

    hidden = {}
    partial = {}
    for step in (0, 1, 3, 2):
        sent = pair_dot(panel[False, step], w_in, w_out)
        summed = pair_dot(panel[True, step], w_in, w_out, swap(sent))
        slots = [summed[k * half:(k + 1) * half] for k in range(RING)]
        value = total_of([slots[0]] + [z_from(slots[k], -k) for k in range(1, RING)])
        pre, back = value[:, :width], value[:, width:]
        activated, slope = gelu_parts(pre)
        mine = jnp.concatenate([activated.astype(BF), (back * slope).astype(BF)], axis=1)
        hidden[True, step] = jnp.concatenate(
            [mine] + [z_from(mine, k) for k in range(1, RING)], axis=0
        )
        hidden[False, step] = swap(hidden[True, step])
        for keep in (True, False):
            partial[keep, step] = pair_dot(hidden[keep, step], w_out, w_in)

    done = {}
    for keep in (True, False):
        arrived = [partial[keep, 0]] + [
            second_from(partial[keep, step], keep, -step) for step in (1, 3, 2)
        ]
        near = total_of(arrived).astype(BF)
        done[keep] = total_of(
            [first_to(near[k * half:(k + 1) * half], keep, k) for k in range(RING)]
        ).astype(BF)

    order = [(keep, step) for step in (0, 1, 3, 2) for keep in (True, False)]
    panels = [panel[o] for o in order]
    hiddens = [hidden[o] for o in order]
    grad_in = grad_dot(panels, 0, hiddens, 1, factor)
    grad_out = grad_dot(hiddens, 0, panels, 1, factor)

    low = jnp.where(core == 0, done[True], done[False])
    high = jnp.where(core == 0, done[False], done[True])
    result = jnp.concatenate([low, high], axis=0)
    return (result[:, :width], result[:, width:], grad_in, grad_out)


def solution(mesh):
    placed = (P(("col", "dp"), "row"), P(("col", "dp"), "row"), P("row", "col"), P("col", "row"))
    return jax.shard_map(
        shards,
        mesh=mesh,
        in_specs=placed,
        out_specs=(
            P(("col", "dp"), "row"),
            P(("col", "dp"), "row"),
            P("row", ("col", "dp")),
            P(("col", "dp"), "row"),
        ),
        check_vma=False,
    )
```

```python
import functools
import math

import jax
import jax.numpy as jnp
from jax import lax
from jax.experimental import pallas as pl
from jax.experimental.pallas import tpu as pltpu
from jax.sharding import PartitionSpec as P

AXES = ("row", "col", "dp")
RING = 4
BF = jnp.bfloat16
F32 = jnp.float32
NN = (((1,), (0,)), ((), ()))
NT = (((1,), (1,)), ((), ()))
TN = (((0,), (0,)), ((), ()))


def gelu_parts(pre):
    cdf = 0.5 * (1.0 + jax.scipy.special.erf(pre * (1.0 / math.sqrt(2.0))))
    activated = pre * cdf
    slope = cdf + pre * jnp.exp(-0.5 * pre * pre) * (1.0 / math.sqrt(2.0 * math.pi))
    return (activated, slope)


def flat(z, c, x, y):
    return ((z * 2 + c) * RING + x) * RING + y


def exchange(array, partner):
    pairs = []
    for z in range(RING):
        for c in range(2):
            for x in range(RING):
                for y in range(RING):
                    pairs.append((flat(*partner(z, c, x, y)), flat(z, c, x, y)))
    return lax.ppermute(array, AXES, pairs)


NEAR = ((1, 3), (3, 1))
Z_PAIR = ((1, 3), (3, 1))
OWNER_SLOT = ((0, 2, 3, 1), (0, 1, 3, 2))


def along(keep, first, turn):
    def partner(z, c, x, y):
        half = c if keep else 1 - c
        step = NEAR[c][turn]
        if (half == 0) == first:
            return (z, c, x ^ step, y)
        return (z, c, x, y ^ step)

    return partner


def along_z(turn):
    return lambda z, c, x, y: (z ^ Z_PAIR[c][turn], c, x, y)


def other_core(z, c, x, y):
    return (z, 1 - c, x, y)


def slots_of(keep, z, core):
    def one(c):
        owner = c if keep else 1 - c
        table = jnp.array(OWNER_SLOT[owner], jnp.int32)
        near = NEAR[c]
        arrival = jnp.array([0, near[0], near[1], near[0] ^ near[1]], jnp.int32)
        return table[z ^ arrival]

    return jnp.where(core == 0, one(0), one(1))


def assemble_kernel(slot_ref, a_ref, b_ref, c_ref, out_ref):
    rows = a_ref.shape[0]

    def put(i, value):
        out_ref[pl.ds(pl.multiple_of(slot_ref[i] * rows, rows), rows), :] = value

    put(0, a_ref[...])
    put(1, b_ref[...])
    put(2, c_ref[:rows, :])
    put(3, c_ref[rows:, :])


def assemble(slots, a, b, c):
    rows, wide = a.shape
    tiles = 2
    spec = lambda n: pl.BlockSpec((n, wide // tiles), lambda i, slot: (0, i))
    return pl.pallas_call(
        assemble_kernel,
        grid_spec=pltpu.PrefetchScalarGridSpec(
            num_scalar_prefetch=1,
            grid=(tiles,),
            in_specs=[spec(rows), spec(rows), spec(2 * rows)],
            out_specs=spec(4 * rows),
        ),
        out_shape=jax.ShapeDtypeStruct((4 * rows, wide), BF),
        cost_estimate=pl.CostEstimate(flops=0, bytes_accessed=16 * rows * wide, transcendentals=0),
    )(slots, a, b, c)


def pair_kernel(pieces, added, split, ordered, block, slot_ref, *refs):
    a_refs, rest = refs[:pieces], refs[pieces:]
    left_ref, right_ref = rest[:2]
    rest = rest[2:]
    if added:
        more_ref, rest = rest[0], rest[1:]

    def rows_of():
        values = []
        for a_ref in a_refs:
            for i in range(a_ref.shape[0] // (4 * block)):
                if ordered:
                    for j in range(4):
                        first = pl.multiple_of(slot_ref[j] * block, block)
                        values.append(a_ref[pl.ds(i * 4 * block + first, block), :])
                else:
                    values.append(a_ref[i * 4 * block:(i + 1) * 4 * block, :])
        return values[0] if len(values) == 1 else jnp.concatenate(values, axis=0)

    def finish(total):
        if added:
            total = total + more_ref[...].astype(F32)
        total = total.astype(BF)
        if not split:
            rest[0][...] = total
            return
        two = 2 * block
        for i in range(total.shape[0] // (2 * two)):
            rest[0][i * two:(i + 1) * two, :] = total[2 * i * two:(2 * i + 1) * two]
            rest[1][i * two:(i + 1) * two, :] = total[(2 * i + 1) * two:(2 * i + 2) * two]

    @pl.when(pl.program_id(0) == 0)
    def _():
        finish(lax.dot_general(rows_of(), left_ref[...], NN, preferred_element_type=F32))

    @pl.when(pl.program_id(0) == 1)
    def _():
        finish(lax.dot_general(rows_of(), right_ref[...], NT, preferred_element_type=F32))


def pair_dot(pieces, left, right, slots, block, more=None, split=False, ordered=False, tile=512):
    rows = sum(a.shape[0] for a in pieces)
    depth, wide = left.shape
    tiles = wide // tile
    in_specs = [pl.BlockSpec((a.shape[0], depth), lambda h, n, slot: (0, h)) for a in pieces]
    in_specs += [
        pl.BlockSpec((depth, tile), lambda h, n, slot: (0, n * (1 - h) + (tiles - 1) * h)),
        pl.BlockSpec((tile, depth), lambda h, n, slot: (n * h, 0)),
    ]
    out_of = lambda n_rows: pl.BlockSpec((n_rows, tile), lambda h, n, slot: (0, h * tiles + n))
    args = [*pieces, left, right]
    if more is not None:
        in_specs.append(out_of(rows))
        args.append(more)
    outs = [rows // 2, rows // 2] if split else [rows]
    result = pl.pallas_call(
        functools.partial(pair_kernel, len(pieces), more is not None, split, ordered, block),
        grid_spec=pltpu.PrefetchScalarGridSpec(
            num_scalar_prefetch=1,
            grid=(2, tiles),
            in_specs=in_specs,
            out_specs=[out_of(n) for n in outs],
        ),
        out_shape=[jax.ShapeDtypeStruct((n, 2 * wide), BF) for n in outs],
        compiler_params=pltpu.CompilerParams(vmem_limit_bytes=24 * 2**20),
        cost_estimate=pl.CostEstimate(
            flops=4 * rows * depth * wide,
            bytes_accessed=4 * depth * wide + 8 * rows * wide,
            transcendentals=0,
        ),
    )(slots, *args)
    return result if split else result[0]


def grad_kernel(left_count, pairs, factor, *refs):
    lefts, rights, out_ref = refs[:left_count], refs[left_count:-1], refs[-1]
    total = None
    for i, first, j, second, rows in pairs:
        term = lax.dot_general(
            lefts[i][first:first + rows, :],
            rights[j][second:second + rows, :],
            TN,
            preferred_element_type=F32,
        )
        total = term if total is None else total + term
    out_ref[...] = total * factor


def grad_dot(lefts, left_part, rights, right_part, pairs, factor, tile=256):
    wide = lefts[0].shape[1] // 2
    tiles = wide // tile
    tokens = sum(a.shape[0] for a in lefts)
    return pl.pallas_call(
        functools.partial(grad_kernel, len(lefts), pairs, factor),
        grid=(tiles,),
        in_specs=[pl.BlockSpec((a.shape[0], wide), lambda n: (0, left_part)) for a in lefts]
        + [pl.BlockSpec((a.shape[0], tile), lambda n: (0, right_part * tiles + n)) for a in rights],
        out_specs=pl.BlockSpec((wide, tile), lambda n: (0, n)),
        out_shape=jax.ShapeDtypeStruct((wide, wide), F32),
        compiler_params=pltpu.CompilerParams(vmem_limit_bytes=40 * 2**20),
        cost_estimate=pl.CostEstimate(
            flops=2 * tokens * wide * wide,
            bytes_accessed=4 * tokens * wide + 4 * wide * wide,
            transcendentals=0,
        ),
    )(*lefts, *rights)


def blocks_of(array, count, block):
    pieces = array.shape[0] // (count * block)
    cut = array.reshape(pieces, count, block, array.shape[1])
    return [cut[:, i].reshape(pieces * block, array.shape[1]) for i in range(count)]


def shards(tokens, out_grad, weight_in, weight_out):
    core = lax.axis_index("row") % 2
    z = lax.axis_index("row") // 2
    dp = lax.axis_index("dp")
    rows, width = tokens.shape
    block = rows // 2
    inner = weight_in.shape[1] // 2
    factor = 1.0 / math.sqrt(rows * 16)
    both_ways = (True, False)

    both = jnp.concatenate([tokens, out_grad], axis=1)
    slots = {keep: slots_of(keep, z, core) for keep in both_ways}
    w_in = lax.dynamic_slice_in_dim(weight_in, dp * inner, inner, 1)
    w_out = lax.dynamic_slice_in_dim(weight_out, dp * inner, inner, 0)

    panel = {}
    one, two = {}, {}
    start = {
        True: lax.dynamic_slice_in_dim(both, core * block, block, 0),
        False: lax.dynamic_slice_in_dim(both, (1 - core) * block, block, 0),
    }
    for keep in both_ways:
        one[keep] = exchange(start[keep], along(keep, True, 0))
    for keep in both_ways:
        pair = jnp.concatenate([start[keep], one[keep]], axis=0)
        two[keep] = exchange(pair, along(keep, True, 1))
    for keep in both_ways:
        panel[keep, 0] = assemble(slots[keep], start[keep], one[keep], two[keep])
    for keep in both_ways:
        panel[keep, 1] = exchange(panel[keep, 0], along(keep, False, 0))
    for keep in both_ways:
        panel[keep, 2] = exchange(panel[keep, 0], along(keep, False, 1))
    for keep in both_ways:
        panel[keep, 3] = exchange(panel[keep, 1], along(keep, False, 1))

    batches = {True: ((0,), (1, 2), (3,)), False: ((0,), (2, 1), (3,))}
    hidden = {}
    summed = {}
    for b in range(3):
        sent = pair_dot(
            [panel[False, p] for p in batches[False][b]], w_in, w_out, slots[False], block
        )
        kept, passed = pair_dot(
            [panel[True, p] for p in batches[True][b]],
            w_in,
            w_out,
            slots[True],
            block,
            more=exchange(sent, other_core),
            split=True,
        )
        got = exchange(passed, along_z(0))
        kept, got = blocks_of(kept, 2, block), blocks_of(got, 2, block)
        halfway = [kept[i].astype(F32) + got[i].astype(F32) for i in range(2)]
        value = halfway[0] + exchange(halfway[1].astype(BF), along_z(1)).astype(F32)
        pre, back = value[:, :width], value[:, width:]
        activated, slope = gelu_parts(pre)
        mine = jnp.concatenate([activated.astype(BF), (back * slope).astype(BF)], axis=1)
        pair = jnp.concatenate([mine, exchange(mine, along_z(1))], axis=0)
        other = exchange(pair, along_z(0))
        count = len(batches[True][b])
        hidden[True, b] = jnp.concatenate(
            [a.reshape(2, count, block, 2 * width) for a in (pair, other)], axis=0
        ).transpose(1, 0, 2, 3).reshape(4 * count * block, 2 * width)
        hidden[False, b] = exchange(hidden[True, b], other_core)

        for keep in both_ways:
            kept, passed = pair_dot(
                [hidden[keep, b]], w_out, w_in, slots[keep], block, split=True, ordered=True
            )
            got = exchange(passed, along(keep, True, 1))
            kept, got = blocks_of(kept, 2, block), blocks_of(got, 2, block)
            halfway = [kept[i].astype(F32) + got[i].astype(F32) for i in range(2)]
            total = halfway[0] + exchange(
                halfway[1].astype(BF), along(keep, True, 0)
            ).astype(F32)
            for i, p in enumerate(batches[keep][b]):
                summed[keep, p] = total[i * block:(i + 1) * block]

    done = {}
    for keep in both_ways:
        passed = jnp.concatenate([summed[keep, 2], summed[keep, 3]], axis=0).astype(BF)
        got = exchange(passed, along(keep, False, 1)).astype(F32)
        last = (summed[keep, 1] + got[block:]).astype(BF)
        done[keep] = (
            summed[keep, 0] + got[:block] + exchange(last, along(keep, False, 0)).astype(F32)
        ).astype(BF)

    panels, hiddens, in_pairs, out_pairs = [], [], [], []
    for keep in both_ways:
        for b in range(3):
            for i, p in enumerate(batches[keep][b]):
                in_pairs.append((len(panels), 0, len(hiddens), i * 4 * block, 4 * block))
                out_pairs.append((len(hiddens), i * 4 * block, len(panels), 0, 4 * block))
                panels.append(panel[keep, p])
            hiddens.append(hidden[keep, b])
    grad_in = grad_dot(panels, 0, hiddens, 1, in_pairs, factor)
    grad_out = grad_dot(hiddens, 0, panels, 1, out_pairs, factor)

    low = jnp.where(core == 0, done[True], done[False])
    high = jnp.where(core == 0, done[False], done[True])
    result = jnp.concatenate([low, high], axis=0)
    return (result[:, :width], result[:, width:], grad_in, grad_out)


def solution(mesh):
    placed = (P(("col", "dp"), "row"), P(("col", "dp"), "row"), P("row", "col"), P("col", "row"))
    return jax.shard_map(
        shards,
        mesh=mesh,
        in_specs=placed,
        out_specs=(
            P(("col", "dp"), "row"),
            P(("col", "dp"), "row"),
            P("row", ("col", "dp")),
            P(("col", "dp"), "row"),
        ),
        check_vma=False,
    )
```

```python
import functools
import math

import jax
import jax.numpy as jnp
from jax import lax
from jax.experimental import pallas as pl
from jax.experimental.pallas import tpu as pltpu
from jax.sharding import PartitionSpec as P

AXES = ("row", "col", "dp")
RING = 4
BF = jnp.bfloat16
F32 = jnp.float32
NN = (((1,), (0,)), ((), ()))
NT = (((1,), (1,)), ((), ()))
TN = (((0,), (0,)), ((), ()))


def cost(flops, bytes_accessed, transcendentals):
    return pl.CostEstimate(
        flops=flops // 100, bytes_accessed=bytes_accessed // 100, transcendentals=transcendentals
    )


def gelu_parts(pre):
    cdf = 0.5 * (1.0 + jax.scipy.special.erf(pre * (1.0 / math.sqrt(2.0))))
    activated = pre * cdf
    slope = cdf + pre * jnp.exp(-0.5 * pre * pre) * (1.0 / math.sqrt(2.0 * math.pi))
    return (activated, slope)


def flat(z, c, x, y):
    return ((z * 2 + c) * RING + x) * RING + y


def exchange(array, partner):
    pairs = []
    for z in range(RING):
        for c in range(2):
            for x in range(RING):
                for y in range(RING):
                    pairs.append((flat(*partner(z, c, x, y)), flat(z, c, x, y)))
    return lax.ppermute(array, AXES, pairs)


NEAR = ((1, 3), (3, 1))
Z_PAIR = ((1, 3), (3, 1))
OWNER_SLOT = ((0, 2, 3, 1), (0, 1, 3, 2))


def along(keep, first, turn):
    def partner(z, c, x, y):
        half = c if keep else 1 - c
        step = NEAR[c][turn]
        if (half == 0) == first:
            return (z, c, x ^ step, y)
        return (z, c, x, y ^ step)

    return partner


def along_z(turn):
    return lambda z, c, x, y: (z ^ Z_PAIR[c][turn], c, x, y)


def other_core(z, c, x, y):
    return (z, 1 - c, x, y)


def slot_of(keep, place_ref, i):
    z, core = place_ref[0], place_ref[1]

    def one(c):
        near = NEAR[c]
        owned = z ^ (0, near[0], near[1], near[0] ^ near[1])[i]
        table = OWNER_SLOT[c if keep else 1 - c]
        slot = jnp.int32(table[0])
        for j in range(1, RING):
            slot = jnp.where(owned == j, table[j], slot)
        return slot

    return jnp.where(core == 0, one(0), one(1))


def cut_kernel(place_ref, tokens_ref, grad_ref, kept_ref, passed_ref):
    block, wide = kept_ref.shape[0], tokens_ref.shape[1]
    core = place_ref[1]
    for ref, which in ((kept_ref, core), (passed_ref, 1 - core)):
        rows = pl.ds(pl.multiple_of(which * block, block), block)
        ref[:, :wide] = tokens_ref[rows, :]
        ref[:, wide:] = grad_ref[rows, :]


def cut(place, tokens, out_grad):
    rows, wide = tokens.shape
    half = jax.ShapeDtypeStruct((rows // 2, 2 * wide), BF)
    return pl.pallas_call(
        cut_kernel,
        grid_spec=pltpu.PrefetchScalarGridSpec(
            num_scalar_prefetch=1,
            grid=(1,),
            in_specs=[pl.BlockSpec((rows, wide), lambda i, place: (0, 0))] * 2,
            out_specs=[pl.BlockSpec((rows // 2, 2 * wide), lambda i, place: (0, 0))] * 2,
        ),
        out_shape=[half, half],
        cost_estimate=cost(flops=0, bytes_accessed=8 * rows * wide, transcendentals=0),
    )(place, tokens, out_grad)


def assemble_kernel(keep, place_ref, a_ref, b_ref, c_ref, out_ref):
    rows = a_ref.shape[0]

    def put(i, value):
        out_ref[pl.ds(pl.multiple_of(slot_of(keep, place_ref, i) * rows, rows), rows), :] = value

    put(0, a_ref[...])
    put(1, b_ref[...])
    put(2, c_ref[:rows, :])
    put(3, c_ref[rows:, :])


def assemble(keep, place, a, b, c):
    rows, wide = a.shape
    tiles = 2
    spec = lambda n: pl.BlockSpec((n, wide // tiles), lambda i, place: (0, i))
    return pl.pallas_call(
        functools.partial(assemble_kernel, keep),
        grid_spec=pltpu.PrefetchScalarGridSpec(
            num_scalar_prefetch=1,
            grid=(tiles,),
            in_specs=[spec(rows), spec(rows), spec(2 * rows)],
            out_specs=spec(4 * rows),
        ),
        out_shape=jax.ShapeDtypeStruct((4 * rows, wide), BF),
        cost_estimate=cost(flops=0, bytes_accessed=16 * rows * wide, transcendentals=0),
    )(place, a, b, c)


def pair_kernel(pieces, added, split, keep, block, place_ref, *refs):
    a_refs, rest = refs[:pieces], refs[pieces:]
    left_ref, right_ref = rest[:2]
    rest = rest[2:]
    if added:
        more_ref, rest = rest[0], rest[1:]

    def rows_of():
        if keep is None:
            values = [a_ref[...] for a_ref in a_refs]
        else:
            size = a_refs[0].shape[0] // RING
            values = [
                a_refs[0][pl.ds(pl.multiple_of(slot_of(keep, place_ref, i) * size, size), size), :]
                for i in range(RING)
            ]
        return values[0] if len(values) == 1 else jnp.concatenate(values, axis=0)

    def finish(total):
        if added:
            total = total + more_ref[...].astype(F32)
        total = total.astype(BF)
        if not split:
            rest[0][...] = total
        elif keep is not None or pieces == 1:
            half = total.shape[0] // 2
            rest[0][...] = total[:half]
            rest[1][...] = total[half:]
        else:
            for i in range(RING):
                for j in range(pieces):
                    first = (j * RING + i) * block
                    at = ((i % 2) * pieces + j) * block
                    rest[i // 2][at:at + block, :] = total[first:first + block]

    @pl.when(pl.program_id(0) == 0)
    def _():
        finish(lax.dot_general(rows_of(), left_ref[...], NN, preferred_element_type=F32))

    @pl.when(pl.program_id(0) == 1)
    def _():
        finish(lax.dot_general(rows_of(), right_ref[...], NT, preferred_element_type=F32))


def pair_dot(pieces, left, right, place, block, more=None, split=False, keep=None, tile=512):
    rows = sum(a.shape[0] for a in pieces)
    depth, wide = left.shape
    tiles = wide // tile
    in_specs = [pl.BlockSpec((a.shape[0], depth), lambda h, n, place: (0, h)) for a in pieces]
    in_specs += [
        pl.BlockSpec((depth, tile), lambda h, n, place: (0, n * (1 - h) + (tiles - 1) * h)),
        pl.BlockSpec((tile, depth), lambda h, n, place: (n * h, 0)),
    ]
    out_of = lambda n_rows: pl.BlockSpec((n_rows, tile), lambda h, n, place: (0, h * tiles + n))
    args = [*pieces, left, right]
    if more is not None:
        in_specs.append(out_of(rows))
        args.append(more)
    outs = [rows // 2, rows // 2] if split else [rows]
    result = pl.pallas_call(
        functools.partial(pair_kernel, len(pieces), more is not None, split, keep, block),
        grid_spec=pltpu.PrefetchScalarGridSpec(
            num_scalar_prefetch=1,
            grid=(2, tiles),
            in_specs=in_specs,
            out_specs=[out_of(n) for n in outs],
        ),
        out_shape=[jax.ShapeDtypeStruct((n, 2 * wide), BF) for n in outs],
        compiler_params=pltpu.CompilerParams(vmem_limit_bytes=24 * 2**20),
        cost_estimate=cost(
            flops=4 * rows * depth * wide,
            bytes_accessed=4 * depth * wide + 8 * rows * wide,
            transcendentals=0,
        ),
    )(place, *args)
    return result if split else result[0]


def stacked(refs):
    if len(refs) == 1:
        return refs[0][...]
    block = refs[0].shape[0] // RING
    return jnp.concatenate(
        [ref[i * block:(i + 1) * block, :] for i in range(RING) for ref in refs], axis=0
    )


def grad_kernel(left_count, right_count, pairs, factor, *refs):
    lefts, rights, out_ref = refs[:left_count], refs[left_count:left_count + right_count], refs[-1]
    total = None
    for left, right in pairs:
        term = lax.dot_general(
            stacked([lefts[i] for i in left]),
            stacked([rights[i] for i in right]),
            TN,
            preferred_element_type=F32,
        )
        total = term if total is None else total + term
    out_ref[...] = total * factor


def grad_dot(lefts, left_part, rights, right_part, pairs, factor, begun=None, tile=256):
    wide = lefts[0].shape[1] // 2
    tiles = wide // tile // 2
    skip = 0 if begun is None else tiles
    base = right_part * 2 * tiles + skip
    tokens = sum(a.shape[0] for a in lefts)
    args = [*lefts, *rights]
    in_specs = [pl.BlockSpec((a.shape[0], wide), lambda n: (0, left_part)) for a in lefts]
    in_specs += [pl.BlockSpec((a.shape[0], tile), lambda n: (0, base + n)) for a in rights]
    aliases = {}
    if begun is not None:
        aliases = {len(args): 0}
        args.append(begun)
        in_specs.append(pl.BlockSpec(memory_space=pl.ANY))
    return pl.pallas_call(
        functools.partial(grad_kernel, len(lefts), len(rights), pairs, factor),
        grid=(tiles,),
        in_specs=in_specs,
        out_specs=pl.BlockSpec((wide, tile), lambda n: (0, skip + n)),
        out_shape=jax.ShapeDtypeStruct((wide, wide), F32),
        input_output_aliases=aliases,
        compiler_params=pltpu.CompilerParams(vmem_limit_bytes=40 * 2**20),
        cost_estimate=cost(
            flops=tokens * wide * wide,
            bytes_accessed=3 * tokens * wide + 2 * wide * wide,
            transcendentals=0,
        ),
    )(*args)


def after(value, *events):
    return lax.optimization_barrier((value, *events))[0]


def shards(tokens, out_grad, weight_in, weight_out):
    core = lax.axis_index("row") % 2
    z = lax.axis_index("row") // 2
    dp = lax.axis_index("dp")
    rows, width = tokens.shape
    block = rows // 2
    inner = weight_in.shape[1] // 2
    factor = 1.0 / math.sqrt(rows * 16)
    both_ways = (True, False)

    place = jnp.stack([z, core]).astype(jnp.int32)
    w_in = lax.dynamic_slice_in_dim(weight_in, dp * inner, inner, 1)
    w_out = lax.dynamic_slice_in_dim(weight_out, dp * inner, inner, 0)

    panel = {}
    start, one, two = {}, {}, {}
    start[True], start[False] = cut(place, tokens, out_grad)
    order = (False, True)
    for keep in order:
        one[keep] = exchange(start[keep], along(keep, True, 0))
    for keep in order:
        pair = jnp.concatenate([start[keep], one[keep]], axis=0)
        two[keep] = exchange(pair, along(keep, True, 1))
    for keep in order:
        panel[keep, 0] = assemble(keep, place, start[keep], one[keep], two[keep])
    panel[True, 0], panel[False, 0] = lax.optimization_barrier((panel[True, 0], panel[False, 0]))
    for keep in order:
        panel[keep, 1] = exchange(panel[keep, 0], along(keep, False, 0))
    for keep in order:
        panel[keep, 2] = exchange(panel[keep, 0], along(keep, False, 1))
    for keep in order:
        panel[keep, 3] = exchange(panel[keep, 1], along(keep, False, 1))

    batches = {True: ((0,), (1, 2), (3,)), False: ((0,), (2, 1), (3,))}

    def passed_dot(b, *events):
        pieces = [panel[False, p] for p in batches[False][b]]
        pieces[0] = after(pieces[0], *events)
        return pair_dot(pieces, w_in, w_out, place, block)

    def kept_dot(b, got, *events):
        pieces = [panel[True, p] for p in batches[True][b]]
        got = after(got, *events) if events else got
        return pair_dot(pieces, w_in, w_out, place, block, more=got, split=True)

    def halfway(kept, got):
        half = kept.shape[0] // 2
        sums = kept.astype(F32) + got.astype(F32)
        return [sums[:half], sums[half:]]

    def hidden_of(value):
        pre, back = value[:, :width], value[:, width:]
        activated, slope = gelu_parts(pre)
        return jnp.concatenate([activated.astype(BF), (back * slope).astype(BF)], axis=1)

    def joined(pair, other):
        return jnp.concatenate([pair, other], axis=0)

    def out_dot(keep, b, *events):
        value = hidden[keep, b]
        value = after(value, *events) if events else value
        return pair_dot([value], w_out, w_in, place, block, split=True, keep=keep)

    def first_half(keep, kept, passed):
        return halfway(kept, exchange(passed, along(keep, True, 1)))

    def first_sum(keep, sums, *events):
        passed = sums[1].astype(BF)
        passed = after(passed, *events) if events else passed
        return sums[0] + exchange(passed, along(keep, True, 0)).astype(F32)

    hidden, firsts, summed = {}, {}, {}

    sent0 = passed_dot(0)
    kept0, send0 = kept_dot(0, exchange(sent0, other_core))
    half0 = halfway(kept0, exchange(send0, along_z(0)))
    turned = after(half0[1].astype(BF), *(panel[keep, p] for keep in order for p in (1, 2)))
    mine0 = hidden_of(half0[0] + exchange(turned, along_z(1)).astype(F32))
    next0 = exchange(mine0, along_z(1))

    sent1 = passed_dot(1, turned)
    got1 = exchange(sent1, other_core)
    pair0 = jnp.concatenate([mine0, next0], axis=0)
    far0 = exchange(pair0, along_z(0))
    kept1, send1 = kept_dot(1, got1, pair0)
    send1 = after(send1, panel[True, 3], panel[False, 3])
    step1 = exchange(send1, along_z(0))

    hidden[True, 0] = joined(after(pair0, send1), far0)
    hidden[False, 0] = exchange(hidden[True, 0], other_core)
    sent2 = passed_dot(2, hidden[True, 0])
    got2 = exchange(sent2, other_core)
    out_kept0 = out_dot(True, 0, sent2)
    kept2, send2 = kept_dot(2, got2, out_kept0[0])
    step2 = exchange(send2, along_z(0))
    out_passed0 = out_dot(False, 0, send2)

    half1 = halfway(kept1, step1)
    turned1 = after(half1[1].astype(BF), out_passed0[0])
    value1 = half1[0] + exchange(turned1, along_z(1)).astype(F32)
    half2 = halfway(kept2, step2)
    mine1 = hidden_of(value1)
    own_kept = first_half(True, *out_kept0)
    own_passed = first_half(False, *out_passed0)
    next1 = exchange(after(mine1, own_kept[0], own_passed[0]), along_z(1))
    mine2 = hidden_of(half2[0] + exchange(half2[1].astype(BF), along_z(1)).astype(F32))
    next2 = exchange(mine2, along_z(1))
    firsts[True, 0] = first_sum(True, own_kept)
    firsts[False, 0] = first_sum(False, own_passed)
    pair1 = after(jnp.concatenate([mine1, next1], axis=0), firsts[True, 0], firsts[False, 0])
    far1 = exchange(pair1, along_z(0))
    pair2 = jnp.concatenate([mine2, next2], axis=0)
    far2 = exchange(pair2, along_z(0))

    hidden[True, 1] = joined(pair1, far1)
    hidden[False, 1] = exchange(hidden[True, 1], other_core)
    out_kept1 = out_dot(True, 1)
    hidden[True, 2] = joined(after(pair2, out_kept1[0]), far2)
    hidden[False, 2] = exchange(hidden[True, 2], other_core)
    out_passed1 = out_dot(False, 1, hidden[True, 2])
    half_kept1 = first_half(True, *out_kept1)
    out_kept2 = out_dot(True, 2, out_passed1[0])
    half_passed1 = first_half(False, *out_passed1)
    out_passed2 = out_dot(False, 2, out_kept2[0])

    panels, hiddens, in_pairs, out_pairs = [], [], [], []
    for keep in both_ways:
        for b in range(3):
            numbers = tuple(range(len(panels), len(panels) + len(batches[keep][b])))
            in_pairs.append((numbers, (len(hiddens),)))
            out_pairs.append(((len(hiddens),), numbers))
            panels += [panel[keep, p] for p in batches[keep][b]]
            hiddens.append(hidden[keep, b])

    def grads(which, begun, *events):
        if which == 0:
            lefts, rights, parts, pairs = panels, list(hiddens), (0, 1), in_pairs
        else:
            lefts, rights, parts, pairs = hiddens, list(panels), (0, 1), out_pairs
        rights[0] = after(rights[0], *events)
        return grad_dot(lefts, parts[0], rights, parts[1], pairs, factor, begun)

    firsts[True, 1] = first_sum(True, half_kept1)
    firsts[False, 1] = first_sum(False, half_passed1)
    grad_in = grads(0, None, out_passed2[0])
    half_kept2 = first_half(True, *out_kept2)
    half_passed2 = first_half(False, *out_passed2)
    firsts[True, 2] = first_sum(True, half_kept2, grad_in)
    firsts[False, 2] = first_sum(False, half_passed2, grad_in)
    grad_in = grads(0, grad_in, half_kept2[0], half_passed2[0])
    for keep in both_ways:
        for b in range(3):
            for i, p in enumerate(batches[keep][b]):
                summed[keep, p] = firsts[keep, b][i * block:(i + 1) * block]
    lasts, gots = {}, {}
    for keep in both_ways:
        passed = jnp.concatenate([summed[keep, 2], summed[keep, 3]], axis=0).astype(BF)
        passed = after(passed, grad_in)
        gots[keep] = exchange(passed, along(keep, False, 1))
    grad_out = grads(1, None, grad_in)
    done = {}
    for keep in both_ways:
        got = gots[keep].astype(F32)
        last = after((summed[keep, 1] + got[block:]).astype(BF), grad_out)
        lasts[keep] = exchange(last, along(keep, False, 0))
    grad_out = grads(1, grad_out, gots[True], gots[False])
    for keep in both_ways:
        got = gots[keep].astype(F32)
        got_last = after(lasts[keep], grad_out)
        done[keep] = (summed[keep, 0] + got[:block] + got_last.astype(F32)).astype(BF)

    low = jnp.where(core == 0, done[True], done[False])
    high = jnp.where(core == 0, done[False], done[True])
    result = jnp.concatenate([low, high], axis=0)
    return (result[:, :width], result[:, width:], grad_in, grad_out)


def solution(mesh):
    placed = (P(("col", "dp"), "row"), P(("col", "dp"), "row"), P("row", "col"), P("col", "row"))
    return jax.shard_map(
        shards,
        mesh=mesh,
        in_specs=placed,
        out_specs=(
            P(("col", "dp"), "row"),
            P(("col", "dp"), "row"),
            P("row", ("col", "dp")),
            P(("col", "dp"), "row"),
        ),
        check_vma=False,
    )
```

```python
import functools
import math

import jax
import jax.numpy as jnp
from jax import lax
from jax.experimental import pallas as pl
from jax.experimental.pallas import tpu as pltpu
from jax.sharding import PartitionSpec as P

AXES = ("row", "col", "dp")
RING = 4
PARTS = 2
BF = jnp.bfloat16
F32 = jnp.float32
NN = (((1,), (0,)), ((), ()))
NT = (((1,), (1,)), ((), ()))
TN = (((0,), (0,)), ((), ()))


def cost(flops, bytes_accessed, transcendentals):
    return pl.CostEstimate(
        flops=flops // 100, bytes_accessed=bytes_accessed // 100, transcendentals=transcendentals
    )


def gelu_parts(pre):
    cdf = 0.5 * (1.0 + jax.scipy.special.erf(pre * (1.0 / math.sqrt(2.0))))
    activated = pre * cdf
    slope = cdf + pre * jnp.exp(-0.5 * pre * pre) * (1.0 / math.sqrt(2.0 * math.pi))
    return (activated, slope)


def flat(z, c, x, y):
    return ((z * 2 + c) * RING + x) * RING + y


def exchange(array, partner):
    pairs = []
    for z in range(RING):
        for c in range(2):
            for x in range(RING):
                for y in range(RING):
                    pairs.append((flat(*partner(z, c, x, y)), flat(z, c, x, y)))
    return lax.ppermute(array, AXES, pairs)


NEAR = ((1, 3), (3, 1))
Z_PAIR = ((1, 3), (3, 1))
OWNER_SLOT = ((0, 2, 3, 1), (0, 1, 3, 2))


def along(keep, first, turn):
    def partner(z, c, x, y):
        half = c if keep else 1 - c
        step = NEAR[c][turn]
        if (half == 0) == first:
            return (z, c, x ^ step, y)
        return (z, c, x, y ^ step)

    return partner


def along_z(turn):
    return lambda z, c, x, y: (z ^ Z_PAIR[c][turn], c, x, y)


def other_core(z, c, x, y):
    return (z, 1 - c, x, y)


def slot_of(keep, place_ref, i):
    z, core = place_ref[0], place_ref[1]

    def one(c):
        near = NEAR[c]
        owned = z ^ (0, near[0], near[1], near[0] ^ near[1])[i]
        table = OWNER_SLOT[c if keep else 1 - c]
        slot = jnp.int32(table[0])
        for j in range(1, RING):
            slot = jnp.where(owned == j, table[j], slot)
        return slot

    return jnp.where(core == 0, one(0), one(1))


def arrival_of(keep, place_ref, i):
    z, core = place_ref[0], place_ref[1]

    def one(c):
        near = NEAR[c]
        arrival = (0, near[0], near[1], near[0] ^ near[1])
        owned = z ^ OWNER_SLOT[c if keep else 1 - c].index(i)
        place = jnp.int32(arrival.index(0))
        for j in range(1, RING):
            place = jnp.where(owned == j, arrival.index(j), place)
        return place

    return jnp.where(core == 0, one(0), one(1))


def cut_kernel(place_ref, tokens_ref, grad_ref, kept_ref, passed_ref):
    block, wide = kept_ref.shape[0], tokens_ref.shape[1]
    core = place_ref[1]
    for ref, which in ((kept_ref, core), (passed_ref, 1 - core)):
        rows = pl.ds(pl.multiple_of(which * block, block), block)
        ref[:, :wide] = tokens_ref[rows, :]
        ref[:, wide:] = grad_ref[rows, :]


def cut(place, tokens, out_grad):
    rows, wide = tokens.shape
    half = jax.ShapeDtypeStruct((rows // 2, 2 * wide), BF)
    return pl.pallas_call(
        cut_kernel,
        grid_spec=pltpu.PrefetchScalarGridSpec(
            num_scalar_prefetch=1,
            grid=(1,),
            in_specs=[pl.BlockSpec((rows, wide), lambda i, place: (0, 0))] * 2,
            out_specs=[pl.BlockSpec((rows // 2, 2 * wide), lambda i, place: (0, 0))] * 2,
        ),
        out_shape=[half, half],
        cost_estimate=cost(flops=0, bytes_accessed=8 * rows * wide, transcendentals=0),
    )(place, tokens, out_grad)


def assemble_kernel(keep, place_ref, a_ref, b_ref, c_ref, *out_refs):
    rows = a_ref.shape[0]
    part = rows // PARTS

    def put(i, ref, first):
        at = pl.multiple_of(slot_of(keep, place_ref, i) * part, part)
        for j, out_ref in enumerate(out_refs):
            out_ref[pl.ds(at, part), :] = ref[first + j * part:first + (j + 1) * part, :]

    put(0, a_ref, 0)
    put(1, b_ref, 0)
    put(2, c_ref, 0)
    put(3, c_ref, rows)


def assemble(keep, place, a, b, c):
    rows, wide = a.shape
    tiles = 2
    spec = lambda n: pl.BlockSpec((n, wide // tiles), lambda i, place: (0, i))
    out_rows = RING * rows // PARTS
    return pl.pallas_call(
        functools.partial(assemble_kernel, keep),
        grid_spec=pltpu.PrefetchScalarGridSpec(
            num_scalar_prefetch=1,
            grid=(tiles,),
            in_specs=[spec(rows), spec(rows), spec(2 * rows)],
            out_specs=[spec(out_rows)] * PARTS,
        ),
        out_shape=[jax.ShapeDtypeStruct((out_rows, wide), BF)] * PARTS,
        cost_estimate=cost(flops=0, bytes_accessed=16 * rows * wide, transcendentals=0),
    )(place, a, b, c)


def order_of(keep):
    return (0, 1, 2, 3) if keep else (0, 2, 1, 3)


def panel_at(piece, slot):
    return piece // 2, (piece % 2) * RING + slot


def hidden_at(keep, piece, slot):
    return slot // 2, (slot % 2) * RING + order_of(keep).index(piece)


def pair_kernel(keep, hidden, added, split, block, place_ref, *refs):
    a_refs, (left_ref, right_ref), rest = refs[:2], refs[2:4], refs[4:]
    if added:
        more_ref, rest = rest[0], rest[1:]
    rows_ref = rest[-1]
    out_refs = rest[:-1]

    @pl.when(pl.program_id(1) == 0)
    def _():
        if hidden:
            size = RING * block
            for i in range(RING):
                at = pl.multiple_of(arrival_of(keep, place_ref, i) * size, size)
                first = (i % 2) * size
                rows_ref[pl.ds(at, size), :] = a_refs[i // 2][first:first + size, :]
        else:
            for i in range(RING):
                for j, piece in enumerate(order_of(keep)):
                    which, first = panel_at(piece, i)
                    at = (i * RING + j) * block
                    rows_ref[at:at + block, :] = a_refs[which][first * block:(first + 1) * block, :]

    def finish(total):
        if added:
            total = total + more_ref[...].astype(F32)
        total = total.astype(BF)
        if not split:
            out_refs[0][...] = total
        else:
            half = total.shape[0] // 2
            out_refs[0][...] = total[:half]
            out_refs[1][...] = total[half:]

    @pl.when(pl.program_id(0) == 0)
    def _():
        finish(lax.dot_general(rows_ref[...], left_ref[...], NN, preferred_element_type=F32))

    @pl.when(pl.program_id(0) == 1)
    def _():
        finish(lax.dot_general(rows_ref[...], right_ref[...], NT, preferred_element_type=F32))


def pair_dot(keep, hidden, pair, left, right, place, more=None, split=True, tile=512):
    rows = sum(a.shape[0] for a in pair)
    block = rows // RING // RING
    depth, wide = left.shape
    tiles = wide // tile
    in_specs = [pl.BlockSpec((a.shape[0], depth), lambda h, n, place: (0, h)) for a in pair]
    in_specs += [
        pl.BlockSpec((depth, tile), lambda h, n, place: (0, n * (1 - h) + (tiles - 1) * h)),
        pl.BlockSpec((tile, depth), lambda h, n, place: (n * h, 0)),
    ]
    out_of = lambda n_rows: pl.BlockSpec((n_rows, tile), lambda h, n, place: (0, h * tiles + n))
    args = [*pair, left, right]
    if more is not None:
        in_specs.append(out_of(rows))
        args.append(more)
    outs = [rows // 2, rows // 2] if split else [rows]
    result = pl.pallas_call(
        functools.partial(pair_kernel, keep, hidden, more is not None, split, block),
        grid_spec=pltpu.PrefetchScalarGridSpec(
            num_scalar_prefetch=1,
            grid=(2, tiles),
            in_specs=in_specs,
            out_specs=[out_of(n) for n in outs],
            scratch_shapes=[pltpu.VMEM((rows, depth), BF)],
        ),
        out_shape=[jax.ShapeDtypeStruct((n, 2 * wide), BF) for n in outs],
        compiler_params=pltpu.CompilerParams(vmem_limit_bytes=18 * 2**20),
        cost_estimate=cost(
            flops=4 * rows * depth * wide,
            bytes_accessed=4 * depth * wide + 8 * rows * wide,
            transcendentals=0,
        ),
    )(place, *args)
    return result if split else result[0]


def grad_kernel(pairs, block, factor, begun, *refs):
    lefts, rights, out_ref = refs[:4], refs[4:8], refs[-1]
    total = None
    for i, blocks in enumerate(pairs):
        right = jnp.concatenate(
            [rights[j][first * block:(first + 1) * block, :] for j, first in blocks], axis=0
        )
        term = lax.dot_general(lefts[i][...], right, TN, preferred_element_type=F32)
        total = term if total is None else total + term
    total = total * factor
    out_ref[...] = total + refs[8][...] if begun else total


def grad_dot(lefts, left_part, rights, right_part, pairs, factor, begun=None, tile=256):
    wide = lefts[0].shape[1] // 2
    tiles = wide // tile
    tokens = sum(a.shape[0] for a in lefts)
    args = [*lefts, *rights]
    in_specs = [pl.BlockSpec((a.shape[0], wide), lambda n: (0, left_part)) for a in lefts]
    in_specs += [
        pl.BlockSpec((a.shape[0], tile), lambda n: (0, right_part * tiles + n)) for a in rights
    ]
    out_spec = pl.BlockSpec((wide, tile), lambda n: (0, n))
    aliases = {}
    if begun is not None:
        aliases = {len(args): 0}
        args.append(begun)
        in_specs.append(out_spec)
    block = rights[0].shape[0] // (2 * RING)
    return pl.pallas_call(
        functools.partial(grad_kernel, pairs, block, factor, begun is not None),
        grid=(tiles,),
        in_specs=in_specs,
        out_specs=out_spec,
        out_shape=jax.ShapeDtypeStruct((wide, wide), F32),
        input_output_aliases=aliases,
        compiler_params=pltpu.CompilerParams(vmem_limit_bytes=24 * 2**20),
        cost_estimate=cost(
            flops=2 * tokens * wide * wide,
            bytes_accessed=3 * tokens * wide + 2 * wide * wide,
            transcendentals=0,
        ),
    )(*args)


def after(value, *events):
    return lax.optimization_barrier((value, *events))[0]


def shards(tokens, out_grad, weight_in, weight_out):
    core = lax.axis_index("row") % 2
    z = lax.axis_index("row") // 2
    dp = lax.axis_index("dp")
    rows, width = tokens.shape
    block = rows // 2
    inner = weight_in.shape[1] // 2
    factor = 1.0 / math.sqrt(rows * 16)
    both_ways = (True, False)

    place = jnp.stack([z, core]).astype(jnp.int32)
    w_in = lax.dynamic_slice_in_dim(weight_in, dp * inner, inner, 1)
    w_out = lax.dynamic_slice_in_dim(weight_out, dp * inner, inner, 0)

    order = (False, True)
    start, one, two, own_a, own_b = {}, {}, {}, {}, {}
    start[True], start[False] = cut(place, tokens, out_grad)
    for keep in order:
        one[keep] = exchange(start[keep], along(keep, True, 0))
    for keep in order:
        pair = jnp.concatenate([start[keep], one[keep]], axis=0)
        two[keep] = exchange(pair, along(keep, True, 1))
    for keep in order:
        own_a[keep], own_b[keep] = assemble(keep, place, start[keep], one[keep], two[keep])

    def every(values, *events):
        both = lax.optimization_barrier((values[True], values[False], *events))
        return {True: both[0], False: both[1]}

    def neighbours(own):
        near = {keep: exchange(own[keep], along(keep, False, 0)) for keep in order}
        return {keep: jnp.concatenate([own[keep], near[keep]], axis=0) for keep in order}

    def others(near):
        return {keep: exchange(near[keep], along(keep, False, 1)) for keep in order}

    def panel_dot(keep, near, rest, *events, more=None):
        pair = [near[keep], rest[keep]]
        pair[0] = after(pair[0], *events) if events else pair[0]
        return pair_dot(keep, False, pair, w_in, w_out, place, more=more, split=keep)

    def out_dot(keep, pair, *events):
        pair = list(pair)
        pair[1] = after(pair[1], *events) if events else pair[1]
        return pair_dot(keep, True, pair, w_out, w_in, place)

    def halfway(kept, got):
        half = kept.shape[0] // 2
        sums = kept.astype(F32) + got.astype(F32)
        return [sums[:half], sums[half:]]

    def hidden_of(value):
        pre, back = value[:, :width], value[:, width:]
        activated, slope = gelu_parts(pre)
        return jnp.concatenate([activated.astype(BF), (back * slope).astype(BF)], axis=1)

    near_a = neighbours(every(own_a))
    rest_a = others(near_a)
    near_b = neighbours(every(own_b, near_a[True], near_a[False]))
    sent_a = panel_dot(False, near_a, rest_a, near_b[True], near_b[False])
    kept_a, send_a = panel_dot(True, near_a, rest_a, more=exchange(sent_a, other_core))
    step_a = exchange(send_a, along_z(0))
    rest_b = others(near_b)
    sent_b = panel_dot(False, near_b, rest_b, send_a)
    kept_b, send_b = panel_dot(True, near_b, rest_b, more=exchange(sent_b, other_core))
    step_b = exchange(send_b, along_z(0))

    half_a = halfway(kept_a, step_a)
    turn_a = exchange(after(half_a[1].astype(BF), send_b), along_z(1))
    half_b = halfway(kept_b, step_b)
    mine_a = hidden_of(half_a[0] + turn_a.astype(F32))
    next_a = exchange(mine_a, along_z(1))
    turn_b = exchange(after(half_b[1].astype(BF), mine_a), along_z(1))
    pair_a = jnp.concatenate([mine_a, next_a], axis=0)
    far_a = exchange(pair_a, along_z(0))
    mine_b = hidden_of(half_b[0] + turn_b.astype(F32))
    next_b = exchange(mine_b, along_z(1))
    pair_b = jnp.concatenate([mine_b, next_b], axis=0)
    far_b = exchange(pair_b, along_z(0))
    far_a = after(far_a, pair_b)
    hid_a = {True: (pair_a, far_a)}
    hid_a[False] = (exchange(pair_a, other_core), exchange(far_a, other_core))
    hid_b = {True: (pair_b, far_b)}
    hid_b[False] = (exchange(pair_b, other_core), exchange(far_b, other_core))

    in_pairs, out_pairs = [], []
    for base, keep in ((0, True), (2, False)):
        for i in range(2):
            in_pairs.append(
                tuple(
                    (base + hidden_at(keep, 2 * i + p, slot)[0], hidden_at(keep, 2 * i + p, slot)[1])
                    for p in range(2)
                    for slot in range(RING)
                )
            )
            out_pairs.append(
                tuple(
                    (base + panel_at(piece, 2 * i + s)[0], panel_at(piece, 2 * i + s)[1])
                    for s in range(2)
                    for piece in order_of(keep)
                )
            )

    def grads(which, near, rest, hid, begun, *events):
        panels = [near[True], rest[True], near[False], rest[False]]
        hiddens = [*hid[True], *hid[False]]
        lefts, rights, pairs = (
            (panels, hiddens, in_pairs) if which == 0 else (hiddens, panels, out_pairs)
        )
        lefts[0] = after(lefts[0], *events)
        return grad_dot(lefts, 0, rights, 1, pairs, factor, begun)

    def first_half(keep, kept, passed):
        return halfway(kept, exchange(passed, along(keep, True, 1)))

    def first_sum(keep, sums, *events):
        passed = sums[1].astype(BF)
        passed = after(passed, *events) if events else passed
        return sums[0] + exchange(passed, along(keep, True, 0)).astype(F32)

    out_a, out_b, sums_a, sums_b, total_a, total_b = {}, {}, {}, {}, {}, {}
    out_a[True] = out_dot(True, hid_a[True])
    out_a[False] = out_dot(False, hid_a[False], out_a[True][0])
    grad_in = grads(0, near_a, rest_a, hid_a, None, out_a[False][0])
    for keep in both_ways:
        sums_a[keep] = first_half(keep, *out_a[keep])
    out_b[True] = out_dot(True, hid_b[True], grad_in, sums_a[True][0], sums_a[False][0])
    out_b[False] = out_dot(False, hid_b[False], out_b[True][0])
    for keep in both_ways:
        total_a[keep] = first_sum(keep, sums_a[keep])
    grad_out = grads(1, near_a, rest_a, hid_a, None, out_b[False][0])
    for keep in both_ways:
        sums_b[keep] = first_half(keep, *out_b[keep])
    for keep in both_ways:
        total_b[keep] = first_sum(keep, sums_b[keep], grad_out, total_a[True], total_a[False])
    grad_in = grads(0, near_b, rest_b, hid_b, grad_in, sums_b[True][0], sums_b[False][0])

    part = block // PARTS
    pick = lambda keep, piece: jnp.concatenate(
        [
            total[keep][order_of(keep).index(piece) * part:(order_of(keep).index(piece) + 1) * part]
            for total in (total_a, total_b)
        ],
        axis=0,
    )
    gots, done = {}, {}
    for keep in both_ways:
        passed = jnp.concatenate([pick(keep, 2), pick(keep, 3)], axis=0).astype(BF)
        gots[keep] = exchange(after(passed, grad_in), along(keep, False, 1))
    grad_out = grads(1, near_b, rest_b, hid_b, grad_out, grad_in)
    for keep in both_ways:
        got = gots[keep].astype(F32)
        last = after((pick(keep, 1) + got[block:]).astype(BF), grad_out)
        done[keep] = (
            pick(keep, 0) + got[:block] + exchange(last, along(keep, False, 0)).astype(F32)
        ).astype(BF)

    low = jnp.where(core == 0, done[True], done[False])
    high = jnp.where(core == 0, done[False], done[True])
    result = jnp.concatenate([low, high], axis=0)
    return (result[:, :width], result[:, width:], grad_in, grad_out)


def solution(mesh):
    placed = (P(("col", "dp"), "row"), P(("col", "dp"), "row"), P("row", "col"), P("col", "row"))
    return jax.shard_map(
        shards,
        mesh=mesh,
        in_specs=placed,
        out_specs=(
            P(("col", "dp"), "row"),
            P(("col", "dp"), "row"),
            P("row", ("col", "dp")),
            P(("col", "dp"), "row"),
        ),
        check_vma=False,
    )
```

```python
import functools
import math

import jax
import jax.numpy as jnp
from jax import lax
from jax.experimental import pallas as pl
from jax.experimental.pallas import tpu as pltpu
from jax.sharding import PartitionSpec as P

AXES = ("row", "col", "dp")
RING = 4
PARTS = 2
BF = jnp.bfloat16
F32 = jnp.float32
NN = (((1,), (0,)), ((), ()))
NT = (((1,), (1,)), ((), ()))
TN = (((0,), (0,)), ((), ()))


def cost(flops, bytes_accessed, transcendentals):
    return pl.CostEstimate(
        flops=flops // 1000, bytes_accessed=bytes_accessed // 1000, transcendentals=transcendentals
    )


def gelu_parts(pre):
    cdf = 0.5 * (1.0 + jax.scipy.special.erf(pre * (1.0 / math.sqrt(2.0))))
    activated = pre * cdf
    slope = cdf + pre * jnp.exp(-0.5 * pre * pre) * (1.0 / math.sqrt(2.0 * math.pi))
    return (activated, slope)


def flat(z, c, x, y):
    return ((z * 2 + c) * RING + x) * RING + y


def exchange(array, partner):
    pairs = []
    for z in range(RING):
        for c in range(2):
            for x in range(RING):
                for y in range(RING):
                    pairs.append((flat(*partner(z, c, x, y)), flat(z, c, x, y)))
    return lax.ppermute(array, AXES, pairs)


NEAR = ((1, 3), (3, 1))
Z_PAIR = ((1, 3), (3, 1))
OWNER_SLOT = ((0, 2, 3, 1), (0, 1, 3, 2))


def along(keep, first, turn):
    def partner(z, c, x, y):
        half = c if keep else 1 - c
        step = NEAR[c][turn]
        if (half == 0) == first:
            return (z, c, x ^ step, y)
        return (z, c, x, y ^ step)

    return partner


def along_z(turn):
    return lambda z, c, x, y: (z ^ Z_PAIR[c][turn], c, x, y)


def other_core(z, c, x, y):
    return (z, 1 - c, x, y)


def slot_of(keep, place_ref, i):
    z, core = place_ref[0], place_ref[1]

    def one(c):
        near = NEAR[c]
        owned = z ^ (0, near[0], near[1], near[0] ^ near[1])[i]
        table = OWNER_SLOT[c if keep else 1 - c]
        slot = jnp.int32(table[0])
        for j in range(1, RING):
            slot = jnp.where(owned == j, table[j], slot)
        return slot

    return jnp.where(core == 0, one(0), one(1))


def arrival_of(keep, place_ref, i):
    z, core = place_ref[0], place_ref[1]

    def one(c):
        near = NEAR[c]
        arrival = (0, near[0], near[1], near[0] ^ near[1])
        owned = z ^ OWNER_SLOT[c if keep else 1 - c].index(i)
        place = jnp.int32(arrival.index(0))
        for j in range(1, RING):
            place = jnp.where(owned == j, arrival.index(j), place)
        return place

    return jnp.where(core == 0, one(0), one(1))


def cut_kernel(place_ref, tokens_ref, grad_ref, kept_ref, passed_ref):
    block, wide = kept_ref.shape[0], tokens_ref.shape[1]
    core = place_ref[1]
    for ref, which in ((kept_ref, core), (passed_ref, 1 - core)):
        rows = pl.ds(pl.multiple_of(which * block, block), block)
        ref[:, :wide] = tokens_ref[rows, :]
        ref[:, wide:] = grad_ref[rows, :]


def whole(kernel, place, arrays, shapes):
    return pl.pallas_call(
        kernel,
        in_specs=[pl.BlockSpec(memory_space=pltpu.SMEM)]
        + [pl.BlockSpec(memory_space=pltpu.VMEM)] * len(arrays),
        out_specs=[pl.BlockSpec(memory_space=pltpu.VMEM)] * len(shapes),
        out_shape=[jax.ShapeDtypeStruct(shape, BF) for shape in shapes],
        compiler_params=pltpu.CompilerParams(vmem_limit_bytes=8 * 2**20),
        cost_estimate=cost(flops=0, bytes_accessed=0, transcendentals=0),
    )(place, *arrays)


def cut(place, tokens, out_grad):
    rows, wide = tokens.shape
    return whole(cut_kernel, place, [tokens, out_grad], [(rows // 2, 2 * wide)] * 2)


def join_kernel(place_ref, a_ref, b_ref, out_ref):
    rows = a_ref.shape[0]
    out_ref[:rows, :] = a_ref[...]
    out_ref[rows:, :] = b_ref[...]


def join(place, a, b):
    return whole(join_kernel, place, [a, b], [(2 * a.shape[0], a.shape[1])])[0]


def assemble_kernel(keep, place_ref, a_ref, b_ref, c_ref, *out_refs):
    rows = a_ref.shape[0]
    part = rows // PARTS

    def put(i, ref, first):
        at = pl.multiple_of(slot_of(keep, place_ref, i) * part, part)
        for j, out_ref in enumerate(out_refs):
            out_ref[pl.ds(at, part), :] = ref[first + j * part:first + (j + 1) * part, :]

    put(0, a_ref, 0)
    put(1, b_ref, 0)
    put(2, c_ref, 0)
    put(3, c_ref, rows)


def assemble(keep, place, a, b, c):
    rows, wide = a.shape
    kernel = functools.partial(assemble_kernel, keep)
    return whole(kernel, place, [a, b, c], [(RING * rows // PARTS, wide)] * PARTS)


def order_of(keep):
    return (0, 1, 2, 3) if keep else (0, 2, 1, 3)


def panel_at(piece, slot):
    return piece // 2, (piece % 2) * RING + slot


def hidden_at(keep, piece, slot):
    return slot // 2, (slot % 2) * RING + order_of(keep).index(piece)


def pair_kernel(keep, hidden, added, split, block, place_ref, *refs):
    a_refs, (left_ref, right_ref), rest = refs[:2], refs[2:4], refs[4:]
    if added:
        more_ref, rest = rest[0], rest[1:]
    rows_ref = rest[-1]
    out_refs = rest[:-1]

    @pl.when(pl.program_id(1) == 0)
    def _():
        if hidden:
            size = RING * block
            for i in range(RING):
                at = pl.multiple_of(arrival_of(keep, place_ref, i) * size, size)
                first = (i % 2) * size
                rows_ref[pl.ds(at, size), :] = a_refs[i // 2][first:first + size, :]
        else:
            for i in range(RING):
                for j, piece in enumerate(order_of(keep)):
                    which, first = panel_at(piece, i)
                    at = (i * RING + j) * block
                    rows_ref[at:at + block, :] = a_refs[which][first * block:(first + 1) * block, :]

    def finish(total):
        if added:
            total = total + more_ref[...].astype(F32)
        total = total.astype(BF)
        if not split:
            out_refs[0][...] = total
        else:
            half = total.shape[0] // 2
            out_refs[0][...] = total[:half]
            out_refs[1][...] = total[half:]

    @pl.when(pl.program_id(0) == 0)
    def _():
        finish(lax.dot_general(rows_ref[...], left_ref[...], NN, preferred_element_type=F32))

    @pl.when(pl.program_id(0) == 1)
    def _():
        finish(lax.dot_general(rows_ref[...], right_ref[...], NT, preferred_element_type=F32))


def pair_dot(keep, hidden, pair, left, right, place, more=None, split=True, tile=512):
    rows = sum(a.shape[0] for a in pair)
    block = rows // RING // RING
    depth, wide = left.shape
    tiles = wide // tile
    in_specs = [pl.BlockSpec((a.shape[0], depth), lambda h, n, place: (0, h)) for a in pair]
    in_specs += [
        pl.BlockSpec((depth, tile), lambda h, n, place: (0, n * (1 - h) + (tiles - 1) * h)),
        pl.BlockSpec((tile, depth), lambda h, n, place: (n * h, 0)),
    ]
    out_of = lambda n_rows: pl.BlockSpec((n_rows, tile), lambda h, n, place: (0, h * tiles + n))
    args = [*pair, left, right]
    if more is not None:
        in_specs.append(out_of(rows))
        args.append(more)
    outs = [rows // 2, rows // 2] if split else [rows]
    result = pl.pallas_call(
        functools.partial(pair_kernel, keep, hidden, more is not None, split, block),
        grid_spec=pltpu.PrefetchScalarGridSpec(
            num_scalar_prefetch=1,
            grid=(2, tiles),
            in_specs=in_specs,
            out_specs=[out_of(n) for n in outs],
            scratch_shapes=[pltpu.VMEM((rows, depth), BF)],
        ),
        out_shape=[jax.ShapeDtypeStruct((n, 2 * wide), BF) for n in outs],
        compiler_params=pltpu.CompilerParams(vmem_limit_bytes=18 * 2**20),
        cost_estimate=cost(
            flops=4 * rows * depth * wide,
            bytes_accessed=4 * depth * wide + 8 * rows * wide,
            transcendentals=0,
        ),
    )(place, *args)
    return result if split else result[0]


def grad_kernel(pairs, block, factor, begun, *refs):
    lefts, rights, out_ref = refs[:4], refs[4:8], refs[-1]
    total = None
    for i, blocks in enumerate(pairs):
        right = jnp.concatenate(
            [rights[j][first * block:(first + 1) * block, :] for j, first in blocks], axis=0
        )
        term = lax.dot_general(lefts[i][...], right, TN, preferred_element_type=F32)
        total = term if total is None else total + term
    total = total * factor
    out_ref[...] = total + refs[8][...] if begun else total


def grad_dot(lefts, left_part, rights, right_part, pairs, factor, begun=None, tile=256):
    wide = lefts[0].shape[1] // 2
    tiles = wide // tile
    tokens = sum(a.shape[0] for a in lefts)
    args = [*lefts, *rights]
    in_specs = [pl.BlockSpec((a.shape[0], wide), lambda n: (0, left_part)) for a in lefts]
    in_specs += [
        pl.BlockSpec((a.shape[0], tile), lambda n: (0, right_part * tiles + n)) for a in rights
    ]
    out_spec = pl.BlockSpec((wide, tile), lambda n: (0, n))
    aliases = {}
    if begun is not None:
        aliases = {len(args): 0}
        args.append(begun)
        in_specs.append(out_spec)
    block = rights[0].shape[0] // (2 * RING)
    return pl.pallas_call(
        functools.partial(grad_kernel, pairs, block, factor, begun is not None),
        grid=(tiles,),
        in_specs=in_specs,
        out_specs=out_spec,
        out_shape=jax.ShapeDtypeStruct((wide, wide), F32),
        input_output_aliases=aliases,
        compiler_params=pltpu.CompilerParams(vmem_limit_bytes=24 * 2**20),
        cost_estimate=cost(
            flops=2 * tokens * wide * wide,
            bytes_accessed=3 * tokens * wide + 2 * wide * wide,
            transcendentals=0,
        ),
    )(*args)


def after(value, *events):
    return lax.optimization_barrier((value, *events))[0]


def shards(tokens, out_grad, weight_in, weight_out):
    core = lax.axis_index("row") % 2
    z = lax.axis_index("row") // 2
    dp = lax.axis_index("dp")
    rows, width = tokens.shape
    block = rows // 2
    inner = weight_in.shape[1] // 2
    factor = 1.0 / math.sqrt(rows * 16)
    both_ways = (True, False)

    place = jnp.stack([z, core]).astype(jnp.int32)
    w_in = lax.dynamic_slice_in_dim(weight_in, dp * inner, inner, 1)
    w_out = lax.dynamic_slice_in_dim(weight_out, dp * inner, inner, 0)

    order = (False, True)
    start, one, two, own_a, own_b = {}, {}, {}, {}, {}
    start[True], start[False] = cut(place, tokens, out_grad)
    for keep in order:
        one[keep] = exchange(start[keep], along(keep, True, 0))
    for keep in order:
        two[keep] = exchange(join(place, start[keep], one[keep]), along(keep, True, 1))
    for keep in order:
        own_a[keep], own_b[keep] = assemble(keep, place, start[keep], one[keep], two[keep])

    def neighbours(own):
        return {keep: exchange(own[keep], along(keep, False, 0)) for keep in order}

    def joined(own, near):
        return {keep: join(place, own[keep], near[keep]) for keep in order}

    def others(near):
        return {keep: exchange(near[keep], along(keep, False, 1)) for keep in order}

    def panel_dot(keep, near, rest, *events, more=None):
        pair = [near[keep], after(rest[keep], *events) if events else rest[keep]]
        return pair_dot(keep, False, pair, w_in, w_out, place, more=more, split=keep)

    def out_dot(keep, pair, *events):
        pair = list(pair)
        pair[1] = after(pair[1], *events) if events else pair[1]
        return pair_dot(keep, True, pair, w_out, w_in, place)

    def halfway(kept, got):
        half = kept.shape[0] // 2
        sums = kept.astype(F32) + got.astype(F32)
        return [sums[:half], sums[half:]]

    def hidden_of(value):
        pre, back = value[:, :width], value[:, width:]
        activated, slope = gelu_parts(pre)
        return jnp.concatenate([activated.astype(BF), (back * slope).astype(BF)], axis=1)

    both = lax.optimization_barrier((own_a[True], own_a[False]))
    own_a = {True: both[0], False: both[1]}
    near_a = joined(own_a, neighbours(own_a))
    rest_a = others(near_a)
    step_b = neighbours(own_b)
    sent_a = panel_dot(False, near_a, rest_a, rest_a[True])
    got_a = after(exchange(sent_a, other_core), step_b[True], step_b[False])
    kept_a, send_a = panel_dot(True, near_a, rest_a, more=got_a)
    step_a = exchange(send_a, along_z(0))
    near_b = joined(own_b, step_b)
    rest_b = others(near_b)
    sent_b = panel_dot(False, near_b, rest_b, rest_b[True], send_a)
    half_a = halfway(kept_a, step_a)
    turn_a = exchange(half_a[1].astype(BF), along_z(1))
    got_b = after(exchange(sent_b, other_core), turn_a)
    kept_b, send_b = panel_dot(True, near_b, rest_b, more=got_b)
    step_b = exchange(send_b, along_z(0))
    half_b = halfway(kept_b, step_b)
    mine_a = hidden_of(half_a[0] + turn_a.astype(F32))
    next_a = exchange(mine_a, along_z(1))
    turn_b = exchange(half_b[1].astype(BF), along_z(1))
    pair_a = jnp.concatenate([mine_a, next_a], axis=0)
    far_a = exchange(pair_a, along_z(0))
    mine_b = hidden_of(half_b[0] + turn_b.astype(F32))
    next_b = exchange(mine_b, along_z(1))
    pair_b = jnp.concatenate([mine_b, next_b], axis=0)
    far_b = exchange(pair_b, along_z(0))
    far_a = after(far_a, pair_b)
    hid_a = {True: (pair_a, far_a)}
    hid_a[False] = (exchange(pair_a, other_core), exchange(far_a, other_core))
    hid_b = {True: (pair_b, far_b)}
    hid_b[False] = (exchange(pair_b, other_core), exchange(far_b, other_core))

    in_pairs, out_pairs = [], []
    for base, keep in ((0, True), (2, False)):
        for i in range(2):
            in_pairs.append(
                tuple(
                    (base + hidden_at(keep, 2 * i + p, slot)[0], hidden_at(keep, 2 * i + p, slot)[1])
                    for p in range(2)
                    for slot in range(RING)
                )
            )
            out_pairs.append(
                tuple(
                    (base + panel_at(piece, 2 * i + s)[0], panel_at(piece, 2 * i + s)[1])
                    for s in range(2)
                    for piece in order_of(keep)
                )
            )

    def grads(which, near, rest, hid, begun, *events):
        panels = [near[True], rest[True], near[False], rest[False]]
        hiddens = [*hid[True], *hid[False]]
        lefts, rights, pairs = (
            (panels, hiddens, in_pairs) if which == 0 else (hiddens, panels, out_pairs)
        )
        lefts[0] = after(lefts[0], *events)
        return grad_dot(lefts, 0, rights, 1, pairs, factor, begun)

    def second_half(keep, kept, got):
        sums = halfway(kept, got)
        return sums[0], exchange(sums[1].astype(BF), along(keep, True, 0))

    out_a, out_b, got_a, got_b = {}, {}, {}, {}
    sums_a, sums_b, last_a, last_b, total_a, total_b = {}, {}, {}, {}, {}, {}
    out_a[True] = out_dot(True, hid_a[True])
    out_a[False] = out_dot(False, hid_a[False], out_a[True][0])
    for keep in both_ways:
        got_a[keep] = exchange(out_a[keep][1], along(keep, True, 1))
    grad_in = grads(0, near_a, rest_a, hid_a, None, out_a[False][0])
    for keep in both_ways:
        got = after(got_a[keep], grad_in, got_a[not keep])
        sums_a[keep], last_a[keep] = second_half(keep, out_a[keep][0], got)
    out_b[True] = out_dot(True, hid_b[True], got_a[True], got_a[False], grad_in)
    out_b[False] = out_dot(False, hid_b[False], out_b[True][0])
    for keep in both_ways:
        got_b[keep] = exchange(out_b[keep][1], along(keep, True, 1))
    grad_out = grads(1, near_a, rest_a, hid_a, None, out_b[False][0], last_a[True], last_a[False])
    for keep in both_ways:
        got = after(got_b[keep], grad_out, got_b[not keep])
        sums_b[keep], last_b[keep] = second_half(keep, out_b[keep][0], got)
    grad_in = grads(0, near_b, rest_b, hid_b, grad_in, got_b[True], got_b[False], grad_out)
    for keep in both_ways:
        total_a[keep] = sums_a[keep] + last_a[keep].astype(F32)
        total_b[keep] = sums_b[keep] + after(last_b[keep], grad_in).astype(F32)

    part = block // PARTS
    pick = lambda keep, piece: jnp.concatenate(
        [
            total[keep][order_of(keep).index(piece) * part:(order_of(keep).index(piece) + 1) * part]
            for total in (total_a, total_b)
        ],
        axis=0,
    )
    gots, done = {}, {}
    for keep in both_ways:
        passed = jnp.concatenate([pick(keep, 2), pick(keep, 3)], axis=0).astype(BF)
        gots[keep] = exchange(passed, along(keep, False, 1))
    grad_out = grads(1, near_b, rest_b, hid_b, grad_out, last_b[True], last_b[False], grad_in)
    for keep in both_ways:
        got = after(gots[keep], grad_out).astype(F32)
        last = (pick(keep, 1) + got[block:]).astype(BF)
        done[keep] = (
            pick(keep, 0) + got[:block] + exchange(last, along(keep, False, 0)).astype(F32)
        ).astype(BF)

    low = jnp.where(core == 0, done[True], done[False])
    high = jnp.where(core == 0, done[False], done[True])
    result = jnp.concatenate([low, high], axis=0)
    return (result[:, :width], result[:, width:], grad_in, grad_out)


def solution(mesh):
    placed = (P(("col", "dp"), "row"), P(("col", "dp"), "row"), P("row", "col"), P("col", "row"))
    return jax.shard_map(
        shards,
        mesh=mesh,
        in_specs=placed,
        out_specs=(
            P(("col", "dp"), "row"),
            P(("col", "dp"), "row"),
            P("row", ("col", "dp")),
            P(("col", "dp"), "row"),
        ),
        check_vma=False,
    )
```

```python
import functools
import math

import jax
import jax.numpy as jnp
from jax import lax
from jax.experimental import pallas as pl
from jax.experimental.pallas import tpu as pltpu
from jax.sharding import PartitionSpec as P

AXES = ("row", "col", "dp")
RING = 4
PARTS = 2
BF = jnp.bfloat16
F32 = jnp.float32
NN = (((1,), (0,)), ((), ()))
NT = (((1,), (1,)), ((), ()))
TN = (((0,), (0,)), ((), ()))


def cost(flops, bytes_accessed, transcendentals):
    return pl.CostEstimate(
        flops=flops // 1000, bytes_accessed=bytes_accessed // 1000, transcendentals=transcendentals
    )


def gelu_parts(pre):
    cdf = 0.5 * (1.0 + jax.scipy.special.erf(pre * (1.0 / math.sqrt(2.0))))
    activated = pre * cdf
    slope = cdf + pre * jnp.exp(-0.5 * pre * pre) * (1.0 / math.sqrt(2.0 * math.pi))
    return (activated, slope)


def flat(z, c, x, y):
    return ((z * 2 + c) * RING + x) * RING + y


def exchange(array, partner):
    pairs = []
    for z in range(RING):
        for c in range(2):
            for x in range(RING):
                for y in range(RING):
                    pairs.append((flat(*partner(z, c, x, y)), flat(z, c, x, y)))
    return lax.ppermute(array, AXES, pairs)


NEAR = ((1, 3), (3, 1))
Z_PAIR = ((1, 3), (3, 1))
OWNER_SLOT = ((0, 2, 3, 1), (0, 1, 3, 2))


def along(keep, first, turn):
    def partner(z, c, x, y):
        half = c if keep else 1 - c
        step = NEAR[c][turn]
        if (half == 0) == first:
            return (z, c, x ^ step, y)
        return (z, c, x, y ^ step)

    return partner


def along_z(turn):
    return lambda z, c, x, y: (z ^ Z_PAIR[c][turn], c, x, y)


def other_core(z, c, x, y):
    return (z, 1 - c, x, y)


def slot_of(keep, place_ref, i):
    z, core = place_ref[0], place_ref[1]

    def one(c):
        near = NEAR[c]
        owned = z ^ (0, near[0], near[1], near[0] ^ near[1])[i]
        table = OWNER_SLOT[c if keep else 1 - c]
        slot = jnp.int32(table[0])
        for j in range(1, RING):
            slot = jnp.where(owned == j, table[j], slot)
        return slot

    return jnp.where(core == 0, one(0), one(1))


def arrival_of(keep, place_ref, i):
    z, core = place_ref[0], place_ref[1]

    def one(c):
        near = NEAR[c]
        arrival = (0, near[0], near[1], near[0] ^ near[1])
        owned = z ^ OWNER_SLOT[c if keep else 1 - c].index(i)
        place = jnp.int32(arrival.index(0))
        for j in range(1, RING):
            place = jnp.where(owned == j, arrival.index(j), place)
        return place

    return jnp.where(core == 0, one(0), one(1))


def cut_kernel(place_ref, tokens_ref, grad_ref, kept_ref, passed_ref):
    block, wide = kept_ref.shape[0], tokens_ref.shape[1]
    core = place_ref[1]
    for ref, which in ((kept_ref, core), (passed_ref, 1 - core)):
        rows = pl.ds(pl.multiple_of(which * block, block), block)
        ref[:, :wide] = tokens_ref[rows, :]
        ref[:, wide:] = grad_ref[rows, :]


def whole(kernel, place, arrays, shapes):
    return pl.pallas_call(
        kernel,
        in_specs=[pl.BlockSpec(memory_space=pltpu.SMEM)]
        + [pl.BlockSpec(memory_space=pltpu.VMEM)] * len(arrays),
        out_specs=[pl.BlockSpec(memory_space=pltpu.VMEM)] * len(shapes),
        out_shape=[jax.ShapeDtypeStruct(shape, BF) for shape in shapes],
        compiler_params=pltpu.CompilerParams(vmem_limit_bytes=8 * 2**20),
        cost_estimate=cost(flops=0, bytes_accessed=0, transcendentals=0),
    )(place, *arrays)


def cut(place, tokens, out_grad):
    rows, wide = tokens.shape
    return whole(cut_kernel, place, [tokens, out_grad], [(rows // 2, 2 * wide)] * 2)


def join_kernel(place_ref, a_ref, b_ref, out_ref):
    rows = a_ref.shape[0]
    out_ref[:rows, :] = a_ref[...]
    out_ref[rows:, :] = b_ref[...]


def join(place, a, b):
    return whole(join_kernel, place, [a, b], [(2 * a.shape[0], a.shape[1])])[0]


def assemble_kernel(keep, place_ref, a_ref, b_ref, c_ref, *out_refs):
    rows = a_ref.shape[0]
    part = rows // PARTS

    def put(i, ref, first):
        at = pl.multiple_of(slot_of(keep, place_ref, i) * part, part)
        for j, out_ref in enumerate(out_refs):
            out_ref[pl.ds(at, part), :] = ref[first + j * part:first + (j + 1) * part, :]

    put(0, a_ref, 0)
    put(1, b_ref, 0)
    put(2, c_ref, 0)
    put(3, c_ref, rows)


def assemble(keep, place, a, b, c):
    rows, wide = a.shape
    kernel = functools.partial(assemble_kernel, keep)
    return whole(kernel, place, [a, b, c], [(RING * rows // PARTS, wide)] * PARTS)


def order_of(keep):
    return (0, 1, 2, 3) if keep else (0, 2, 1, 3)


def panel_at(piece, slot):
    return piece // 2, (piece % 2) * RING + slot


def hidden_at(keep, piece, slot):
    return slot // 2, (slot % 2) * RING + order_of(keep).index(piece)


def pair_kernel(keep, hidden, added, split, block, place_ref, *refs):
    a_refs, (left_ref, right_ref), rest = refs[:2], refs[2:4], refs[4:]
    if added:
        more_ref, rest = rest[0], rest[1:]
    rows_ref = rest[-1]
    out_refs = rest[:-1]

    @pl.when(pl.program_id(1) == 0)
    def _():
        if hidden:
            size = RING * block
            for i in range(RING):
                at = pl.multiple_of(arrival_of(keep, place_ref, i) * size, size)
                first = (i % 2) * size
                rows_ref[pl.ds(at, size), :] = a_refs[i // 2][first:first + size, :]
        else:
            for i in range(RING):
                for j, piece in enumerate(order_of(keep)):
                    which, first = panel_at(piece, i)
                    at = (i * RING + j) * block
                    rows_ref[at:at + block, :] = a_refs[which][first * block:(first + 1) * block, :]

    def finish(total):
        if added:
            total = total + more_ref[...].astype(F32)
        total = total.astype(BF)
        if not split:
            out_refs[0][...] = total
        else:
            half = total.shape[0] // 2
            out_refs[0][...] = total[:half]
            out_refs[1][...] = total[half:]

    @pl.when(pl.program_id(0) == 0)
    def _():
        finish(lax.dot_general(rows_ref[...], left_ref[...], NN, preferred_element_type=F32))

    @pl.when(pl.program_id(0) == 1)
    def _():
        finish(lax.dot_general(rows_ref[...], right_ref[...], NT, preferred_element_type=F32))


def pair_dot(keep, hidden, pair, left, right, place, more=None, split=True, tile=512):
    rows = sum(a.shape[0] for a in pair)
    block = rows // RING // RING
    depth, wide = left.shape
    tiles = wide // tile
    in_specs = [pl.BlockSpec((a.shape[0], depth), lambda h, n, place: (0, h)) for a in pair]
    in_specs += [
        pl.BlockSpec((depth, tile), lambda h, n, place: (0, n * (1 - h) + (tiles - 1) * h)),
        pl.BlockSpec((tile, depth), lambda h, n, place: (n * h, 0)),
    ]
    out_of = lambda n_rows: pl.BlockSpec((n_rows, tile), lambda h, n, place: (0, h * tiles + n))
    args = [*pair, left, right]
    if more is not None:
        in_specs.append(out_of(rows))
        args.append(more)
    outs = [rows // 2, rows // 2] if split else [rows]
    result = pl.pallas_call(
        functools.partial(pair_kernel, keep, hidden, more is not None, split, block),
        grid_spec=pltpu.PrefetchScalarGridSpec(
            num_scalar_prefetch=1,
            grid=(2, tiles),
            in_specs=in_specs,
            out_specs=[out_of(n) for n in outs],
            scratch_shapes=[pltpu.VMEM((rows, depth), BF)],
        ),
        out_shape=[jax.ShapeDtypeStruct((n, 2 * wide), BF) for n in outs],
        compiler_params=pltpu.CompilerParams(vmem_limit_bytes=18 * 2**20),
        cost_estimate=cost(
            flops=4 * rows * depth * wide,
            bytes_accessed=4 * depth * wide + 8 * rows * wide,
            transcendentals=0,
        ),
    )(place, *args)
    return result if split else result[0]


def grad_kernel(pairs, block, factor, begun, *refs):
    lefts, rights, out_ref = refs[:4], refs[4:8], refs[-1]
    total = None
    for i, blocks in enumerate(pairs):
        right = jnp.concatenate(
            [rights[j][first * block:(first + 1) * block, :] for j, first in blocks], axis=0
        )
        term = lax.dot_general(lefts[i][...], right, TN, preferred_element_type=F32)
        total = term if total is None else total + term
    total = total * factor
    out_ref[...] = total + refs[8][...] if begun else total


def grad_dot(lefts, left_part, rights, right_part, pairs, factor, begun=None, tile=256):
    wide = lefts[0].shape[1] // 2
    tiles = wide // tile
    tokens = sum(a.shape[0] for a in lefts)
    args = [*lefts, *rights]
    in_specs = [pl.BlockSpec((a.shape[0], wide), lambda n: (0, left_part)) for a in lefts]
    in_specs += [
        pl.BlockSpec((a.shape[0], tile), lambda n: (0, right_part * tiles + n)) for a in rights
    ]
    out_spec = pl.BlockSpec((wide, tile), lambda n: (0, n))
    aliases = {}
    if begun is not None:
        aliases = {len(args): 0}
        args.append(begun)
        in_specs.append(out_spec)
    block = rights[0].shape[0] // (2 * RING)
    return pl.pallas_call(
        functools.partial(grad_kernel, pairs, block, factor, begun is not None),
        grid=(tiles,),
        in_specs=in_specs,
        out_specs=out_spec,
        out_shape=jax.ShapeDtypeStruct((wide, wide), F32),
        input_output_aliases=aliases,
        compiler_params=pltpu.CompilerParams(vmem_limit_bytes=24 * 2**20),
        cost_estimate=cost(
            flops=2 * tokens * wide * wide,
            bytes_accessed=3 * tokens * wide + 2 * wide * wide,
            transcendentals=0,
        ),
    )(*args)


def after(value, *events):
    return lax.optimization_barrier((value, *events))[0]


def shards(tokens, out_grad, weight_in, weight_out):
    core = lax.axis_index("row") % 2
    z = lax.axis_index("row") // 2
    dp = lax.axis_index("dp")
    rows, width = tokens.shape
    block = rows // 2
    inner = weight_in.shape[1] // 2
    factor = 1.0 / math.sqrt(rows * 16)
    both_ways = (True, False)

    place = jnp.stack([z, core]).astype(jnp.int32)
    w_in = lax.dynamic_slice_in_dim(weight_in, dp * inner, inner, 1)
    w_out = lax.dynamic_slice_in_dim(weight_out, dp * inner, inner, 0)

    order = (False, True)
    start, one, two, own_a, own_b = {}, {}, {}, {}, {}
    start[True], start[False] = cut(place, tokens, out_grad)
    for keep in order:
        one[keep] = exchange(start[keep], along(keep, True, 0))
    for keep in order:
        two[keep] = exchange(join(place, start[keep], one[keep]), along(keep, True, 1))
    for keep in order:
        own_a[keep], own_b[keep] = assemble(keep, place, start[keep], one[keep], two[keep])

    def neighbours(own):
        return {keep: exchange(own[keep], along(keep, False, 0)) for keep in order}

    def joined(own, near):
        return {keep: join(place, own[keep], near[keep]) for keep in order}

    def others(near):
        return {keep: exchange(near[keep], along(keep, False, 1)) for keep in order}

    def panel_dot(keep, near, rest, *events, more=None):
        pair = [near[keep], after(rest[keep], *events) if events else rest[keep]]
        return pair_dot(keep, False, pair, w_in, w_out, place, more=more, split=keep)

    def out_dot(keep, pair, *events):
        pair = list(pair)
        pair[1] = after(pair[1], *events) if events else pair[1]
        return pair_dot(keep, True, pair, w_out, w_in, place)

    def halfway(kept, got):
        half = kept.shape[0] // 2
        sums = kept.astype(F32) + got.astype(F32)
        return [sums[:half], sums[half:]]

    def hidden_of(value):
        pre, back = value[:, :width], value[:, width:]
        activated, slope = gelu_parts(pre)
        return jnp.concatenate([activated.astype(BF), (back * slope).astype(BF)], axis=1)

    both = lax.optimization_barrier((own_a[True], own_a[False]))
    own_a = {True: both[0], False: both[1]}
    near_a = joined(own_a, neighbours(own_a))
    rest_a = others(near_a)
    near_of_b = neighbours(own_b)
    sent_a = panel_dot(False, near_a, rest_a, rest_a[True])
    kept_a, send_a = panel_dot(True, near_a, rest_a, more=exchange(sent_a, other_core))
    step_a = after(exchange(send_a, along_z(0)), near_of_b[True], near_of_b[False])
    near_b = joined(own_b, near_of_b)
    rest_b = others(near_b)
    half_a = halfway(kept_a, step_a)
    turn_a = exchange(half_a[1].astype(BF), along_z(1))
    mine_a = hidden_of(half_a[0] + turn_a.astype(F32))
    sent_b = panel_dot(False, near_b, rest_b, rest_b[True], mine_a)
    next_a = exchange(mine_a, along_z(1))
    got_b = after(exchange(sent_b, other_core), next_a)
    pair_a = join(place, mine_a, next_a)
    far_a = exchange(pair_a, along_z(0))
    kept_b, send_b = panel_dot(True, near_b, rest_b, pair_a, more=got_b)
    step_b = exchange(send_b, along_z(0))
    hid_a = {True: (pair_a, far_a)}
    hid_a[False] = (exchange(pair_a, other_core), exchange(far_a, other_core))

    in_pairs, out_pairs = [], []
    for base, keep in ((0, True), (2, False)):
        for i in range(2):
            in_pairs.append(
                tuple(
                    (base + hidden_at(keep, 2 * i + p, slot)[0], hidden_at(keep, 2 * i + p, slot)[1])
                    for p in range(2)
                    for slot in range(RING)
                )
            )
            out_pairs.append(
                tuple(
                    (base + panel_at(piece, 2 * i + s)[0], panel_at(piece, 2 * i + s)[1])
                    for s in range(2)
                    for piece in order_of(keep)
                )
            )

    def grads(which, near, rest, hid, begun, *events):
        panels = [near[True], rest[True], near[False], rest[False]]
        hiddens = [*hid[True], *hid[False]]
        lefts, rights, pairs = (
            (panels, hiddens, in_pairs) if which == 0 else (hiddens, panels, out_pairs)
        )
        lefts[0] = after(lefts[0], *events)
        return grad_dot(lefts, 0, rights, 1, pairs, factor, begun)

    def second_half(keep, kept, got):
        sums = halfway(kept, got)
        return sums[0], exchange(sums[1].astype(BF), along(keep, True, 0))

    out_a, out_b, got_a, got_b = {}, {}, {}, {}
    sums_a, sums_b, last_a, last_b, total_a, total_b = {}, {}, {}, {}, {}, {}
    out_a[True] = out_dot(True, hid_a[True])
    half_b = halfway(kept_b, after(step_b, out_a[True][0]))
    turn_b = exchange(half_b[1].astype(BF), along_z(1))
    out_a[False] = out_dot(False, hid_a[False], out_a[True][0], step_b)
    mine_b = hidden_of(half_b[0] + after(turn_b, out_a[False][0]).astype(F32))
    next_b = exchange(mine_b, along_z(1))
    for keep in both_ways:
        got_a[keep] = exchange(out_a[keep][1], along(keep, True, 1))
    grad_in = grads(0, near_a, rest_a, hid_a, None, out_a[False][0], turn_b)
    pair_b = join(place, mine_b, after(next_b, grad_in))
    far_b = exchange(pair_b, along_z(0))
    grad_out = grads(1, near_a, rest_a, hid_a, None, next_b, got_a[True], got_a[False], grad_in)
    for keep in both_ways:
        got = after(got_a[keep], grad_in, got_a[not keep])
        sums_a[keep], last_a[keep] = second_half(keep, out_a[keep][0], got)
    far_b = after(far_b, grad_out)
    hid_b = {True: (pair_b, far_b)}
    hid_b[False] = (exchange(pair_b, other_core), exchange(far_b, other_core))

    out_b[True] = out_dot(True, hid_b[True])
    out_b[False] = out_dot(False, hid_b[False], out_b[True][0])
    for keep in both_ways:
        got_b[keep] = exchange(out_b[keep][1], along(keep, True, 1))
    grad_in = grads(
        0, near_b, rest_b, hid_b, grad_in, out_b[False][0], last_a[True], last_a[False]
    )
    for keep in both_ways:
        got = after(got_b[keep], grad_in, got_b[not keep])
        sums_b[keep], last_b[keep] = second_half(keep, out_b[keep][0], got)
    grad_out = grads(1, near_b, rest_b, hid_b, grad_out, got_b[True], got_b[False], grad_in)
    for keep in both_ways:
        total_a[keep] = sums_a[keep] + last_a[keep].astype(F32)
        total_b[keep] = sums_b[keep] + after(last_b[keep], grad_out, last_b[not keep]).astype(F32)

    part = block // PARTS
    pick = lambda keep, piece: jnp.concatenate(
        [
            total[keep][order_of(keep).index(piece) * part:(order_of(keep).index(piece) + 1) * part]
            for total in (total_a, total_b)
        ],
        axis=0,
    )
    gots, done = {}, {}
    for keep in both_ways:
        passed = jnp.concatenate([pick(keep, 2), pick(keep, 3)], axis=0).astype(BF)
        gots[keep] = exchange(passed, along(keep, False, 1))
    for keep in both_ways:
        got = after(gots[keep], gots[not keep]).astype(F32)
        last = (pick(keep, 1) + got[block:]).astype(BF)
        done[keep] = (
            pick(keep, 0) + got[:block] + exchange(last, along(keep, False, 0)).astype(F32)
        ).astype(BF)

    low = jnp.where(core == 0, done[True], done[False])
    high = jnp.where(core == 0, done[False], done[True])
    result = jnp.concatenate([low, high], axis=0)
    return (result[:, :width], result[:, width:], grad_in, grad_out)


def solution(mesh):
    placed = (P(("col", "dp"), "row"), P(("col", "dp"), "row"), P("row", "col"), P("col", "row"))
    return jax.shard_map(
        shards,
        mesh=mesh,
        in_specs=placed,
        out_specs=(
            P(("col", "dp"), "row"),
            P(("col", "dp"), "row"),
            P("row", ("col", "dp")),
            P(("col", "dp"), "row"),
        ),
        check_vma=False,
    )
```

```python
import functools
import math

import jax
import jax.numpy as jnp
from jax import lax
from jax.experimental import pallas as pl
from jax.experimental.pallas import tpu as pltpu
from jax.sharding import PartitionSpec as P

AXES = ("row", "col", "dp")
RING = 4
PARTS = 2
BF = jnp.bfloat16
F32 = jnp.float32
NN = (((1,), (0,)), ((), ()))
NT = (((1,), (1,)), ((), ()))
TN = (((0,), (0,)), ((), ()))


def cost(flops, bytes_accessed, transcendentals):
    return pl.CostEstimate(
        flops=flops // 1000, bytes_accessed=bytes_accessed // 1000, transcendentals=transcendentals
    )


def gelu_parts(pre):
    cdf = 0.5 * (1.0 + jax.scipy.special.erf(pre * (1.0 / math.sqrt(2.0))))
    activated = pre * cdf
    slope = cdf + pre * jnp.exp(-0.5 * pre * pre) * (1.0 / math.sqrt(2.0 * math.pi))
    return (activated, slope)


def flat(z, c, x, y):
    return ((z * 2 + c) * RING + x) * RING + y


def exchange(array, partner):
    pairs = []
    for z in range(RING):
        for c in range(2):
            for x in range(RING):
                for y in range(RING):
                    pairs.append((flat(*partner(z, c, x, y)), flat(z, c, x, y)))
    return lax.ppermute(array, AXES, pairs)


NEAR = ((1, 3), (3, 1))
Z_PAIR = ((1, 3), (3, 1))
OWNER_SLOT = ((0, 2, 3, 1), (0, 1, 3, 2))


def along(keep, first, turn):
    def partner(z, c, x, y):
        half = c if keep else 1 - c
        step = NEAR[c][turn]
        if (half == 0) == first:
            return (z, c, x ^ step, y)
        return (z, c, x, y ^ step)

    return partner


def along_z(turn):
    return lambda z, c, x, y: (z ^ Z_PAIR[c][turn], c, x, y)


def other_core(z, c, x, y):
    return (z, 1 - c, x, y)


def slot_of(keep, place_ref, i):
    z, core = place_ref[0], place_ref[1]

    def one(c):
        near = NEAR[c]
        owned = z ^ (0, near[0], near[1], near[0] ^ near[1])[i]
        table = OWNER_SLOT[c if keep else 1 - c]
        slot = jnp.int32(table[0])
        for j in range(1, RING):
            slot = jnp.where(owned == j, table[j], slot)
        return slot

    return jnp.where(core == 0, one(0), one(1))


def arrival_of(keep, place_ref, i):
    z, core = place_ref[0], place_ref[1]

    def one(c):
        near = NEAR[c]
        arrival = (0, near[0], near[1], near[0] ^ near[1])
        owned = z ^ OWNER_SLOT[c if keep else 1 - c].index(i)
        place = jnp.int32(arrival.index(0))
        for j in range(1, RING):
            place = jnp.where(owned == j, arrival.index(j), place)
        return place

    return jnp.where(core == 0, one(0), one(1))


def cut_kernel(place_ref, tokens_ref, grad_ref, kept_ref, passed_ref):
    block, wide = kept_ref.shape[0], tokens_ref.shape[1]
    core = place_ref[1]
    for ref, which in ((kept_ref, core), (passed_ref, 1 - core)):
        rows = pl.ds(pl.multiple_of(which * block, block), block)
        ref[:, :wide] = tokens_ref[rows, :]
        ref[:, wide:] = grad_ref[rows, :]


def whole(kernel, place, arrays, shapes):
    return pl.pallas_call(
        kernel,
        in_specs=[pl.BlockSpec(memory_space=pltpu.SMEM)]
        + [pl.BlockSpec(memory_space=pltpu.VMEM)] * len(arrays),
        out_specs=[pl.BlockSpec(memory_space=pltpu.VMEM)] * len(shapes),
        out_shape=[jax.ShapeDtypeStruct(shape, BF) for shape in shapes],
        compiler_params=pltpu.CompilerParams(vmem_limit_bytes=8 * 2**20),
        cost_estimate=cost(flops=0, bytes_accessed=0, transcendentals=0),
    )(place, *arrays)


def cut(place, tokens, out_grad):
    rows, wide = tokens.shape
    return whole(cut_kernel, place, [tokens, out_grad], [(rows // 2, 2 * wide)] * 2)


def join_kernel(place_ref, a_ref, b_ref, out_ref):
    rows = a_ref.shape[0]
    out_ref[:rows, :] = a_ref[...]
    out_ref[rows:, :] = b_ref[...]


def join(place, a, b):
    return whole(join_kernel, place, [a, b], [(2 * a.shape[0], a.shape[1])])[0]


def assemble_kernel(keep, place_ref, a_ref, b_ref, c_ref, out_ref):
    rows = a_ref.shape[0]
    part = rows // PARTS

    def put(i, ref, first):
        for j in range(PARTS):
            at = pl.multiple_of((j * RING + slot_of(keep, place_ref, i)) * part, part)
            out_ref[pl.ds(at, part), :] = ref[first + j * part:first + (j + 1) * part, :]

    put(0, a_ref, 0)
    put(1, b_ref, 0)
    put(2, c_ref, 0)
    put(3, c_ref, rows)


def assemble(keep, place, a, b, c):
    rows, wide = a.shape
    kernel = functools.partial(assemble_kernel, keep)
    return whole(kernel, place, [a, b, c], [(RING * rows, wide)])[0]


def regroup_kernel(place_ref, own_ref, near_ref, a_ref, b_ref):
    half = own_ref.shape[0] // 2
    for i, out_ref in enumerate((a_ref, b_ref)):
        out_ref[:half, :] = own_ref[i * half:(i + 1) * half, :]
        out_ref[half:, :] = near_ref[i * half:(i + 1) * half, :]


def regroup(place, own, near):
    return whole(regroup_kernel, place, [own, near], [own.shape] * 2)


def order_of(keep):
    return (0, 1, 2, 3) if keep else (0, 2, 1, 3)


def panel_at(piece, slot):
    return piece // 2, (piece % 2) * RING + slot


def hidden_at(keep, piece, slot):
    return slot // 2, (slot % 2) * RING + order_of(keep).index(piece)


def pair_kernel(keep, hidden, added, split, block, place_ref, *refs):
    a_refs, (left_ref, right_ref), rest = refs[:2], refs[2:4], refs[4:]
    if added:
        more_ref, rest = rest[0], rest[1:]
    rows_ref = rest[-1]
    out_refs = rest[:-1]

    @pl.when(pl.program_id(1) == 0)
    def _():
        if hidden:
            size = RING * block
            for i in range(RING):
                at = pl.multiple_of(arrival_of(keep, place_ref, i) * size, size)
                first = (i % 2) * size
                rows_ref[pl.ds(at, size), :] = a_refs[i // 2][first:first + size, :]
        else:
            for i in range(RING):
                for j, piece in enumerate(order_of(keep)):
                    which, first = panel_at(piece, i)
                    at = (i * RING + j) * block
                    rows_ref[at:at + block, :] = a_refs[which][first * block:(first + 1) * block, :]

    def finish(total):
        if added:
            total = total + more_ref[...].astype(F32)
        total = total.astype(BF)
        if not split:
            out_refs[0][...] = total
        else:
            half = total.shape[0] // 2
            out_refs[0][...] = total[:half]
            out_refs[1][...] = total[half:]

    @pl.when(pl.program_id(0) == 0)
    def _():
        finish(lax.dot_general(rows_ref[...], left_ref[...], NN, preferred_element_type=F32))

    @pl.when(pl.program_id(0) == 1)
    def _():
        finish(lax.dot_general(rows_ref[...], right_ref[...], NT, preferred_element_type=F32))


def pair_dot(keep, hidden, pair, left, right, place, more=None, split=True, tile=512):
    rows = sum(a.shape[0] for a in pair)
    block = rows // RING // RING
    depth, wide = left.shape
    tiles = wide // tile
    in_specs = [pl.BlockSpec((a.shape[0], depth), lambda h, n, place: (0, h)) for a in pair]
    in_specs += [
        pl.BlockSpec((depth, tile), lambda h, n, place: (0, n * (1 - h) + (tiles - 1) * h)),
        pl.BlockSpec((tile, depth), lambda h, n, place: (n * h, 0)),
    ]
    out_of = lambda n_rows: pl.BlockSpec((n_rows, tile), lambda h, n, place: (0, h * tiles + n))
    args = [*pair, left, right]
    if more is not None:
        in_specs.append(out_of(rows))
        args.append(more)
    outs = [rows // 2, rows // 2] if split else [rows]
    result = pl.pallas_call(
        functools.partial(pair_kernel, keep, hidden, more is not None, split, block),
        grid_spec=pltpu.PrefetchScalarGridSpec(
            num_scalar_prefetch=1,
            grid=(2, tiles),
            in_specs=in_specs,
            out_specs=[out_of(n) for n in outs],
            scratch_shapes=[pltpu.VMEM((rows, depth), BF)],
        ),
        out_shape=[jax.ShapeDtypeStruct((n, 2 * wide), BF) for n in outs],
        compiler_params=pltpu.CompilerParams(vmem_limit_bytes=18 * 2**20),
        cost_estimate=cost(
            flops=4 * rows * depth * wide,
            bytes_accessed=4 * depth * wide + 8 * rows * wide,
            transcendentals=0,
        ),
    )(place, *args)
    return result if split else result[0]


def grad_kernel(pairs, block, factor, begun, *refs):
    lefts, rights, out_ref = refs[:4], refs[4:8], refs[-1]
    total = None
    for i, blocks in enumerate(pairs):
        right = jnp.concatenate(
            [rights[j][first * block:(first + 1) * block, :] for j, first in blocks], axis=0
        )
        term = lax.dot_general(lefts[i][...], right, TN, preferred_element_type=F32)
        total = term if total is None else total + term
    total = total * factor
    out_ref[...] = total + refs[8][...] if begun else total


def grad_dot(lefts, left_part, rights, right_part, pairs, factor, begun=None, tile=256):
    wide = lefts[0].shape[1] // 2
    tiles = wide // tile
    tokens = sum(a.shape[0] for a in lefts)
    args = [*lefts, *rights]
    in_specs = [pl.BlockSpec((a.shape[0], wide), lambda n: (0, left_part)) for a in lefts]
    in_specs += [
        pl.BlockSpec((a.shape[0], tile), lambda n: (0, right_part * tiles + n)) for a in rights
    ]
    out_spec = pl.BlockSpec((wide, tile), lambda n: (0, n))
    aliases = {}
    if begun is not None:
        aliases = {len(args): 0}
        args.append(begun)
        in_specs.append(out_spec)
    block = rights[0].shape[0] // (2 * RING)
    return pl.pallas_call(
        functools.partial(grad_kernel, pairs, block, factor, begun is not None),
        grid=(tiles,),
        in_specs=in_specs,
        out_specs=out_spec,
        out_shape=jax.ShapeDtypeStruct((wide, wide), F32),
        input_output_aliases=aliases,
        compiler_params=pltpu.CompilerParams(vmem_limit_bytes=24 * 2**20),
        cost_estimate=cost(
            flops=2 * tokens * wide * wide,
            bytes_accessed=3 * tokens * wide + 2 * wide * wide,
            transcendentals=0,
        ),
    )(*args)


def after(value, *events):
    return lax.optimization_barrier((value, *events))[0]


def shards(tokens, out_grad, weight_in, weight_out):
    core = lax.axis_index("row") % 2
    z = lax.axis_index("row") // 2
    dp = lax.axis_index("dp")
    rows, width = tokens.shape
    block = rows // 2
    inner = weight_in.shape[1] // 2
    factor = 1.0 / math.sqrt(rows * 16)
    both_ways = (True, False)

    place = jnp.stack([z, core]).astype(jnp.int32)
    w_in = lax.dynamic_slice_in_dim(weight_in, dp * inner, inner, 1)
    w_out = lax.dynamic_slice_in_dim(weight_out, dp * inner, inner, 0)

    order = (False, True)
    start, one, two, own, near_a, near_b = {}, {}, {}, {}, {}, {}
    start[True], start[False] = cut(place, tokens, out_grad)
    for keep in order:
        one[keep] = exchange(start[keep], along(keep, True, 0))
    for keep in order:
        two[keep] = exchange(join(place, start[keep], one[keep]), along(keep, True, 1))
    for keep in order:
        own[keep] = assemble(keep, place, start[keep], one[keep], two[keep])

    def others(near):
        return {keep: exchange(near[keep], along(keep, False, 1)) for keep in order}

    def panel_dot(keep, near, rest, *events, more=None):
        pair = [near[keep], after(rest[keep], *events) if events else rest[keep]]
        return pair_dot(keep, False, pair, w_in, w_out, place, more=more, split=keep)

    def out_dot(keep, pair, *events):
        pair = list(pair)
        pair[1] = after(pair[1], *events) if events else pair[1]
        return pair_dot(keep, True, pair, w_out, w_in, place)

    def halfway(kept, got):
        half = kept.shape[0] // 2
        sums = kept.astype(F32) + got.astype(F32)
        return [sums[:half], sums[half:]]

    def hidden_of(value):
        pre, back = value[:, :width], value[:, width:]
        activated, slope = gelu_parts(pre)
        return jnp.concatenate([activated.astype(BF), (back * slope).astype(BF)], axis=1)

    both = lax.optimization_barrier((own[True], own[False]))
    own = {True: both[0], False: both[1]}
    near = {keep: exchange(own[keep], along(keep, False, 0)) for keep in order}
    for keep in order:
        near_a[keep], near_b[keep] = regroup(place, own[keep], near[keep])
    rest_a = others(near_a)
    rest_b = others(near_b)
    sent_a = panel_dot(False, near_a, rest_a, rest_a[True])
    kept_a, send_a = panel_dot(True, near_a, rest_a, more=exchange(sent_a, other_core))
    sent_b = panel_dot(False, near_b, rest_b, rest_b[True], send_a)
    step_a = after(exchange(send_a, along_z(0)), sent_b)
    half_a = halfway(kept_a, step_a)
    turn_a = exchange(half_a[1].astype(BF), along_z(1))
    kept_b, send_b = panel_dot(
        True, near_b, rest_b, step_a, more=exchange(sent_b, other_core)
    )
    mine_a = hidden_of(half_a[0] + after(turn_a, send_b).astype(F32))
    next_a = exchange(mine_a, along_z(1))
    step_b = exchange(after(send_b, next_a), along_z(0))
    pair_a = join(place, mine_a, next_a)
    far_a = exchange(pair_a, along_z(0))
    hid_a = {True: (pair_a, far_a)}
    hid_a[False] = (exchange(pair_a, other_core), exchange(far_a, other_core))

    in_pairs, out_pairs = [], []
    for base, keep in ((0, True), (2, False)):
        for i in range(2):
            in_pairs.append(
                tuple(
                    (base + hidden_at(keep, 2 * i + p, slot)[0], hidden_at(keep, 2 * i + p, slot)[1])
                    for p in range(2)
                    for slot in range(RING)
                )
            )
            out_pairs.append(
                tuple(
                    (base + panel_at(piece, 2 * i + s)[0], panel_at(piece, 2 * i + s)[1])
                    for s in range(2)
                    for piece in order_of(keep)
                )
            )

    def grads(which, near, rest, hid, begun, *events):
        panels = [near[True], rest[True], near[False], rest[False]]
        hiddens = [*hid[True], *hid[False]]
        lefts, rights, pairs = (
            (panels, hiddens, in_pairs) if which == 0 else (hiddens, panels, out_pairs)
        )
        lefts[0] = after(lefts[0], *events)
        return grad_dot(lefts, 0, rights, 1, pairs, factor, begun)

    def second_half(keep, kept, got):
        sums = halfway(kept, got)
        return sums[0], exchange(sums[1].astype(BF), along(keep, True, 0))

    out_a, out_b, got_a, got_b = {}, {}, {}, {}
    sums_a, sums_b, last_a, last_b, total_a, total_b = {}, {}, {}, {}, {}, {}
    out_a[True] = out_dot(True, hid_a[True])
    half_b = halfway(kept_b, after(step_b, out_a[True][0]))
    turn_b = exchange(half_b[1].astype(BF), along_z(1))
    out_a[False] = out_dot(False, hid_a[False], out_a[True][0], step_b)
    mine_b = hidden_of(half_b[0] + after(turn_b, out_a[False][0]).astype(F32))
    next_b = exchange(mine_b, along_z(1))
    for keep in both_ways:
        got_a[keep] = exchange(out_a[keep][1], along(keep, True, 1))
    grad_in = grads(0, near_a, rest_a, hid_a, None, out_a[False][0], turn_b)
    pair_b = join(place, mine_b, after(next_b, grad_in))
    far_b = exchange(pair_b, along_z(0))
    grad_out = grads(1, near_a, rest_a, hid_a, None, next_b, got_a[True], got_a[False], grad_in)
    for keep in both_ways:
        got = after(got_a[keep], grad_in, got_a[not keep])
        sums_a[keep], last_a[keep] = second_half(keep, out_a[keep][0], got)
    far_b = after(far_b, grad_out)
    hid_b = {True: (pair_b, far_b)}
    hid_b[False] = (exchange(pair_b, other_core), exchange(far_b, other_core))

    out_b[True] = out_dot(True, hid_b[True])
    out_b[False] = out_dot(False, hid_b[False], out_b[True][0])
    for keep in both_ways:
        got_b[keep] = exchange(out_b[keep][1], along(keep, True, 1))
    grad_in = grads(
        0, near_b, rest_b, hid_b, grad_in, out_b[False][0], last_a[True], last_a[False]
    )
    for keep in both_ways:
        got = after(got_b[keep], grad_in, got_b[not keep])
        sums_b[keep], last_b[keep] = second_half(keep, out_b[keep][0], got)
    grad_out = grads(1, near_b, rest_b, hid_b, grad_out, got_b[True], got_b[False], grad_in)
    for keep in both_ways:
        total_a[keep] = sums_a[keep] + last_a[keep].astype(F32)
        total_b[keep] = sums_b[keep] + after(last_b[keep], grad_out, last_b[not keep]).astype(F32)

    part = block // PARTS
    pick = lambda keep, piece: jnp.concatenate(
        [
            total[keep][order_of(keep).index(piece) * part:(order_of(keep).index(piece) + 1) * part]
            for total in (total_a, total_b)
        ],
        axis=0,
    )
    gots, done = {}, {}
    for keep in both_ways:
        passed = jnp.concatenate([pick(keep, 2), pick(keep, 3)], axis=0).astype(BF)
        gots[keep] = exchange(passed, along(keep, False, 1))
    for keep in both_ways:
        got = after(gots[keep], gots[not keep]).astype(F32)
        last = (pick(keep, 1) + got[block:]).astype(BF)
        done[keep] = (
            pick(keep, 0) + got[:block] + exchange(last, along(keep, False, 0)).astype(F32)
        ).astype(BF)

    low = jnp.where(core == 0, done[True], done[False])
    high = jnp.where(core == 0, done[False], done[True])
    result = jnp.concatenate([low, high], axis=0)
    return (result[:, :width], result[:, width:], grad_in, grad_out)


def solution(mesh):
    placed = (P(("col", "dp"), "row"), P(("col", "dp"), "row"), P("row", "col"), P("col", "row"))
    return jax.shard_map(
        shards,
        mesh=mesh,
        in_specs=placed,
        out_specs=(
            P(("col", "dp"), "row"),
            P(("col", "dp"), "row"),
            P("row", ("col", "dp")),
            P(("col", "dp"), "row"),
        ),
        check_vma=False,
    )
```

```python
import functools
import math

import jax
import jax.numpy as jnp
from jax import lax
from jax.experimental import pallas as pl
from jax.experimental.pallas import tpu as pltpu
from jax.sharding import PartitionSpec as P

AXES = ("row", "col", "dp")
RING = 4
PARTS = 2
BF = jnp.bfloat16
F32 = jnp.float32
NN = (((1,), (0,)), ((), ()))
NT = (((1,), (1,)), ((), ()))
TN = (((0,), (0,)), ((), ()))


def cost(flops, bytes_accessed, transcendentals):
    return pl.CostEstimate(
        flops=flops // 1000, bytes_accessed=bytes_accessed // 1000, transcendentals=transcendentals
    )


def gelu_parts(pre):
    cdf = 0.5 * (1.0 + jax.scipy.special.erf(pre * (1.0 / math.sqrt(2.0))))
    activated = pre * cdf
    slope = cdf + pre * jnp.exp(-0.5 * pre * pre) * (1.0 / math.sqrt(2.0 * math.pi))
    return (activated, slope)


def flat(z, c, x, y):
    return ((z * 2 + c) * RING + x) * RING + y


def exchange(array, partner):
    pairs = []
    for z in range(RING):
        for c in range(2):
            for x in range(RING):
                for y in range(RING):
                    pairs.append((flat(*partner(z, c, x, y)), flat(z, c, x, y)))
    return lax.ppermute(array, AXES, pairs)


NEAR = ((1, 3), (3, 1))
Z_PAIR = ((1, 3), (3, 1))
OWNER_SLOT = ((0, 2, 3, 1), (0, 1, 3, 2))


def along(keep, first, turn):
    def partner(z, c, x, y):
        half = c if keep else 1 - c
        step = NEAR[c][turn]
        if (half == 0) == first:
            return (z, c, x ^ step, y)
        return (z, c, x, y ^ step)

    return partner


def along_z(turn):
    return lambda z, c, x, y: (z ^ Z_PAIR[c][turn], c, x, y)


def other_core(z, c, x, y):
    return (z, 1 - c, x, y)


def slot_of(keep, place_ref, i):
    z, core = place_ref[0], place_ref[1]

    def one(c):
        near = NEAR[c]
        owned = z ^ (0, near[0], near[1], near[0] ^ near[1])[i]
        table = OWNER_SLOT[c if keep else 1 - c]
        slot = jnp.int32(table[0])
        for j in range(1, RING):
            slot = jnp.where(owned == j, table[j], slot)
        return slot

    return jnp.where(core == 0, one(0), one(1))


def arrival_of(keep, place_ref, i):
    z, core = place_ref[0], place_ref[1]

    def one(c):
        near = NEAR[c]
        arrival = (0, near[0], near[1], near[0] ^ near[1])
        owned = z ^ OWNER_SLOT[c if keep else 1 - c].index(i)
        place = jnp.int32(arrival.index(0))
        for j in range(1, RING):
            place = jnp.where(owned == j, arrival.index(j), place)
        return place

    return jnp.where(core == 0, one(0), one(1))


def cut_kernel(place_ref, tokens_ref, grad_ref, kept_ref, passed_ref):
    block, wide = kept_ref.shape[0], tokens_ref.shape[1]
    core = place_ref[1]
    for ref, which in ((kept_ref, core), (passed_ref, 1 - core)):
        rows = pl.ds(pl.multiple_of(which * block, block), block)
        ref[:, :wide] = tokens_ref[rows, :]
        ref[:, wide:] = grad_ref[rows, :]


def whole(kernel, place, arrays, shapes):
    return pl.pallas_call(
        kernel,
        in_specs=[pl.BlockSpec(memory_space=pltpu.SMEM)]
        + [pl.BlockSpec(memory_space=pltpu.VMEM)] * len(arrays),
        out_specs=[pl.BlockSpec(memory_space=pltpu.VMEM)] * len(shapes),
        out_shape=[jax.ShapeDtypeStruct(shape, BF) for shape in shapes],
        compiler_params=pltpu.CompilerParams(vmem_limit_bytes=8 * 2**20),
        cost_estimate=cost(flops=0, bytes_accessed=0, transcendentals=0),
    )(place, *arrays)


def cut(place, tokens, out_grad):
    rows, wide = tokens.shape
    return whole(cut_kernel, place, [tokens, out_grad], [(rows // 2, 2 * wide)] * 2)


def join_kernel(place_ref, a_ref, b_ref, out_ref):
    rows = a_ref.shape[0]
    out_ref[:rows, :] = a_ref[...]
    out_ref[rows:, :] = b_ref[...]


def join(place, a, b):
    return whole(join_kernel, place, [a, b], [(2 * a.shape[0], a.shape[1])])[0]


def assemble_kernel(keep, place_ref, a_ref, b_ref, c_ref, out_ref):
    rows = a_ref.shape[0]
    part = rows // PARTS

    def put(i, ref, first):
        for j in range(PARTS):
            at = pl.multiple_of((j * RING + slot_of(keep, place_ref, i)) * part, part)
            out_ref[pl.ds(at, part), :] = ref[first + j * part:first + (j + 1) * part, :]

    put(0, a_ref, 0)
    put(1, b_ref, 0)
    put(2, c_ref, 0)
    put(3, c_ref, rows)


def assemble(keep, place, a, b, c):
    rows, wide = a.shape
    kernel = functools.partial(assemble_kernel, keep)
    return whole(kernel, place, [a, b, c], [(RING * rows, wide)])[0]


def regroup_kernel(place_ref, own_ref, near_ref, a_ref, b_ref):
    half = own_ref.shape[0] // 2
    for i, out_ref in enumerate((a_ref, b_ref)):
        out_ref[:half, :] = own_ref[i * half:(i + 1) * half, :]
        out_ref[half:, :] = near_ref[i * half:(i + 1) * half, :]


def regroup(place, own, near):
    return whole(regroup_kernel, place, [own, near], [own.shape] * 2)


def order_of(keep):
    return (0, 1, 2, 3) if keep else (0, 2, 1, 3)


def panel_at(piece, slot):
    return piece // 2, (piece % 2) * RING + slot


def hidden_at(keep, piece, slot):
    return slot // 2, (slot % 2) * RING + order_of(keep).index(piece)


def pair_kernel(keep, hidden, added, split, block, place_ref, *refs):
    a_refs, (left_ref, right_ref), rest = refs[:2], refs[2:4], refs[4:]
    if added:
        more_ref, rest = rest[0], rest[1:]
    rows_ref = rest[-1]
    out_refs = rest[:-1]

    @pl.when(pl.program_id(1) == 0)
    def _():
        if hidden:
            size = RING * block
            for i in range(RING):
                at = pl.multiple_of(arrival_of(keep, place_ref, i) * size, size)
                first = (i % 2) * size
                rows_ref[pl.ds(at, size), :] = a_refs[i // 2][first:first + size, :]
        else:
            for i in range(RING):
                for j, piece in enumerate(order_of(keep)):
                    which, first = panel_at(piece, i)
                    at = (i * RING + j) * block
                    rows_ref[at:at + block, :] = a_refs[which][first * block:(first + 1) * block, :]

    def finish(total):
        if added:
            total = total + more_ref[...].astype(F32)
        total = total.astype(BF)
        if not split:
            out_refs[0][...] = total
        else:
            half = total.shape[0] // 2
            out_refs[0][...] = total[:half]
            out_refs[1][...] = total[half:]

    @pl.when(pl.program_id(0) == 0)
    def _():
        finish(lax.dot_general(rows_ref[...], left_ref[...], NN, preferred_element_type=F32))

    @pl.when(pl.program_id(0) == 1)
    def _():
        finish(lax.dot_general(rows_ref[...], right_ref[...], NT, preferred_element_type=F32))


def pair_dot(keep, hidden, pair, left, right, place, more=None, split=True, tile=512):
    rows = sum(a.shape[0] for a in pair)
    block = rows // RING // RING
    depth, wide = left.shape
    tiles = wide // tile
    in_specs = [pl.BlockSpec((a.shape[0], depth), lambda h, n, place: (0, h)) for a in pair]
    in_specs += [
        pl.BlockSpec((depth, tile), lambda h, n, place: (0, n * (1 - h) + (tiles - 1) * h)),
        pl.BlockSpec((tile, depth), lambda h, n, place: (n * h, 0)),
    ]
    out_of = lambda n_rows: pl.BlockSpec((n_rows, tile), lambda h, n, place: (0, h * tiles + n))
    args = [*pair, left, right]
    if more is not None:
        in_specs.append(out_of(rows))
        args.append(more)
    outs = [rows // 2, rows // 2] if split else [rows]
    result = pl.pallas_call(
        functools.partial(pair_kernel, keep, hidden, more is not None, split, block),
        grid_spec=pltpu.PrefetchScalarGridSpec(
            num_scalar_prefetch=1,
            grid=(2, tiles),
            in_specs=in_specs,
            out_specs=[out_of(n) for n in outs],
            scratch_shapes=[pltpu.VMEM((rows, depth), BF)],
        ),
        out_shape=[jax.ShapeDtypeStruct((n, 2 * wide), BF) for n in outs],
        compiler_params=pltpu.CompilerParams(vmem_limit_bytes=18 * 2**20),
        cost_estimate=cost(
            flops=4 * rows * depth * wide,
            bytes_accessed=4 * depth * wide + 8 * rows * wide,
            transcendentals=0,
        ),
    )(place, *args)
    return result if split else result[0]


def grad_kernel(pairs, block, factor, begun, *refs):
    lefts, rights, out_ref = refs[:4], refs[4:8], refs[-1]
    total = None
    for i, blocks in enumerate(pairs):
        right = jnp.concatenate(
            [rights[j][first * block:(first + 1) * block, :] for j, first in blocks], axis=0
        )
        term = lax.dot_general(lefts[i][...], right, TN, preferred_element_type=F32)
        total = term if total is None else total + term
    total = total * factor
    out_ref[...] = total + refs[8][...] if begun else total


def grad_dot(lefts, left_part, rights, right_part, pairs, factor, begun=None, tile=256):
    wide = lefts[0].shape[1] // 2
    tiles = wide // tile
    tokens = sum(a.shape[0] for a in lefts)
    args = [*lefts, *rights]
    in_specs = [pl.BlockSpec((a.shape[0], wide), lambda n: (0, left_part)) for a in lefts]
    in_specs += [
        pl.BlockSpec((a.shape[0], tile), lambda n: (0, right_part * tiles + n)) for a in rights
    ]
    out_spec = pl.BlockSpec((wide, tile), lambda n: (0, n))
    aliases = {}
    if begun is not None:
        aliases = {len(args): 0}
        args.append(begun)
        in_specs.append(out_spec)
    block = rights[0].shape[0] // (2 * RING)
    return pl.pallas_call(
        functools.partial(grad_kernel, pairs, block, factor, begun is not None),
        grid=(tiles,),
        in_specs=in_specs,
        out_specs=out_spec,
        out_shape=jax.ShapeDtypeStruct((wide, wide), F32),
        input_output_aliases=aliases,
        compiler_params=pltpu.CompilerParams(vmem_limit_bytes=24 * 2**20),
        cost_estimate=cost(
            flops=2 * tokens * wide * wide,
            bytes_accessed=3 * tokens * wide + 2 * wide * wide,
            transcendentals=0,
        ),
    )(*args)


def after(value, *events):
    return lax.optimization_barrier((value, *events))[0]


def shards(tokens, out_grad, weight_in, weight_out):
    core = lax.axis_index("row") % 2
    z = lax.axis_index("row") // 2
    dp = lax.axis_index("dp")
    rows, width = tokens.shape
    block = rows // 2
    inner = weight_in.shape[1] // 2
    factor = 1.0 / math.sqrt(rows * 16)
    both_ways = (True, False)

    place = jnp.stack([z, core]).astype(jnp.int32)
    w_in = lax.dynamic_slice_in_dim(weight_in, dp * inner, inner, 1)
    w_out = lax.dynamic_slice_in_dim(weight_out, dp * inner, inner, 0)

    order = (False, True)
    start, one, two, own, near_a, near_b = {}, {}, {}, {}, {}, {}
    start[True], start[False] = cut(place, tokens, out_grad)
    for keep in order:
        one[keep] = exchange(start[keep], along(keep, True, 0))
    for keep in order:
        two[keep] = exchange(join(place, start[keep], one[keep]), along(keep, True, 1))
    for keep in order:
        own[keep] = assemble(keep, place, start[keep], one[keep], two[keep])

    def others(near):
        return {keep: exchange(near[keep], along(keep, False, 1)) for keep in order}

    def panel_dot(keep, near, rest, *events, more=None):
        pair = [near[keep], after(rest[keep], *events) if events else rest[keep]]
        return pair_dot(keep, False, pair, w_in, w_out, place, more=more, split=keep)

    def out_dot(keep, pair, *events):
        pair = list(pair)
        pair[1] = after(pair[1], *events) if events else pair[1]
        return pair_dot(keep, True, pair, w_out, w_in, place)

    def halfway(kept, got):
        half = kept.shape[0] // 2
        sums = kept.astype(F32) + got.astype(F32)
        return [sums[:half], sums[half:]]

    def half_sum(kept, got):
        return (kept.astype(F32) + got.astype(F32)).astype(BF)

    def hidden_of(half, got):
        rows = half.shape[0] // 2
        other = jnp.concatenate([got[rows:], got[:rows]], axis=0)
        value = half.astype(F32) + other.astype(F32)
        pre, back = value[:, :width], value[:, width:]
        activated, slope = gelu_parts(pre)
        return jnp.concatenate([activated.astype(BF), (back * slope).astype(BF)], axis=1)

    both = lax.optimization_barrier((own[True], own[False]))
    own = {True: both[0], False: both[1]}
    near = {keep: exchange(own[keep], along(keep, False, 0)) for keep in order}
    for keep in order:
        near_a[keep], near_b[keep] = regroup(place, own[keep], near[keep])
    rest_a = others(near_a)
    rest_b = others(near_b)
    sent_a = panel_dot(False, near_a, rest_a, rest_a[True])
    kept_a, send_a = panel_dot(True, near_a, rest_a, more=exchange(sent_a, other_core))
    sent_b = panel_dot(False, near_b, rest_b, rest_b[True], send_a)
    step_a = after(exchange(send_a, along_z(0)), sent_b)
    half_a = half_sum(kept_a, step_a)
    turn_a = exchange(half_a, along_z(1))
    kept_b, send_b = panel_dot(
        True, near_b, rest_b, step_a, more=exchange(sent_b, other_core)
    )
    pair_a = hidden_of(half_a, after(turn_a, send_b))
    step_b = exchange(after(send_b, turn_a), along_z(0))
    far_a = exchange(pair_a, along_z(0))
    hid_a = {True: (pair_a, far_a)}
    hid_a[False] = (exchange(pair_a, other_core), exchange(far_a, other_core))

    in_pairs, out_pairs = [], []
    for base, keep in ((0, True), (2, False)):
        for i in range(2):
            in_pairs.append(
                tuple(
                    (base + hidden_at(keep, 2 * i + p, slot)[0], hidden_at(keep, 2 * i + p, slot)[1])
                    for p in range(2)
                    for slot in range(RING)
                )
            )
            out_pairs.append(
                tuple(
                    (base + panel_at(piece, 2 * i + s)[0], panel_at(piece, 2 * i + s)[1])
                    for s in range(2)
                    for piece in order_of(keep)
                )
            )

    def grads(which, near, rest, hid, begun, *events):
        panels = [near[True], rest[True], near[False], rest[False]]
        hiddens = [*hid[True], *hid[False]]
        lefts, rights, pairs = (
            (panels, hiddens, in_pairs) if which == 0 else (hiddens, panels, out_pairs)
        )
        lefts[0] = after(lefts[0], *events)
        return grad_dot(lefts, 0, rights, 1, pairs, factor, begun)

    def second_half(keep, kept, got):
        sums = halfway(kept, got)
        return sums[0], exchange(sums[1].astype(BF), along(keep, True, 0))

    out_a, out_b, got_a, got_b = {}, {}, {}, {}
    sums_a, sums_b, last_a, last_b, total_a, total_b = {}, {}, {}, {}, {}, {}
    out_a[True] = out_dot(True, hid_a[True])
    half_b = half_sum(kept_b, after(step_b, out_a[True][0]))
    turn_b = exchange(half_b, along_z(1))
    out_a[False] = out_dot(False, hid_a[False], out_a[True][0], step_b)
    for keep in both_ways:
        got_a[keep] = exchange(out_a[keep][1], along(keep, True, 1))
    grad_in = grads(0, near_a, rest_a, hid_a, None, out_a[False][0])
    pair_b = hidden_of(half_b, after(turn_b, grad_in))
    far_b = exchange(pair_b, along_z(0))
    grad_out = grads(1, near_a, rest_a, hid_a, None, turn_b, got_a[True], got_a[False], grad_in)
    for keep in both_ways:
        got = after(got_a[keep], grad_in, got_a[not keep])
        sums_a[keep], last_a[keep] = second_half(keep, out_a[keep][0], got)
    far_b = after(far_b, grad_out, last_a[True], last_a[False])
    hid_b = {True: (pair_b, far_b)}
    hid_b[False] = (exchange(pair_b, other_core), exchange(far_b, other_core))

    out_b[True] = out_dot(True, hid_b[True])
    out_b[False] = out_dot(False, hid_b[False], out_b[True][0])
    for keep in both_ways:
        got_b[keep] = exchange(out_b[keep][1], along(keep, True, 1))
    grad_in = grads(
        0, near_b, rest_b, hid_b, grad_in, out_b[False][0]
    )
    for keep in both_ways:
        got = after(got_b[keep], grad_in, got_b[not keep])
        sums_b[keep], last_b[keep] = second_half(keep, out_b[keep][0], got)
    grad_out = grads(1, near_b, rest_b, hid_b, grad_out, got_b[True], got_b[False], grad_in)
    for keep in both_ways:
        total_a[keep] = sums_a[keep] + last_a[keep].astype(F32)
        total_b[keep] = sums_b[keep] + after(last_b[keep], grad_out, last_b[not keep]).astype(F32)

    part = block // PARTS
    pick = lambda keep, piece: jnp.concatenate(
        [
            total[keep][order_of(keep).index(piece) * part:(order_of(keep).index(piece) + 1) * part]
            for total in (total_a, total_b)
        ],
        axis=0,
    )
    gots, done = {}, {}
    for keep in both_ways:
        passed = jnp.concatenate([pick(keep, 2), pick(keep, 3)], axis=0).astype(BF)
        gots[keep] = exchange(passed, along(keep, False, 1))
    for keep in both_ways:
        got = after(gots[keep], gots[not keep]).astype(F32)
        last = (pick(keep, 1) + got[block:]).astype(BF)
        done[keep] = (
            pick(keep, 0) + got[:block] + exchange(last, along(keep, False, 0)).astype(F32)
        ).astype(BF)

    low = jnp.where(core == 0, done[True], done[False])
    high = jnp.where(core == 0, done[False], done[True])
    result = jnp.concatenate([low, high], axis=0)
    return (result[:, :width], result[:, width:], grad_in, grad_out)


def solution(mesh):
    placed = (P(("col", "dp"), "row"), P(("col", "dp"), "row"), P("row", "col"), P("col", "row"))
    return jax.shard_map(
        shards,
        mesh=mesh,
        in_specs=placed,
        out_specs=(
            P(("col", "dp"), "row"),
            P(("col", "dp"), "row"),
            P("row", ("col", "dp")),
            P(("col", "dp"), "row"),
        ),
        check_vma=False,
    )
```

```python
import functools
import math

import jax
import jax.numpy as jnp
from jax import lax
from jax.experimental import pallas as pl
from jax.experimental.pallas import tpu as pltpu
from jax.sharding import PartitionSpec as P

AXES = ("row", "col", "dp")
RING = 4
PARTS = 2
BF = jnp.bfloat16
F32 = jnp.float32
NN = (((1,), (0,)), ((), ()))
NT = (((1,), (1,)), ((), ()))
TN = (((0,), (0,)), ((), ()))


def cost(flops, bytes_accessed, transcendentals):
    return pl.CostEstimate(
        flops=flops // 1000, bytes_accessed=bytes_accessed // 1000, transcendentals=transcendentals
    )


def gelu_parts(pre):
    cdf = 0.5 * (1.0 + jax.scipy.special.erf(pre * (1.0 / math.sqrt(2.0))))
    activated = pre * cdf
    slope = cdf + pre * jnp.exp(-0.5 * pre * pre) * (1.0 / math.sqrt(2.0 * math.pi))
    return (activated, slope)


def flat(z, c, x, y):
    return ((z * 2 + c) * RING + x) * RING + y


def exchange(array, partner):
    pairs = []
    for z in range(RING):
        for c in range(2):
            for x in range(RING):
                for y in range(RING):
                    pairs.append((flat(*partner(z, c, x, y)), flat(z, c, x, y)))
    return lax.ppermute(array, AXES, pairs)


NEAR = ((1, 3), (3, 1))
Z_PAIR = ((1, 3), (3, 1))
OWNER_SLOT = ((0, 2, 3, 1), (0, 1, 3, 2))


def along(keep, first, turn):
    def partner(z, c, x, y):
        half = c if keep else 1 - c
        step = NEAR[c][turn]
        if (half == 0) == first:
            return (z, c, x ^ step, y)
        return (z, c, x, y ^ step)

    return partner


def along_z(turn):
    return lambda z, c, x, y: (z ^ Z_PAIR[c][turn], c, x, y)


def other_core(z, c, x, y):
    return (z, 1 - c, x, y)


def slot_of(keep, place_ref, i):
    z, core = place_ref[0], place_ref[1]

    def one(c):
        near = NEAR[c]
        owned = z ^ (0, near[0], near[1], near[0] ^ near[1])[i]
        table = OWNER_SLOT[c if keep else 1 - c]
        slot = jnp.int32(table[0])
        for j in range(1, RING):
            slot = jnp.where(owned == j, table[j], slot)
        return slot

    return jnp.where(core == 0, one(0), one(1))


def arrival_of(keep, place_ref, i):
    z, core = place_ref[0], place_ref[1]

    def one(c):
        near = NEAR[c]
        arrival = (0, near[0], near[1], near[0] ^ near[1])
        owned = z ^ OWNER_SLOT[c if keep else 1 - c].index(i)
        place = jnp.int32(arrival.index(0))
        for j in range(1, RING):
            place = jnp.where(owned == j, arrival.index(j), place)
        return place

    return jnp.where(core == 0, one(0), one(1))


def cut_kernel(place_ref, tokens_ref, grad_ref, kept_ref, passed_ref):
    block, wide = kept_ref.shape[0], tokens_ref.shape[1]
    core = place_ref[1]
    for ref, which in ((kept_ref, core), (passed_ref, 1 - core)):
        rows = pl.ds(pl.multiple_of(which * block, block), block)
        ref[:, :wide] = tokens_ref[rows, :]
        ref[:, wide:] = grad_ref[rows, :]


def whole(kernel, place, arrays, shapes):
    return pl.pallas_call(
        kernel,
        in_specs=[pl.BlockSpec(memory_space=pltpu.SMEM)]
        + [pl.BlockSpec(memory_space=pltpu.VMEM)] * len(arrays),
        out_specs=[pl.BlockSpec(memory_space=pltpu.VMEM)] * len(shapes),
        out_shape=[jax.ShapeDtypeStruct(shape, BF) for shape in shapes],
        compiler_params=pltpu.CompilerParams(vmem_limit_bytes=8 * 2**20),
        cost_estimate=cost(flops=0, bytes_accessed=0, transcendentals=0),
    )(place, *arrays)


def cut(place, tokens, out_grad):
    rows, wide = tokens.shape
    return whole(cut_kernel, place, [tokens, out_grad], [(rows // 2, 2 * wide)] * 2)


def join_kernel(place_ref, a_ref, b_ref, out_ref):
    rows = a_ref.shape[0]
    out_ref[:rows, :] = a_ref[...]
    out_ref[rows:, :] = b_ref[...]


def join(place, a, b):
    return whole(join_kernel, place, [a, b], [(2 * a.shape[0], a.shape[1])])[0]


def assemble_kernel(keep, place_ref, a_ref, b_ref, c_ref, *out_refs):
    rows = a_ref.shape[0]
    part = rows // PARTS

    def put(i, ref, first):
        at = pl.multiple_of(slot_of(keep, place_ref, i) * part, part)
        for j, out_ref in enumerate(out_refs):
            out_ref[pl.ds(at, part), :] = ref[first + j * part:first + (j + 1) * part, :]

    put(0, a_ref, 0)
    put(1, b_ref, 0)
    put(2, c_ref, 0)
    put(3, c_ref, rows)


def assemble(keep, place, a, b, c):
    rows, wide = a.shape
    kernel = functools.partial(assemble_kernel, keep)
    return whole(kernel, place, [a, b, c], [(RING * rows // PARTS, wide)] * PARTS)


def order_of(keep):
    return (0, 1, 2, 3) if keep else (0, 2, 1, 3)


def panel_at(piece, slot):
    return piece // 2, (piece % 2) * RING + slot


def hidden_at(keep, piece, slot):
    return slot // 2, (slot % 2) * RING + order_of(keep).index(piece)


def pair_kernel(keep, hidden, added, split, block, place_ref, *refs):
    a_refs, (left_ref, right_ref), rest = refs[:2], refs[2:4], refs[4:]
    if added:
        more_ref, rest = rest[0], rest[1:]
    rows_ref = rest[-1]
    out_refs = rest[:-1]

    @pl.when(pl.program_id(1) == 0)
    def _():
        if hidden:
            size = RING * block
            for i in range(RING):
                at = pl.multiple_of(arrival_of(keep, place_ref, i) * size, size)
                first = (i % 2) * size
                rows_ref[pl.ds(at, size), :] = a_refs[i // 2][first:first + size, :]
        else:
            for i in range(RING):
                for j, piece in enumerate(order_of(keep)):
                    which, first = panel_at(piece, i)
                    at = (i * RING + j) * block
                    rows_ref[at:at + block, :] = a_refs[which][first * block:(first + 1) * block, :]

    def finish(total):
        if added:
            total = total + more_ref[...].astype(F32)
        total = total.astype(BF)
        if not split:
            out_refs[0][...] = total
        else:
            half = total.shape[0] // 2
            out_refs[0][...] = total[:half]
            out_refs[1][...] = total[half:]

    @pl.when(pl.program_id(0) == 0)
    def _():
        finish(lax.dot_general(rows_ref[...], left_ref[...], NN, preferred_element_type=F32))

    @pl.when(pl.program_id(0) == 1)
    def _():
        finish(lax.dot_general(rows_ref[...], right_ref[...], NT, preferred_element_type=F32))


def pair_dot(keep, hidden, pair, left, right, place, more=None, split=True, tile=512):
    rows = sum(a.shape[0] for a in pair)
    block = rows // RING // RING
    depth, wide = left.shape
    tiles = wide // tile
    in_specs = [pl.BlockSpec((a.shape[0], depth), lambda h, n, place: (0, h)) for a in pair]
    in_specs += [
        pl.BlockSpec((depth, tile), lambda h, n, place: (0, n * (1 - h) + (tiles - 1) * h)),
        pl.BlockSpec((tile, depth), lambda h, n, place: (n * h, 0)),
    ]
    out_of = lambda n_rows: pl.BlockSpec((n_rows, tile), lambda h, n, place: (0, h * tiles + n))
    args = [*pair, left, right]
    if more is not None:
        in_specs.append(out_of(rows))
        args.append(more)
    outs = [rows // 2, rows // 2] if split else [rows]
    result = pl.pallas_call(
        functools.partial(pair_kernel, keep, hidden, more is not None, split, block),
        grid_spec=pltpu.PrefetchScalarGridSpec(
            num_scalar_prefetch=1,
            grid=(2, tiles),
            in_specs=in_specs,
            out_specs=[out_of(n) for n in outs],
            scratch_shapes=[pltpu.VMEM((rows, depth), BF)],
        ),
        out_shape=[jax.ShapeDtypeStruct((n, 2 * wide), BF) for n in outs],
        compiler_params=pltpu.CompilerParams(vmem_limit_bytes=18 * 2**20),
        cost_estimate=cost(
            flops=4 * rows * depth * wide,
            bytes_accessed=4 * depth * wide + 8 * rows * wide,
            transcendentals=0,
        ),
    )(place, *args)
    return result if split else result[0]


def grad_kernel(pairs, block, factor, begun, *refs):
    lefts, rights, out_ref = refs[:4], refs[4:8], refs[-1]
    total = None
    for i, blocks in enumerate(pairs):
        right = jnp.concatenate(
            [rights[j][first * block:(first + 1) * block, :] for j, first in blocks], axis=0
        )
        term = lax.dot_general(lefts[i][...], right, TN, preferred_element_type=F32)
        total = term if total is None else total + term
    total = total * factor
    out_ref[...] = total + refs[8][...] if begun else total


def grad_dot(lefts, left_part, rights, right_part, pairs, factor, begun=None, tile=256):
    wide = lefts[0].shape[1] // 2
    tiles = wide // tile
    tokens = sum(a.shape[0] for a in lefts)
    args = [*lefts, *rights]
    in_specs = [pl.BlockSpec((a.shape[0], wide), lambda n: (0, left_part)) for a in lefts]
    in_specs += [
        pl.BlockSpec((a.shape[0], tile), lambda n: (0, right_part * tiles + n)) for a in rights
    ]
    out_spec = pl.BlockSpec((wide, tile), lambda n: (0, n))
    aliases = {}
    if begun is not None:
        aliases = {len(args): 0}
        args.append(begun)
        in_specs.append(out_spec)
    block = rights[0].shape[0] // (2 * RING)
    return pl.pallas_call(
        functools.partial(grad_kernel, pairs, block, factor, begun is not None),
        grid=(tiles,),
        in_specs=in_specs,
        out_specs=out_spec,
        out_shape=jax.ShapeDtypeStruct((wide, wide), F32),
        input_output_aliases=aliases,
        compiler_params=pltpu.CompilerParams(vmem_limit_bytes=24 * 2**20),
        cost_estimate=cost(
            flops=2 * tokens * wide * wide,
            bytes_accessed=3 * tokens * wide + 2 * wide * wide,
            transcendentals=0,
        ),
    )(*args)


def after(value, *events):
    return lax.optimization_barrier((value, *events))[0]


def shards(tokens, out_grad, weight_in, weight_out):
    core = lax.axis_index("row") % 2
    z = lax.axis_index("row") // 2
    dp = lax.axis_index("dp")
    rows, width = tokens.shape
    block = rows // 2
    inner = weight_in.shape[1] // 2
    factor = 1.0 / math.sqrt(rows * 16)
    both_ways = (True, False)

    place = jnp.stack([z, core]).astype(jnp.int32)
    w_in = lax.dynamic_slice_in_dim(weight_in, dp * inner, inner, 1)
    w_out = lax.dynamic_slice_in_dim(weight_out, dp * inner, inner, 0)

    order = (False, True)
    start, one, two, own_a, own_b = {}, {}, {}, {}, {}
    start[True], start[False] = cut(place, tokens, out_grad)
    for keep in order:
        one[keep] = exchange(start[keep], along(keep, True, 0))
    for keep in order:
        two[keep] = exchange(join(place, start[keep], one[keep]), along(keep, True, 1))
    for keep in order:
        own_a[keep], own_b[keep] = assemble(keep, place, start[keep], one[keep], two[keep])

    def others(near):
        return {keep: exchange(near[keep], along(keep, False, 1)) for keep in order}

    def panel_dot(keep, near, rest, *events, more=None):
        pair = [near[keep], after(rest[keep], *events) if events else rest[keep]]
        return pair_dot(keep, False, pair, w_in, w_out, place, more=more, split=keep)

    def out_dot(keep, pair, *events):
        pair = list(pair)
        pair[1] = after(pair[1], *events) if events else pair[1]
        return pair_dot(keep, True, pair, w_out, w_in, place)

    def halfway(kept, got):
        half = kept.shape[0] // 2
        sums = kept.astype(F32) + got.astype(F32)
        return [sums[:half], sums[half:]]

    def half_sum(kept, got):
        return (kept.astype(F32) + got.astype(F32)).astype(BF)

    def hidden_of(half, got):
        rows = half.shape[0] // 2
        other = jnp.concatenate([got[rows:], got[:rows]], axis=0)
        value = half.astype(F32) + other.astype(F32)
        pre, back = value[:, :width], value[:, width:]
        activated, slope = gelu_parts(pre)
        return jnp.concatenate([activated.astype(BF), (back * slope).astype(BF)], axis=1)

    def neighbours(own):
        return {keep: exchange(own[keep], along(keep, False, 0)) for keep in order}

    def joined(own, near):
        return {keep: join(place, own[keep], near[keep]) for keep in order}

    both = lax.optimization_barrier((own_a[True], own_a[False]))
    own_a = {True: both[0], False: both[1]}
    near_a = joined(own_a, neighbours(own_a))
    rest_a = others(near_a)
    near_of_b = neighbours(own_b)
    sent_a = panel_dot(False, near_a, rest_a, rest_a[True])
    kept_a, send_a = panel_dot(True, near_a, rest_a, more=exchange(sent_a, other_core))
    near_b = joined(own_b, {keep: after(near_of_b[keep], send_a) for keep in order})
    rest_b = others(near_b)
    step_a = after(exchange(send_a, along_z(0)), rest_b[True], rest_b[False])
    sent_b = panel_dot(False, near_b, rest_b, step_a)
    half_a = half_sum(kept_a, step_a)
    turn_a = exchange(half_a, along_z(1))
    kept_b, send_b = panel_dot(
        True, near_b, rest_b, more=exchange(sent_b, other_core)
    )
    pair_a = hidden_of(half_a, after(turn_a, send_b))
    step_b = exchange(after(send_b, turn_a), along_z(0))
    far_a = exchange(pair_a, along_z(0))
    hid_a = {True: (pair_a, far_a)}
    hid_a[False] = (exchange(pair_a, other_core), exchange(far_a, other_core))

    in_pairs, out_pairs = [], []
    for base, keep in ((0, True), (2, False)):
        for i in range(2):
            in_pairs.append(
                tuple(
                    (base + hidden_at(keep, 2 * i + p, slot)[0], hidden_at(keep, 2 * i + p, slot)[1])
                    for p in range(2)
                    for slot in range(RING)
                )
            )
            out_pairs.append(
                tuple(
                    (base + panel_at(piece, 2 * i + s)[0], panel_at(piece, 2 * i + s)[1])
                    for s in range(2)
                    for piece in order_of(keep)
                )
            )

    def grads(which, near, rest, hid, begun, *events):
        panels = [near[True], rest[True], near[False], rest[False]]
        hiddens = [*hid[True], *hid[False]]
        lefts, rights, pairs = (
            (panels, hiddens, in_pairs) if which == 0 else (hiddens, panels, out_pairs)
        )
        lefts[0] = after(lefts[0], *events)
        return grad_dot(lefts, 0, rights, 1, pairs, factor, begun)

    def second_half(keep, kept, got):
        sums = halfway(kept, got)
        return sums[0], exchange(sums[1].astype(BF), along(keep, True, 0))

    out_a, out_b, got_a, got_b = {}, {}, {}, {}
    sums_a, sums_b, last_a, last_b, total_a, total_b = {}, {}, {}, {}, {}, {}
    out_a[True] = out_dot(True, hid_a[True])
    half_b = half_sum(kept_b, after(step_b, out_a[True][0]))
    turn_b = exchange(half_b, along_z(1))
    out_a[False] = out_dot(False, hid_a[False], out_a[True][0], step_b)
    for keep in both_ways:
        got_a[keep] = exchange(out_a[keep][1], along(keep, True, 1))
    grad_in = grads(0, near_a, rest_a, hid_a, None, out_a[False][0])
    pair_b = hidden_of(half_b, after(turn_b, grad_in))
    far_b = exchange(pair_b, along_z(0))
    grad_out = grads(1, near_a, rest_a, hid_a, None, turn_b, got_a[True], got_a[False], grad_in)
    for keep in both_ways:
        got = after(got_a[keep], grad_in, got_a[not keep])
        sums_a[keep], last_a[keep] = second_half(keep, out_a[keep][0], got)
    far_b = after(far_b, grad_out, last_a[True], last_a[False])
    hid_b = {True: (pair_b, far_b)}
    hid_b[False] = (exchange(pair_b, other_core), exchange(far_b, other_core))

    out_b[True] = out_dot(True, hid_b[True], hid_b[False][0])
    out_b[False] = out_dot(False, hid_b[False], out_b[True][0])
    for keep in both_ways:
        got_b[keep] = exchange(out_b[keep][1], along(keep, True, 1))
    grad_in = grads(
        0, near_b, rest_b, hid_b, grad_in, out_b[False][0]
    )
    for keep in both_ways:
        got = after(got_b[keep], grad_in, got_b[not keep])
        sums_b[keep], last_b[keep] = second_half(keep, out_b[keep][0], got)
    grad_out = grads(1, near_b, rest_b, hid_b, grad_out, got_b[True], got_b[False], grad_in)
    for keep in both_ways:
        total_a[keep] = sums_a[keep] + last_a[keep].astype(F32)
        total_b[keep] = sums_b[keep] + after(last_b[keep], grad_out, last_b[not keep]).astype(F32)

    part = block // PARTS
    pick = lambda keep, piece: jnp.concatenate(
        [
            total[keep][order_of(keep).index(piece) * part:(order_of(keep).index(piece) + 1) * part]
            for total in (total_a, total_b)
        ],
        axis=0,
    )
    gots, done = {}, {}
    for keep in both_ways:
        passed = jnp.concatenate([pick(keep, 2), pick(keep, 3)], axis=0).astype(BF)
        gots[keep] = exchange(passed, along(keep, False, 1))
    for keep in both_ways:
        got = after(gots[keep], gots[not keep]).astype(F32)
        last = (pick(keep, 1) + got[block:]).astype(BF)
        done[keep] = (
            pick(keep, 0) + got[:block] + exchange(last, along(keep, False, 0)).astype(F32)
        ).astype(BF)

    low = jnp.where(core == 0, done[True], done[False])
    high = jnp.where(core == 0, done[False], done[True])
    result = jnp.concatenate([low, high], axis=0)
    return (result[:, :width], result[:, width:], grad_in, grad_out)


def solution(mesh):
    placed = (P(("col", "dp"), "row"), P(("col", "dp"), "row"), P("row", "col"), P("col", "row"))
    return jax.shard_map(
        shards,
        mesh=mesh,
        in_specs=placed,
        out_specs=(
            P(("col", "dp"), "row"),
            P(("col", "dp"), "row"),
            P("row", ("col", "dp")),
            P(("col", "dp"), "row"),
        ),
        check_vma=False,
    )
```

```python
import functools
import math

import jax
import jax.numpy as jnp
from jax import lax
from jax.experimental import pallas as pl
from jax.experimental.pallas import tpu as pltpu
from jax.sharding import PartitionSpec as P

AXES = ("row", "col", "dp")
RING = 4
PARTS = 2
BF = jnp.bfloat16
F32 = jnp.float32
NN = (((1,), (0,)), ((), ()))
NT = (((1,), (1,)), ((), ()))
TN = (((0,), (0,)), ((), ()))


def cost(flops, bytes_accessed, transcendentals):
    return pl.CostEstimate(
        flops=flops // 1000, bytes_accessed=bytes_accessed // 1000, transcendentals=transcendentals
    )


def gelu_parts(pre):
    cdf = 0.5 * (1.0 + jax.scipy.special.erf(pre * (1.0 / math.sqrt(2.0))))
    activated = pre * cdf
    slope = cdf + pre * jnp.exp(-0.5 * pre * pre) * (1.0 / math.sqrt(2.0 * math.pi))
    return (activated, slope)


def flat(z, c, x, y):
    return ((z * 2 + c) * RING + x) * RING + y


def exchange(array, partner):
    pairs = []
    for z in range(RING):
        for c in range(2):
            for x in range(RING):
                for y in range(RING):
                    pairs.append((flat(*partner(z, c, x, y)), flat(z, c, x, y)))
    return lax.ppermute(array, AXES, pairs)


NEAR = ((1, 3), (3, 1))
Z_PAIR = ((1, 3), (3, 1))
OWNER_SLOT = ((0, 2, 3, 1), (0, 1, 3, 2))


def along(keep, first, turn):
    def partner(z, c, x, y):
        half = c if keep else 1 - c
        step = NEAR[c][turn]
        if (half == 0) == first:
            return (z, c, x ^ step, y)
        return (z, c, x, y ^ step)

    return partner


def along_z(turn):
    return lambda z, c, x, y: (z ^ Z_PAIR[c][turn], c, x, y)


def other_core(z, c, x, y):
    return (z, 1 - c, x, y)


def slot_of(keep, place_ref, i):
    z, core = place_ref[0], place_ref[1]

    def one(c):
        near = NEAR[c]
        owned = z ^ (0, near[0], near[1], near[0] ^ near[1])[i]
        table = OWNER_SLOT[c if keep else 1 - c]
        slot = jnp.int32(table[0])
        for j in range(1, RING):
            slot = jnp.where(owned == j, table[j], slot)
        return slot

    return jnp.where(core == 0, one(0), one(1))


def arrival_of(keep, place_ref, i):
    z, core = place_ref[0], place_ref[1]

    def one(c):
        near = NEAR[c]
        arrival = (0, near[0], near[1], near[0] ^ near[1])
        owned = z ^ OWNER_SLOT[c if keep else 1 - c].index(i)
        place = jnp.int32(arrival.index(0))
        for j in range(1, RING):
            place = jnp.where(owned == j, arrival.index(j), place)
        return place

    return jnp.where(core == 0, one(0), one(1))


def cut_kernel(place_ref, tokens_ref, grad_ref, kept_ref, passed_ref, sems):
    block, wide = kept_ref.shape[0], tokens_ref.shape[1]
    core = place_ref[1]
    copies = []
    for ref, which in ((kept_ref, core), (passed_ref, 1 - core)):
        rows = pl.ds(pl.multiple_of(which * block, block), block)
        for i, source in enumerate((tokens_ref, grad_ref)):
            copies.append(
                pltpu.make_async_copy(
                    source.at[rows, :],
                    ref.at[:, i * wide:(i + 1) * wide],
                    sems.at[len(copies)],
                )
            )
    for copy in copies:
        copy.start()
    for copy in copies:
        copy.wait()


def whole(kernel, place, arrays, shapes):
    return pl.pallas_call(
        kernel,
        in_specs=[pl.BlockSpec(memory_space=pltpu.SMEM)]
        + [pl.BlockSpec(memory_space=pltpu.VMEM)] * len(arrays),
        out_specs=[pl.BlockSpec(memory_space=pltpu.VMEM)] * len(shapes),
        out_shape=[jax.ShapeDtypeStruct(shape, BF) for shape in shapes],
        compiler_params=pltpu.CompilerParams(vmem_limit_bytes=8 * 2**20),
        cost_estimate=cost(flops=0, bytes_accessed=0, transcendentals=0),
    )(place, *arrays)


def cut(place, tokens, out_grad):
    rows, wide = tokens.shape
    half = jax.ShapeDtypeStruct((rows // 2, 2 * wide), BF)
    return pl.pallas_call(
        cut_kernel,
        in_specs=[pl.BlockSpec(memory_space=pltpu.SMEM)]
        + [pl.BlockSpec(memory_space=pltpu.HBM)] * 2,
        out_specs=[pl.BlockSpec(memory_space=pltpu.VMEM)] * 2,
        out_shape=[half, half],
        scratch_shapes=[pltpu.SemaphoreType.DMA((4,))],
        compiler_params=pltpu.CompilerParams(vmem_limit_bytes=8 * 2**20),
        cost_estimate=cost(flops=0, bytes_accessed=0, transcendentals=0),
    )(place, tokens, out_grad)


def join_kernel(place_ref, a_ref, b_ref, out_ref):
    rows = a_ref.shape[0]
    out_ref[:rows, :] = a_ref[...]
    out_ref[rows:, :] = b_ref[...]


def join(place, a, b):
    return whole(join_kernel, place, [a, b], [(2 * a.shape[0], a.shape[1])])[0]


def assemble_kernel(keep, place_ref, a_ref, b_ref, c_ref, *out_refs):
    rows = a_ref.shape[0]
    part = rows // PARTS

    def put(i, ref, first):
        at = pl.multiple_of(slot_of(keep, place_ref, i) * part, part)
        for j, out_ref in enumerate(out_refs):
            out_ref[pl.ds(at, part), :] = ref[first + j * part:first + (j + 1) * part, :]

    put(0, a_ref, 0)
    put(1, b_ref, 0)
    put(2, c_ref, 0)
    put(3, c_ref, rows)


def assemble(keep, place, a, b, c):
    rows, wide = a.shape
    kernel = functools.partial(assemble_kernel, keep)
    return whole(kernel, place, [a, b, c], [(RING * rows // PARTS, wide)] * PARTS)


def order_of(keep):
    return (0, 1, 2, 3) if keep else (0, 2, 1, 3)


def panel_at(piece, slot):
    return piece // 2, (piece % 2) * RING + slot


def hidden_at(keep, piece, slot):
    return slot // 2, (slot % 2) * RING + order_of(keep).index(piece)


def pair_kernel(keep, hidden, added, split, side, block, place_ref, *refs):
    a_refs, (left_ref, right_ref), rest = refs[:2], refs[2:4], refs[4:]
    if added:
        more_ref, rest = rest[0], rest[1:]
    rows_ref = rest[-1]
    out_refs = rest[:-1]

    @pl.when(pl.program_id(1) == 0)
    def _():
        if hidden:
            size = RING * block
            for i in range(RING):
                at = pl.multiple_of(arrival_of(keep, place_ref, i) * size, size)
                first = (i % 2) * size
                rows_ref[pl.ds(at, size), :] = a_refs[i // 2][first:first + size, :]
        else:
            for i in range(RING):
                for j, piece in enumerate(order_of(keep)):
                    which, first = panel_at(piece, i)
                    at = (i * RING + j) * block
                    rows_ref[at:at + block, :] = a_refs[which][first * block:(first + 1) * block, :]

    def rows():
        if side is None:
            return rows_ref[...]
        half = rows_ref.shape[0] // 2
        return rows_ref[side * half:(side + 1) * half, :]

    def finish(total):
        if added:
            total = total + more_ref[...].astype(F32)
        total = total.astype(BF)
        if not split:
            out_refs[0][...] = total
        else:
            half = total.shape[0] // 2
            out_refs[0][...] = total[:half]
            out_refs[1][...] = total[half:]

    @pl.when(pl.program_id(0) == 0)
    def _():
        finish(lax.dot_general(rows(), left_ref[...], NN, preferred_element_type=F32))

    @pl.when(pl.program_id(0) == 1)
    def _():
        finish(lax.dot_general(rows(), right_ref[...], NT, preferred_element_type=F32))


def pair_dot(keep, hidden, pair, left, right, place, more=None, split=True, side=None, tile=512):
    rows = sum(a.shape[0] for a in pair)
    block = rows // RING // RING
    depth, wide = left.shape
    tiles = wide // tile
    in_specs = [pl.BlockSpec((a.shape[0], depth), lambda h, n, place: (0, h)) for a in pair]
    in_specs += [
        pl.BlockSpec((depth, tile), lambda h, n, place: (0, n * (1 - h) + (tiles - 1) * h)),
        pl.BlockSpec((tile, depth), lambda h, n, place: (n * h, 0)),
    ]
    out_of = lambda n_rows: pl.BlockSpec((n_rows, tile), lambda h, n, place: (0, h * tiles + n))
    args = [*pair, left, right]
    if more is not None:
        in_specs.append(out_of(rows))
        args.append(more)
    outs = [rows // 2, rows // 2] if split else [rows if side is None else rows // 2]
    result = pl.pallas_call(
        functools.partial(pair_kernel, keep, hidden, more is not None, split, side, block),
        grid_spec=pltpu.PrefetchScalarGridSpec(
            num_scalar_prefetch=1,
            grid=(2, tiles),
            in_specs=in_specs,
            out_specs=[out_of(n) for n in outs],
            scratch_shapes=[pltpu.VMEM((rows, depth), BF)],
        ),
        out_shape=[jax.ShapeDtypeStruct((n, 2 * wide), BF) for n in outs],
        compiler_params=pltpu.CompilerParams(vmem_limit_bytes=18 * 2**20),
        cost_estimate=cost(
            flops=4 * rows * depth * wide,
            bytes_accessed=4 * depth * wide + 8 * rows * wide,
            transcendentals=0,
        ),
    )(place, *args)
    return result if split else result[0]


def grad_kernel(pairs, block, factor, begun, *refs):
    lefts, rights, out_ref = refs[:4], refs[4:8], refs[-1]
    total = None
    for i, blocks in enumerate(pairs):
        right = jnp.concatenate(
            [rights[j][first * block:(first + 1) * block, :] for j, first in blocks], axis=0
        )
        term = lax.dot_general(lefts[i][...], right, TN, preferred_element_type=F32)
        total = term if total is None else total + term
    total = total * factor
    out_ref[...] = total + refs[8][...] if begun else total


def grad_dot(lefts, left_part, rights, right_part, pairs, factor, begun=None, tile=256):
    wide = lefts[0].shape[1] // 2
    tiles = wide // tile
    tokens = sum(a.shape[0] for a in lefts)
    args = [*lefts, *rights]
    in_specs = [pl.BlockSpec((a.shape[0], wide), lambda n: (0, left_part)) for a in lefts]
    in_specs += [
        pl.BlockSpec((a.shape[0], tile), lambda n: (0, right_part * tiles + n)) for a in rights
    ]
    out_spec = pl.BlockSpec((wide, tile), lambda n: (0, n))
    aliases = {}
    if begun is not None:
        aliases = {len(args): 0}
        args.append(begun)
        in_specs.append(out_spec)
    block = rights[0].shape[0] // (2 * RING)
    return pl.pallas_call(
        functools.partial(grad_kernel, pairs, block, factor, begun is not None),
        grid=(tiles,),
        in_specs=in_specs,
        out_specs=out_spec,
        out_shape=jax.ShapeDtypeStruct((wide, wide), F32),
        input_output_aliases=aliases,
        compiler_params=pltpu.CompilerParams(vmem_limit_bytes=24 * 2**20),
        cost_estimate=cost(
            flops=2 * tokens * wide * wide,
            bytes_accessed=3 * tokens * wide + 2 * wide * wide,
            transcendentals=0,
        ),
    )(*args)


def after(value, *events):
    return lax.optimization_barrier((value, *events))[0]


def shards(tokens, out_grad, weight_in, weight_out):
    core = lax.axis_index("row") % 2
    z = lax.axis_index("row") // 2
    dp = lax.axis_index("dp")
    rows, width = tokens.shape
    block = rows // 2
    inner = weight_in.shape[1] // 2
    factor = 1.0 / math.sqrt(rows * 16)
    both_ways = (True, False)

    place = jnp.stack([z, core]).astype(jnp.int32)
    w_in = lax.dynamic_slice_in_dim(weight_in, dp * inner, inner, 1)
    w_out = lax.dynamic_slice_in_dim(weight_out, dp * inner, inner, 0)

    order = (False, True)
    start, one, two, own_a, own_b = {}, {}, {}, {}, {}
    start[True], start[False] = cut(place, tokens, out_grad)
    for keep in order:
        one[keep] = exchange(start[keep], along(keep, True, 0))
    for keep in order:
        two[keep] = exchange(join(place, start[keep], one[keep]), along(keep, True, 1))
    for keep in order:
        own_a[keep], own_b[keep] = assemble(keep, place, start[keep], one[keep], two[keep])

    def others(near):
        return {keep: exchange(near[keep], along(keep, False, 1)) for keep in order}

    def panel_dot(keep, near, rest, *events, more=None):
        pair = [near[keep], after(rest[keep], *events) if events else rest[keep]]
        return pair_dot(keep, False, pair, w_in, w_out, place, more=more, split=keep)

    def out_dot(keep, pair, *events, side=None):
        pair = list(pair)
        pair[1] = after(pair[1], *events) if events else pair[1]
        return pair_dot(
            keep, True, pair, w_out, w_in, place, split=side is None, side=side
        )

    def halfway(kept, got):
        half = kept.shape[0] // 2
        sums = kept.astype(F32) + got.astype(F32)
        return [sums[:half], sums[half:]]

    def half_sum(kept, got):
        return (kept.astype(F32) + got.astype(F32)).astype(BF)

    def hidden_of(half, got):
        rows = half.shape[0] // 2
        other = jnp.concatenate([got[rows:], got[:rows]], axis=0)
        value = half.astype(F32) + other.astype(F32)
        pre, back = value[:, :width], value[:, width:]
        activated, slope = gelu_parts(pre)
        return jnp.concatenate([activated.astype(BF), (back * slope).astype(BF)], axis=1)

    def neighbours(own):
        return {keep: exchange(own[keep], along(keep, False, 0)) for keep in order}

    def joined(own, near):
        return {keep: join(place, own[keep], near[keep]) for keep in order}

    both = lax.optimization_barrier((own_a[True], own_a[False]))
    own_a = {True: both[0], False: both[1]}
    near_a = joined(own_a, neighbours(own_a))
    rest_a = others(near_a)
    near_of_b = neighbours(own_b)
    sent_a = panel_dot(False, near_a, rest_a, rest_a[True])
    kept_a, send_a = panel_dot(True, near_a, rest_a, more=exchange(sent_a, other_core))
    near_b = joined(own_b, {keep: after(near_of_b[keep], send_a) for keep in order})
    rest_b = others(near_b)
    step_a = after(exchange(send_a, along_z(0)), rest_b[True], rest_b[False])
    sent_b = panel_dot(False, near_b, rest_b, step_a)
    half_a = half_sum(kept_a, step_a)
    turn_a = exchange(half_a, along_z(1))
    pair_a = hidden_of(half_a, turn_a)
    kept_b, send_b = panel_dot(
        True, near_b, rest_b, pair_a, more=exchange(sent_b, other_core)
    )
    step_b = exchange(send_b, along_z(0))
    far_a = exchange(pair_a, along_z(0))
    hid_a = {True: (pair_a, far_a)}
    hid_a[False] = (exchange(pair_a, other_core), exchange(far_a, other_core))

    in_pairs, out_pairs = [], []
    for base, keep in ((0, True), (2, False)):
        for i in range(2):
            in_pairs.append(
                tuple(
                    (base + hidden_at(keep, 2 * i + p, slot)[0], hidden_at(keep, 2 * i + p, slot)[1])
                    for p in range(2)
                    for slot in range(RING)
                )
            )
            out_pairs.append(
                tuple(
                    (base + panel_at(piece, 2 * i + s)[0], panel_at(piece, 2 * i + s)[1])
                    for s in range(2)
                    for piece in order_of(keep)
                )
            )

    def grads(which, near, rest, hid, begun, *events):
        panels = [near[True], rest[True], near[False], rest[False]]
        hiddens = [*hid[True], *hid[False]]
        lefts, rights, pairs = (
            (panels, hiddens, in_pairs) if which == 0 else (hiddens, panels, out_pairs)
        )
        lefts[0] = after(lefts[0], *events)
        return grad_dot(lefts, 0, rights, 1, pairs, factor, begun)

    def second_half(keep, kept, got):
        sums = halfway(kept, got)
        return sums[0], exchange(sums[1].astype(BF), along(keep, True, 0))

    out_a, out_b, got_a, got_b = {}, {}, {}, {}
    sums_a, sums_b, last_a, last_b, total_a, total_b = {}, {}, {}, {}, {}, {}
    out_a[True] = out_dot(True, hid_a[True])
    out_a[False] = out_dot(False, hid_a[False], out_a[True][0])
    half_b = half_sum(kept_b, after(step_b, out_a[True][0], out_a[False][0]))
    turn_b = exchange(half_b, along_z(1))
    for keep in both_ways:
        got_a[keep] = exchange(out_a[keep][1], along(keep, True, 1))
    grad_in = grads(0, near_a, rest_a, hid_a, None, out_a[False][0])
    pair_b = hidden_of(half_b, after(turn_b, grad_in))
    far_b = exchange(pair_b, along_z(0))
    grad_out = grads(1, near_a, rest_a, hid_a, None, turn_b, got_a[True], got_a[False], grad_in)
    for keep in both_ways:
        got = after(got_a[keep], grad_in, got_a[not keep])
        sums_a[keep], last_a[keep] = second_half(keep, out_a[keep][0], got)
    far_b = after(far_b, grad_out, last_a[True], last_a[False])
    hid_b = {True: (pair_b, far_b)}
    hid_b[False] = (exchange(pair_b, other_core), exchange(far_b, other_core))

    leaves, stays = {}, {}
    leaves[True] = out_dot(True, hid_b[True], hid_b[False][0], side=1)
    leaves[False] = out_dot(False, hid_b[False], leaves[True], side=1)
    stays[True] = out_dot(True, hid_b[True], leaves[False], side=0)
    stays[False] = out_dot(False, hid_b[False], stays[True], side=0)
    out_b = {keep: (stays[keep], leaves[keep]) for keep in both_ways}
    for keep in both_ways:
        got_b[keep] = exchange(out_b[keep][1], along(keep, True, 1))
    grad_in = grads(
        0, near_b, rest_b, hid_b, grad_in, out_b[False][0]
    )
    for keep in both_ways:
        got = after(got_b[keep], grad_in, got_b[not keep])
        sums_b[keep], last_b[keep] = second_half(keep, out_b[keep][0], got)
    grad_out = grads(1, near_b, rest_b, hid_b, grad_out, got_b[True], got_b[False], grad_in)
    for keep in both_ways:
        total_a[keep] = sums_a[keep] + last_a[keep].astype(F32)
        total_b[keep] = sums_b[keep] + after(last_b[keep], grad_out, last_b[not keep]).astype(F32)

    part = block // PARTS
    pick = lambda keep, piece: jnp.concatenate(
        [
            total[keep][order_of(keep).index(piece) * part:(order_of(keep).index(piece) + 1) * part]
            for total in (total_a, total_b)
        ],
        axis=0,
    )
    gots, done = {}, {}
    for keep in both_ways:
        passed = jnp.concatenate([pick(keep, 2), pick(keep, 3)], axis=0).astype(BF)
        gots[keep] = exchange(passed, along(keep, False, 1))
    for keep in both_ways:
        got = after(gots[keep], gots[not keep]).astype(F32)
        last = (pick(keep, 1) + got[block:]).astype(BF)
        done[keep] = (
            pick(keep, 0) + got[:block] + exchange(last, along(keep, False, 0)).astype(F32)
        ).astype(BF)

    low = jnp.where(core == 0, done[True], done[False])
    high = jnp.where(core == 0, done[False], done[True])
    result = jnp.concatenate([low, high], axis=0)
    return (result[:, :width], result[:, width:], grad_in, grad_out)


def solution(mesh):
    placed = (P(("col", "dp"), "row"), P(("col", "dp"), "row"), P("row", "col"), P("col", "row"))
    return jax.shard_map(
        shards,
        mesh=mesh,
        in_specs=placed,
        out_specs=(
            P(("col", "dp"), "row"),
            P(("col", "dp"), "row"),
            P("row", ("col", "dp")),
            P(("col", "dp"), "row"),
        ),
        check_vma=False,
    )
```

```python
import functools
import math

import jax
import jax.numpy as jnp
from jax import lax
from jax.experimental import pallas as pl
from jax.experimental.pallas import tpu as pltpu
from jax.sharding import PartitionSpec as P

AXES = ("row", "col", "dp")
RING = 4
PARTS = 2
BF = jnp.bfloat16
F32 = jnp.float32
NN = (((1,), (0,)), ((), ()))
NT = (((1,), (1,)), ((), ()))
TN = (((0,), (0,)), ((), ()))


def cost(flops, bytes_accessed, transcendentals):
    return pl.CostEstimate(
        flops=flops // 1000, bytes_accessed=bytes_accessed // 1000, transcendentals=transcendentals
    )


def gelu_parts(pre):
    cdf = 0.5 * (1.0 + jax.scipy.special.erf(pre * (1.0 / math.sqrt(2.0))))
    activated = pre * cdf
    slope = cdf + pre * jnp.exp(-0.5 * pre * pre) * (1.0 / math.sqrt(2.0 * math.pi))
    return (activated, slope)


def flat(z, c, x, y):
    return ((z * 2 + c) * RING + x) * RING + y


def exchange(array, partner):
    pairs = []
    for z in range(RING):
        for c in range(2):
            for x in range(RING):
                for y in range(RING):
                    pairs.append((flat(*partner(z, c, x, y)), flat(z, c, x, y)))
    return lax.ppermute(array, AXES, pairs)


NEAR = ((1, 3), (3, 1))
Z_PAIR = ((1, 3), (3, 1))
OWNER_SLOT = ((0, 2, 3, 1), (0, 1, 3, 2))


def along(keep, first, turn):
    def partner(z, c, x, y):
        half = c if keep else 1 - c
        step = NEAR[c][turn]
        if (half == 0) == first:
            return (z, c, x ^ step, y)
        return (z, c, x, y ^ step)

    return partner


def along_z(turn):
    return lambda z, c, x, y: (z ^ Z_PAIR[c][turn], c, x, y)


def other_core(z, c, x, y):
    return (z, 1 - c, x, y)


def slot_of(keep, place_ref, i):
    z, core = place_ref[0], place_ref[1]

    def one(c):
        near = NEAR[c]
        owned = z ^ (0, near[0], near[1], near[0] ^ near[1])[i]
        table = OWNER_SLOT[c if keep else 1 - c]
        slot = jnp.int32(table[0])
        for j in range(1, RING):
            slot = jnp.where(owned == j, table[j], slot)
        return slot

    return jnp.where(core == 0, one(0), one(1))


def arrival_of(keep, place_ref, i):
    z, core = place_ref[0], place_ref[1]

    def one(c):
        near = NEAR[c]
        arrival = (0, near[0], near[1], near[0] ^ near[1])
        owned = z ^ OWNER_SLOT[c if keep else 1 - c].index(i)
        place = jnp.int32(arrival.index(0))
        for j in range(1, RING):
            place = jnp.where(owned == j, arrival.index(j), place)
        return place

    return jnp.where(core == 0, one(0), one(1))


def cut_kernel(place_ref, tokens_ref, grad_ref, kept_ref, passed_ref, sems):
    block, wide = kept_ref.shape[0], tokens_ref.shape[1]
    core = place_ref[1]
    copies = []
    for ref, which in ((kept_ref, core), (passed_ref, 1 - core)):
        rows = pl.ds(pl.multiple_of(which * block, block), block)
        for i, source in enumerate((tokens_ref, grad_ref)):
            copies.append(
                pltpu.make_async_copy(
                    source.at[rows, :],
                    ref.at[:, i * wide:(i + 1) * wide],
                    sems.at[len(copies)],
                )
            )
    for copy in copies:
        copy.start()
    for copy in copies:
        copy.wait()


def whole(kernel, place, arrays, shapes):
    return pl.pallas_call(
        kernel,
        in_specs=[pl.BlockSpec(memory_space=pltpu.SMEM)]
        + [pl.BlockSpec(memory_space=pltpu.VMEM)] * len(arrays),
        out_specs=[pl.BlockSpec(memory_space=pltpu.VMEM)] * len(shapes),
        out_shape=[jax.ShapeDtypeStruct(shape, BF) for shape in shapes],
        compiler_params=pltpu.CompilerParams(vmem_limit_bytes=8 * 2**20),
        cost_estimate=cost(flops=0, bytes_accessed=0, transcendentals=0),
    )(place, *arrays)


def cut(place, tokens, out_grad):
    rows, wide = tokens.shape
    half = jax.ShapeDtypeStruct((rows // 2, 2 * wide), BF)
    return pl.pallas_call(
        cut_kernel,
        in_specs=[pl.BlockSpec(memory_space=pltpu.SMEM)]
        + [pl.BlockSpec(memory_space=pltpu.HBM)] * 2,
        out_specs=[pl.BlockSpec(memory_space=pltpu.VMEM)] * 2,
        out_shape=[half, half],
        scratch_shapes=[pltpu.SemaphoreType.DMA((4,))],
        compiler_params=pltpu.CompilerParams(vmem_limit_bytes=8 * 2**20),
        cost_estimate=cost(flops=0, bytes_accessed=0, transcendentals=0),
    )(place, tokens, out_grad)


def join_kernel(place_ref, a_ref, b_ref, out_ref):
    rows = a_ref.shape[0]
    out_ref[:rows, :] = a_ref[...]
    out_ref[rows:, :] = b_ref[...]


def join(place, a, b):
    return whole(join_kernel, place, [a, b], [(2 * a.shape[0], a.shape[1])])[0]


def assemble_kernel(keep, place_ref, a_ref, b_ref, c_ref, *out_refs):
    rows = a_ref.shape[0]
    part = rows // PARTS

    def put(i, ref, first):
        at = pl.multiple_of(slot_of(keep, place_ref, i) * part, part)
        for j, out_ref in enumerate(out_refs):
            out_ref[pl.ds(at, part), :] = ref[first + j * part:first + (j + 1) * part, :]

    put(0, a_ref, 0)
    put(1, b_ref, 0)
    put(2, c_ref, 0)
    put(3, c_ref, rows)


def assemble(keep, place, a, b, c):
    rows, wide = a.shape
    kernel = functools.partial(assemble_kernel, keep)
    return whole(kernel, place, [a, b, c], [(RING * rows // PARTS, wide)] * PARTS)


def order_of(keep):
    return (0, 1, 2, 3) if keep else (0, 2, 1, 3)


def panel_at(piece, slot):
    return piece // 2, (piece % 2) * RING + slot


def hidden_at(keep, piece, slot):
    return slot // 2, (slot % 2) * RING + order_of(keep).index(piece)


def pair_kernel(keep, hidden, added, split, side, block, place_ref, *refs):
    a_refs, (left_ref, right_ref), rest = refs[:2], refs[2:4], refs[4:]
    if added:
        more_ref, rest = rest[0], rest[1:]
    rows_ref = rest[-1]
    out_refs = rest[:-1]

    @pl.when(pl.program_id(1) == 0)
    def _():
        if hidden:
            size = RING * block
            for i in range(RING):
                at = pl.multiple_of(arrival_of(keep, place_ref, i) * size, size)
                first = (i % 2) * size
                rows_ref[pl.ds(at, size), :] = a_refs[i // 2][first:first + size, :]
        else:
            for i in range(RING):
                for j, piece in enumerate(order_of(keep)):
                    which, first = panel_at(piece, i)
                    at = (i * RING + j) * block
                    rows_ref[at:at + block, :] = a_refs[which][first * block:(first + 1) * block, :]

    def rows():
        if side is None:
            return rows_ref[...]
        half = rows_ref.shape[0] // 2
        return rows_ref[side * half:(side + 1) * half, :]

    def finish(total):
        if added:
            total = total + more_ref[...].astype(F32)
        total = total.astype(BF)
        if not split:
            out_refs[0][...] = total
        else:
            half = total.shape[0] // 2
            out_refs[0][...] = total[:half]
            out_refs[1][...] = total[half:]

    @pl.when(pl.program_id(0) == 0)
    def _():
        finish(lax.dot_general(rows(), left_ref[...], NN, preferred_element_type=F32))

    @pl.when(pl.program_id(0) == 1)
    def _():
        finish(lax.dot_general(rows(), right_ref[...], NT, preferred_element_type=F32))


def pair_dot(keep, hidden, pair, left, right, place, more=None, split=True, side=None, tile=512):
    rows = sum(a.shape[0] for a in pair)
    block = rows // RING // RING
    depth, wide = left.shape
    tiles = wide // tile
    in_specs = [pl.BlockSpec((a.shape[0], depth), lambda h, n, place: (0, h)) for a in pair]
    in_specs += [
        pl.BlockSpec((depth, tile), lambda h, n, place: (0, n * (1 - h) + (tiles - 1) * h)),
        pl.BlockSpec((tile, depth), lambda h, n, place: (n * h, 0)),
    ]
    out_of = lambda n_rows: pl.BlockSpec((n_rows, tile), lambda h, n, place: (0, h * tiles + n))
    args = [*pair, left, right]
    if more is not None:
        in_specs.append(out_of(rows))
        args.append(more)
    outs = [rows // 2, rows // 2] if split else [rows if side is None else rows // 2]
    result = pl.pallas_call(
        functools.partial(pair_kernel, keep, hidden, more is not None, split, side, block),
        grid_spec=pltpu.PrefetchScalarGridSpec(
            num_scalar_prefetch=1,
            grid=(2, tiles),
            in_specs=in_specs,
            out_specs=[out_of(n) for n in outs],
            scratch_shapes=[pltpu.VMEM((rows, depth), BF)],
        ),
        out_shape=[jax.ShapeDtypeStruct((n, 2 * wide), BF) for n in outs],
        compiler_params=pltpu.CompilerParams(vmem_limit_bytes=18 * 2**20),
        cost_estimate=cost(
            flops=4 * rows * depth * wide,
            bytes_accessed=4 * depth * wide + 8 * rows * wide,
            transcendentals=0,
        ),
    )(place, *args)
    return result if split else result[0]


def grad_kernel(pairs, block, factor, begun, *refs):
    lefts, rights, out_ref = refs[:4], refs[4:8], refs[-1]
    total = None
    for i, blocks in enumerate(pairs):
        right = jnp.concatenate(
            [rights[j][first * block:(first + 1) * block, :] for j, first in blocks], axis=0
        )
        term = lax.dot_general(lefts[i][...], right, TN, preferred_element_type=F32)
        total = term if total is None else total + term
    total = total * factor
    out_ref[...] = total + refs[8][...] if begun else total


def grad_dot(lefts, left_part, rights, right_part, pairs, factor, begun=None, tile=256):
    wide = lefts[0].shape[1] // 2
    tiles = wide // tile
    tokens = sum(a.shape[0] for a in lefts)
    args = [*lefts, *rights]
    in_specs = [pl.BlockSpec((a.shape[0], wide), lambda n: (0, left_part)) for a in lefts]
    in_specs += [
        pl.BlockSpec((a.shape[0], tile), lambda n: (0, right_part * tiles + n)) for a in rights
    ]
    out_spec = pl.BlockSpec((wide, tile), lambda n: (0, n))
    aliases = {}
    if begun is not None:
        aliases = {len(args): 0}
        args.append(begun)
        in_specs.append(out_spec)
    block = rights[0].shape[0] // (2 * RING)
    return pl.pallas_call(
        functools.partial(grad_kernel, pairs, block, factor, begun is not None),
        grid=(tiles,),
        in_specs=in_specs,
        out_specs=out_spec,
        out_shape=jax.ShapeDtypeStruct((wide, wide), F32),
        input_output_aliases=aliases,
        compiler_params=pltpu.CompilerParams(vmem_limit_bytes=24 * 2**20),
        cost_estimate=cost(
            flops=2 * tokens * wide * wide,
            bytes_accessed=3 * tokens * wide + 2 * wide * wide,
            transcendentals=0,
        ),
    )(*args)


def after(value, *events):
    return lax.optimization_barrier((value, *events))[0]


def shards(tokens, out_grad, weight_in, weight_out):
    core = lax.axis_index("row") % 2
    z = lax.axis_index("row") // 2
    dp = lax.axis_index("dp")
    rows, width = tokens.shape
    block = rows // 2
    inner = weight_in.shape[1] // 2
    factor = 1.0 / math.sqrt(rows * 16)
    both_ways = (True, False)

    place = jnp.stack([z, core]).astype(jnp.int32)
    w_in = lax.dynamic_slice_in_dim(weight_in, dp * inner, inner, 1)
    w_out = lax.dynamic_slice_in_dim(weight_out, dp * inner, inner, 0)

    order = (False, True)
    start, one, two, own_a, own_b = {}, {}, {}, {}, {}
    start[True], start[False] = cut(place, tokens, out_grad)
    for keep in order:
        one[keep] = exchange(start[keep], along(keep, True, 0))
    for keep in order:
        two[keep] = exchange(join(place, start[keep], one[keep]), along(keep, True, 1))
    for keep in order:
        own_a[keep], own_b[keep] = assemble(keep, place, start[keep], one[keep], two[keep])

    def others(near):
        return {keep: exchange(near[keep], along(keep, False, 1)) for keep in order}

    def panel_dot(keep, near, rest, *events, more=None):
        pair = [near[keep], after(rest[keep], *events) if events else rest[keep]]
        return pair_dot(keep, False, pair, w_in, w_out, place, more=more, split=keep)

    def out_dot(keep, pair, *events, side=None):
        pair = list(pair)
        pair[1] = after(pair[1], *events) if events else pair[1]
        return pair_dot(
            keep, True, pair, w_out, w_in, place, split=side is None, side=side
        )

    def halfway(kept, got):
        half = kept.shape[0] // 2
        sums = kept.astype(F32) + got.astype(F32)
        return [sums[:half], sums[half:]]

    def half_sum(kept, got):
        return (kept.astype(F32) + got.astype(F32)).astype(BF)

    def hidden_of(half, got):
        rows = half.shape[0] // 2
        other = jnp.concatenate([got[rows:], got[:rows]], axis=0)
        value = half.astype(F32) + other.astype(F32)
        pre, back = value[:, :width], value[:, width:]
        activated, slope = gelu_parts(pre)
        return jnp.concatenate([activated.astype(BF), (back * slope).astype(BF)], axis=1)

    def neighbours(own):
        return {keep: exchange(own[keep], along(keep, False, 0)) for keep in order}

    def joined(own, near):
        return {keep: join(place, own[keep], near[keep]) for keep in order}

    both = lax.optimization_barrier((own_a[True], own_a[False]))
    own_a = {True: both[0], False: both[1]}
    near_a = joined(own_a, neighbours(own_a))
    rest_a = others(near_a)
    near_of_b = neighbours(own_b)
    sent_a = panel_dot(False, near_a, rest_a, rest_a[True])
    kept_a, send_a = panel_dot(True, near_a, rest_a, more=exchange(sent_a, other_core))
    near_b = joined(own_b, {keep: after(near_of_b[keep], send_a) for keep in order})
    rest_b = others(near_b)
    sent_b = panel_dot(False, near_b, rest_b, rest_b[True], send_a)
    step_a = after(exchange(send_a, along_z(0)), sent_b)
    half_a = half_sum(kept_a, step_a)
    turn_a = exchange(half_a, along_z(1))
    kept_b, send_b = panel_dot(
        True, near_b, rest_b, more=exchange(sent_b, other_core)
    )
    pair_a = hidden_of(half_a, after(turn_a, send_b))
    step_b = exchange(after(send_b, turn_a), along_z(0))
    far_a = exchange(pair_a, along_z(0))
    hid_a = {True: (pair_a, far_a)}
    hid_a[False] = (exchange(pair_a, other_core), exchange(far_a, other_core))

    in_pairs, out_pairs = [], []
    for base, keep in ((0, True), (2, False)):
        for i in range(2):
            in_pairs.append(
                tuple(
                    (base + hidden_at(keep, 2 * i + p, slot)[0], hidden_at(keep, 2 * i + p, slot)[1])
                    for p in range(2)
                    for slot in range(RING)
                )
            )
            out_pairs.append(
                tuple(
                    (base + panel_at(piece, 2 * i + s)[0], panel_at(piece, 2 * i + s)[1])
                    for s in range(2)
                    for piece in order_of(keep)
                )
            )

    def grads(which, near, rest, hid, begun, *events):
        panels = [near[True], rest[True], near[False], rest[False]]
        hiddens = [*hid[True], *hid[False]]
        lefts, rights, pairs = (
            (panels, hiddens, in_pairs) if which == 0 else (hiddens, panels, out_pairs)
        )
        lefts[0] = after(lefts[0], *events)
        return grad_dot(lefts, 0, rights, 1, pairs, factor, begun)

    def second_half(keep, kept, got):
        sums = halfway(kept, got)
        return sums[0], exchange(sums[1].astype(BF), along(keep, True, 0))

    out_a, out_b, got_a, got_b = {}, {}, {}, {}
    sums_a, sums_b, last_a, last_b, total_a, total_b = {}, {}, {}, {}, {}, {}
    out_a[True] = out_dot(True, hid_a[True])
    half_b = half_sum(kept_b, after(step_b, out_a[True][0]))
    turn_b = exchange(half_b, along_z(1))
    out_a[False] = out_dot(False, hid_a[False], out_a[True][0], step_b)
    for keep in both_ways:
        got_a[keep] = exchange(out_a[keep][1], along(keep, True, 1))
    grad_in = grads(0, near_a, rest_a, hid_a, None, out_a[False][0])
    pair_b = hidden_of(half_b, after(turn_b, grad_in))
    far_b = exchange(pair_b, along_z(0))
    grad_out = grads(1, near_a, rest_a, hid_a, None, turn_b, got_a[True], got_a[False], grad_in)
    for keep in both_ways:
        got = after(got_a[keep], grad_in, got_a[not keep])
        sums_a[keep], last_a[keep] = second_half(keep, out_a[keep][0], got)
    far_b = after(far_b, grad_out, last_a[True], last_a[False])
    hid_b = {True: (pair_b, far_b)}
    hid_b[False] = (exchange(pair_b, other_core), exchange(far_b, other_core))

    leaves, stays = {}, {}
    leaves[True] = out_dot(True, hid_b[True], hid_b[False][0], side=1)
    leaves[False] = out_dot(False, hid_b[False], leaves[True], side=1)
    stays[True] = out_dot(True, hid_b[True], leaves[False], side=0)
    stays[False] = out_dot(False, hid_b[False], stays[True], side=0)
    out_b = {keep: (stays[keep], leaves[keep]) for keep in both_ways}
    for keep in both_ways:
        got_b[keep] = exchange(out_b[keep][1], along(keep, True, 1))
    grad_in = grads(
        0, near_b, rest_b, hid_b, grad_in, out_b[False][0]
    )
    for keep in both_ways:
        got = after(got_b[keep], grad_in, got_b[not keep])
        sums_b[keep], last_b[keep] = second_half(keep, out_b[keep][0], got)
    grad_out = grads(1, near_b, rest_b, hid_b, grad_out, got_b[True], got_b[False], grad_in)
    for keep in both_ways:
        total_a[keep] = sums_a[keep] + last_a[keep].astype(F32)
        total_b[keep] = sums_b[keep] + after(last_b[keep], grad_out, last_b[not keep]).astype(F32)

    part = block // PARTS
    pick = lambda keep, piece: jnp.concatenate(
        [
            total[keep][order_of(keep).index(piece) * part:(order_of(keep).index(piece) + 1) * part]
            for total in (total_a, total_b)
        ],
        axis=0,
    )
    gots, done = {}, {}
    for keep in both_ways:
        passed = jnp.concatenate([pick(keep, 2), pick(keep, 3)], axis=0).astype(BF)
        gots[keep] = exchange(passed, along(keep, False, 1))
    for keep in both_ways:
        got = after(gots[keep], gots[not keep]).astype(F32)
        last = (pick(keep, 1) + got[block:]).astype(BF)
        done[keep] = (
            pick(keep, 0) + got[:block] + exchange(last, along(keep, False, 0)).astype(F32)
        ).astype(BF)

    low = jnp.where(core == 0, done[True], done[False])
    high = jnp.where(core == 0, done[False], done[True])
    result = jnp.concatenate([low, high], axis=0)
    return (result[:, :width], result[:, width:], grad_in, grad_out)


def solution(mesh):
    placed = (P(("col", "dp"), "row"), P(("col", "dp"), "row"), P("row", "col"), P("col", "row"))
    return jax.shard_map(
        shards,
        mesh=mesh,
        in_specs=placed,
        out_specs=(
            P(("col", "dp"), "row"),
            P(("col", "dp"), "row"),
            P("row", ("col", "dp")),
            P(("col", "dp"), "row"),
        ),
        check_vma=False,
    )
```

```python
import functools
import math

import jax
import jax.numpy as jnp
from jax import lax
from jax.experimental import pallas as pl
from jax.experimental.pallas import tpu as pltpu
from jax.sharding import PartitionSpec as P

AXES = ("row", "col", "dp")
RING = 4
PARTS = 2
BF = jnp.bfloat16
F32 = jnp.float32
NN = (((1,), (0,)), ((), ()))
NT = (((1,), (1,)), ((), ()))
TN = (((0,), (0,)), ((), ()))


def cost(flops, bytes_accessed, transcendentals):
    return pl.CostEstimate(
        flops=flops // 1000, bytes_accessed=bytes_accessed // 1000, transcendentals=transcendentals
    )


def gelu_parts(pre):
    cdf = 0.5 * (1.0 + jax.scipy.special.erf(pre * (1.0 / math.sqrt(2.0))))
    activated = pre * cdf
    slope = cdf + pre * jnp.exp(-0.5 * pre * pre) * (1.0 / math.sqrt(2.0 * math.pi))
    return (activated, slope)


def flat(z, c, x, y):
    return ((z * 2 + c) * RING + x) * RING + y


def exchange(array, partner):
    pairs = []
    for z in range(RING):
        for c in range(2):
            for x in range(RING):
                for y in range(RING):
                    pairs.append((flat(*partner(z, c, x, y)), flat(z, c, x, y)))
    return lax.ppermute(array, AXES, pairs)


NEAR = ((1, 3), (3, 1))
Z_PAIR = ((1, 3), (3, 1))
OWNER_SLOT = ((0, 2, 3, 1), (0, 1, 3, 2))


def along(keep, first, turn):
    def partner(z, c, x, y):
        half = c if keep else 1 - c
        step = NEAR[c][turn]
        if (half == 0) == first:
            return (z, c, x ^ step, y)
        return (z, c, x, y ^ step)

    return partner


def along_z(turn):
    return lambda z, c, x, y: (z ^ Z_PAIR[c][turn], c, x, y)


def other_core(z, c, x, y):
    return (z, 1 - c, x, y)


def slot_of(keep, place_ref, i):
    z, core = place_ref[0], place_ref[1]

    def one(c):
        near = NEAR[c]
        owned = z ^ (0, near[0], near[1], near[0] ^ near[1])[i]
        table = OWNER_SLOT[c if keep else 1 - c]
        slot = jnp.int32(table[0])
        for j in range(1, RING):
            slot = jnp.where(owned == j, table[j], slot)
        return slot

    return jnp.where(core == 0, one(0), one(1))


def arrival_of(keep, place_ref, i):
    z, core = place_ref[0], place_ref[1]

    def one(c):
        near = NEAR[c]
        arrival = (0, near[0], near[1], near[0] ^ near[1])
        owned = z ^ OWNER_SLOT[c if keep else 1 - c].index(i)
        place = jnp.int32(arrival.index(0))
        for j in range(1, RING):
            place = jnp.where(owned == j, arrival.index(j), place)
        return place

    return jnp.where(core == 0, one(0), one(1))


def cut_kernel(place_ref, tokens_ref, grad_ref, kept_ref, passed_ref, sems):
    block, wide = kept_ref.shape[0], tokens_ref.shape[1]
    core = place_ref[1]
    copies = []
    for ref, which in ((kept_ref, core), (passed_ref, 1 - core)):
        rows = pl.ds(pl.multiple_of(which * block, block), block)
        for i, source in enumerate((tokens_ref, grad_ref)):
            copies.append(
                pltpu.make_async_copy(
                    source.at[rows, :],
                    ref.at[:, i * wide:(i + 1) * wide],
                    sems.at[len(copies)],
                )
            )
    for copy in copies:
        copy.start()
    for copy in copies:
        copy.wait()


def whole(kernel, place, arrays, shapes):
    return pl.pallas_call(
        kernel,
        in_specs=[pl.BlockSpec(memory_space=pltpu.SMEM)]
        + [pl.BlockSpec(memory_space=pltpu.VMEM)] * len(arrays),
        out_specs=[pl.BlockSpec(memory_space=pltpu.VMEM)] * len(shapes),
        out_shape=[jax.ShapeDtypeStruct(shape, BF) for shape in shapes],
        compiler_params=pltpu.CompilerParams(vmem_limit_bytes=8 * 2**20),
        cost_estimate=cost(flops=0, bytes_accessed=0, transcendentals=0),
    )(place, *arrays)


def cut(place, tokens, out_grad):
    rows, wide = tokens.shape
    half = jax.ShapeDtypeStruct((rows // 2, 2 * wide), BF)
    return pl.pallas_call(
        cut_kernel,
        in_specs=[pl.BlockSpec(memory_space=pltpu.SMEM)]
        + [pl.BlockSpec(memory_space=pltpu.HBM)] * 2,
        out_specs=[pl.BlockSpec(memory_space=pltpu.VMEM)] * 2,
        out_shape=[half, half],
        scratch_shapes=[pltpu.SemaphoreType.DMA((4,))],
        compiler_params=pltpu.CompilerParams(vmem_limit_bytes=8 * 2**20),
        cost_estimate=cost(flops=0, bytes_accessed=0, transcendentals=0),
    )(place, tokens, out_grad)


def join_kernel(place_ref, a_ref, b_ref, out_ref):
    rows = a_ref.shape[0]
    out_ref[:rows, :] = a_ref[...]
    out_ref[rows:, :] = b_ref[...]


def join(place, a, b):
    return whole(join_kernel, place, [a, b], [(2 * a.shape[0], a.shape[1])])[0]


def assemble_kernel(keep, place_ref, a_ref, b_ref, c_ref, *out_refs):
    rows = a_ref.shape[0]
    part = rows // PARTS

    def put(i, ref, first):
        at = pl.multiple_of(slot_of(keep, place_ref, i) * part, part)
        for j, out_ref in enumerate(out_refs):
            out_ref[pl.ds(at, part), :] = ref[first + j * part:first + (j + 1) * part, :]

    put(0, a_ref, 0)
    put(1, b_ref, 0)
    put(2, c_ref, 0)
    put(3, c_ref, rows)


def assemble(keep, place, a, b, c):
    rows, wide = a.shape
    kernel = functools.partial(assemble_kernel, keep)
    return whole(kernel, place, [a, b, c], [(RING * rows // PARTS, wide)] * PARTS)


def order_of(keep):
    return (0, 1, 2, 3) if keep else (0, 2, 1, 3)


def panel_at(piece, slot):
    return piece // 2, (piece % 2) * RING + slot


def hidden_at(keep, piece, slot):
    return slot // 2, (slot % 2) * RING + order_of(keep).index(piece)


def pair_kernel(keep, hidden, added, split, side, block, place_ref, *refs):
    a_refs, (left_ref, right_ref), rest = refs[:2], refs[2:4], refs[4:]
    if added:
        more_ref, rest = rest[0], rest[1:]
    rows_ref = rest[-1]
    out_refs = rest[:-1]

    @pl.when(pl.program_id(1) == 0)
    def _():
        if hidden:
            size = RING * block
            for i in range(RING):
                at = pl.multiple_of(arrival_of(keep, place_ref, i) * size, size)
                first = (i % 2) * size
                rows_ref[pl.ds(at, size), :] = a_refs[i // 2][first:first + size, :]
        else:
            for i in range(RING):
                for j, piece in enumerate(order_of(keep)):
                    which, first = panel_at(piece, i)
                    at = (i * RING + j) * block
                    rows_ref[at:at + block, :] = a_refs[which][first * block:(first + 1) * block, :]

    def rows():
        if side is None:
            return rows_ref[...]
        half = rows_ref.shape[0] // 2
        return rows_ref[side * half:(side + 1) * half, :]

    def finish(total):
        if added:
            total = total + more_ref[...].astype(F32)
        total = total.astype(BF)
        if not split:
            out_refs[0][...] = total
        else:
            half = total.shape[0] // 2
            out_refs[0][...] = total[:half]
            out_refs[1][...] = total[half:]

    @pl.when(pl.program_id(0) == 0)
    def _():
        finish(lax.dot_general(rows(), left_ref[...], NN, preferred_element_type=F32))

    @pl.when(pl.program_id(0) == 1)
    def _():
        finish(lax.dot_general(rows(), right_ref[...], NT, preferred_element_type=F32))


def pair_dot(keep, hidden, pair, left, right, place, more=None, split=True, side=None, tile=512):
    rows = sum(a.shape[0] for a in pair)
    block = rows // RING // RING
    depth, wide = left.shape
    tiles = wide // tile
    in_specs = [pl.BlockSpec((a.shape[0], depth), lambda h, n, place: (0, h)) for a in pair]
    in_specs += [
        pl.BlockSpec((depth, tile), lambda h, n, place: (0, n * (1 - h) + (tiles - 1) * h)),
        pl.BlockSpec((tile, depth), lambda h, n, place: (n * h, 0)),
    ]
    out_of = lambda n_rows: pl.BlockSpec((n_rows, tile), lambda h, n, place: (0, h * tiles + n))
    args = [*pair, left, right]
    if more is not None:
        in_specs.append(out_of(rows))
        args.append(more)
    outs = [rows // 2, rows // 2] if split else [rows if side is None else rows // 2]
    result = pl.pallas_call(
        functools.partial(pair_kernel, keep, hidden, more is not None, split, side, block),
        grid_spec=pltpu.PrefetchScalarGridSpec(
            num_scalar_prefetch=1,
            grid=(2, tiles),
            in_specs=in_specs,
            out_specs=[out_of(n) for n in outs],
            scratch_shapes=[pltpu.VMEM((rows, depth), BF)],
        ),
        out_shape=[jax.ShapeDtypeStruct((n, 2 * wide), BF) for n in outs],
        compiler_params=pltpu.CompilerParams(vmem_limit_bytes=18 * 2**20),
        cost_estimate=cost(
            flops=4 * rows * depth * wide,
            bytes_accessed=4 * depth * wide + 8 * rows * wide,
            transcendentals=0,
        ),
    )(place, *args)
    return result if split else result[0]


def grad_kernel(pairs, block, factor, begun, *refs):
    lefts, rights, out_ref = refs[:4], refs[4:8], refs[-1]
    total = None
    for i, blocks in enumerate(pairs):
        right = jnp.concatenate(
            [rights[j][first * block:(first + 1) * block, :] for j, first in blocks], axis=0
        )
        term = lax.dot_general(lefts[i][...], right, TN, preferred_element_type=F32)
        total = term if total is None else total + term
    total = total * factor
    out_ref[...] = total + refs[8][...] if begun else total


def grad_dot(lefts, left_part, rights, right_part, pairs, factor, begun=None, tile=256):
    wide = lefts[0].shape[1] // 2
    tiles = wide // tile
    tokens = sum(a.shape[0] for a in lefts)
    args = [*lefts, *rights]
    in_specs = [pl.BlockSpec((a.shape[0], wide), lambda n: (0, left_part)) for a in lefts]
    in_specs += [
        pl.BlockSpec((a.shape[0], tile), lambda n: (0, right_part * tiles + n)) for a in rights
    ]
    out_spec = pl.BlockSpec((wide, tile), lambda n: (0, n))
    aliases = {}
    if begun is not None:
        aliases = {len(args): 0}
        args.append(begun)
        in_specs.append(out_spec)
    block = rights[0].shape[0] // (2 * RING)
    return pl.pallas_call(
        functools.partial(grad_kernel, pairs, block, factor, begun is not None),
        grid=(tiles,),
        in_specs=in_specs,
        out_specs=out_spec,
        out_shape=jax.ShapeDtypeStruct((wide, wide), F32),
        input_output_aliases=aliases,
        compiler_params=pltpu.CompilerParams(vmem_limit_bytes=24 * 2**20),
        cost_estimate=cost(
            flops=2 * tokens * wide * wide,
            bytes_accessed=3 * tokens * wide + 2 * wide * wide,
            transcendentals=0,
        ),
    )(*args)


def after(value, *events):
    return lax.optimization_barrier((value, *events))[0]


def shards(tokens, out_grad, weight_in, weight_out):
    core = lax.axis_index("row") % 2
    z = lax.axis_index("row") // 2
    dp = lax.axis_index("dp")
    rows, width = tokens.shape
    block = rows // 2
    inner = weight_in.shape[1] // 2
    factor = 1.0 / math.sqrt(rows * 16)
    both_ways = (True, False)

    place = jnp.stack([z, core]).astype(jnp.int32)
    w_in = lax.dynamic_slice_in_dim(weight_in, dp * inner, inner, 1)
    w_out = lax.dynamic_slice_in_dim(weight_out, dp * inner, inner, 0)

    order = (False, True)
    start, one, two, own_a, own_b = {}, {}, {}, {}, {}
    start[True], start[False] = cut(place, tokens, out_grad)
    for keep in order:
        one[keep] = exchange(start[keep], along(keep, True, 0))
    for keep in order:
        two[keep] = exchange(join(place, start[keep], one[keep]), along(keep, True, 1))
    for keep in order:
        own_a[keep], own_b[keep] = assemble(keep, place, start[keep], one[keep], two[keep])

    def others(near):
        return {keep: exchange(near[keep], along(keep, False, 1)) for keep in order}

    def panel_dot(keep, near, rest, *events, more=None):
        pair = [near[keep], after(rest[keep], *events) if events else rest[keep]]
        return pair_dot(keep, False, pair, w_in, w_out, place, more=more, split=keep)

    def out_dot(keep, pair, *events, side=None):
        pair = list(pair)
        pair[1] = after(pair[1], *events) if events else pair[1]
        return pair_dot(
            keep, True, pair, w_out, w_in, place, split=side is None, side=side
        )

    def halfway(kept, got):
        half = kept.shape[0] // 2
        sums = kept.astype(F32) + got.astype(F32)
        return [sums[:half], sums[half:]]

    def half_sum(kept, got):
        return (kept.astype(F32) + got.astype(F32)).astype(BF)

    def hidden_of(half, got):
        rows = half.shape[0] // 2
        other = jnp.concatenate([got[rows:], got[:rows]], axis=0)
        value = half.astype(F32) + other.astype(F32)
        pre, back = value[:, :width], value[:, width:]
        activated, slope = gelu_parts(pre)
        return jnp.concatenate([activated.astype(BF), (back * slope).astype(BF)], axis=1)

    def neighbours(own):
        return {keep: exchange(own[keep], along(keep, False, 0)) for keep in order}

    def joined(own, near):
        return {keep: join(place, own[keep], near[keep]) for keep in order}

    both = lax.optimization_barrier((own_a[True], own_a[False]))
    own_a = {True: both[0], False: both[1]}
    near_a = joined(own_a, neighbours(own_a))
    rest_a = others(near_a)
    near_of_b = neighbours(own_b)
    sent_a = panel_dot(False, near_a, rest_a, rest_a[True])
    kept_a, send_a = panel_dot(True, near_a, rest_a, more=exchange(sent_a, other_core))
    near_b = joined(own_b, {keep: after(near_of_b[keep], send_a) for keep in order})
    rest_b = others(near_b)
    sent_b = panel_dot(False, near_b, rest_b, rest_b[True], send_a)
    step_a = after(exchange(send_a, along_z(0)), sent_b)
    half_a = half_sum(kept_a, step_a)
    turn_a = exchange(half_a, along_z(1))
    kept_b, send_b = panel_dot(
        True, near_b, rest_b, more=exchange(sent_b, other_core)
    )
    pair_a = hidden_of(half_a, after(turn_a, send_b))
    step_b = exchange(after(send_b, turn_a), along_z(0))
    far_a = exchange(pair_a, along_z(0))
    hid_a = {True: (pair_a, far_a)}
    hid_a[False] = (exchange(pair_a, other_core), exchange(far_a, other_core))

    in_pairs, out_pairs = [], []
    for base, keep in ((0, True), (2, False)):
        for i in range(2):
            in_pairs.append(
                tuple(
                    (base + hidden_at(keep, 2 * i + p, slot)[0], hidden_at(keep, 2 * i + p, slot)[1])
                    for p in range(2)
                    for slot in range(RING)
                )
            )
            out_pairs.append(
                tuple(
                    (base + panel_at(piece, 2 * i + s)[0], panel_at(piece, 2 * i + s)[1])
                    for s in range(2)
                    for piece in order_of(keep)
                )
            )

    def grads(which, near, rest, hid, begun, *events):
        panels = [near[True], rest[True], near[False], rest[False]]
        hiddens = [*hid[True], *hid[False]]
        lefts, rights, pairs = (
            (panels, hiddens, in_pairs) if which == 0 else (hiddens, panels, out_pairs)
        )
        lefts[0] = after(lefts[0], *events)
        return grad_dot(lefts, 0, rights, 1, pairs, factor, begun)

    def second_half(keep, kept, got):
        sums = halfway(kept, got)
        return sums[0], exchange(sums[1].astype(BF), along(keep, True, 0))

    out_a, out_b, got_a, got_b = {}, {}, {}, {}
    sums_a, sums_b, last_a, last_b, total_a, total_b = {}, {}, {}, {}, {}, {}
    out_a[True] = out_dot(True, hid_a[True])
    half_b = half_sum(kept_b, after(step_b, out_a[True][0]))
    turn_b = exchange(half_b, along_z(1))
    out_a[False] = out_dot(False, hid_a[False], out_a[True][0], step_b)
    for keep in both_ways:
        got_a[keep] = exchange(out_a[keep][1], along(keep, True, 1))
    grad_in = grads(0, near_a, rest_a, hid_a, None, out_a[False][0])
    pair_b = hidden_of(half_b, after(turn_b, grad_in))
    far_b = exchange(pair_b, along_z(0))
    grad_out = grads(1, near_a, rest_a, hid_a, None, turn_b, got_a[True], got_a[False], grad_in)
    for keep in both_ways:
        got = after(got_a[keep], grad_in, got_a[not keep])
        sums_a[keep], last_a[keep] = second_half(keep, out_a[keep][0], got)
    far_b = after(far_b, grad_out, last_a[True], last_a[False])
    hid_b = {True: (pair_b, far_b)}
    hid_b[False] = (exchange(pair_b, other_core), exchange(far_b, other_core))

    leaves, stays = {}, {}
    leaves[True] = out_dot(True, hid_b[True], hid_b[False][0], side=1)
    leaves[False] = out_dot(False, hid_b[False], leaves[True], side=1)
    stays[True] = out_dot(True, hid_b[True], leaves[False], side=0)
    stays[False] = out_dot(False, hid_b[False], stays[True], side=0)
    out_b = {keep: (stays[keep], leaves[keep]) for keep in both_ways}
    for keep in both_ways:
        got_b[keep] = exchange(out_b[keep][1], along(keep, True, 1))
    grad_in = grads(
        0, near_b, rest_b, hid_b, grad_in, out_b[False][0]
    )
    for keep in both_ways:
        got = after(got_b[keep], grad_in, got_b[not keep])
        sums_b[keep], last_b[keep] = second_half(keep, out_b[keep][0], got)
    grad_out = grads(1, near_b, rest_b, hid_b, grad_out, got_b[True], got_b[False], grad_in)
    for keep in both_ways:
        total_a[keep] = sums_a[keep] + last_a[keep].astype(F32)
        total_b[keep] = sums_b[keep] + after(last_b[keep], grad_out).astype(F32)

    part = block // PARTS
    pick = lambda keep, piece: jnp.concatenate(
        [
            total[keep][order_of(keep).index(piece) * part:(order_of(keep).index(piece) + 1) * part]
            for total in (total_a, total_b)
        ],
        axis=0,
    )
    gots, done = {}, {}
    for keep in both_ways:
        passed = jnp.concatenate([pick(keep, 2), pick(keep, 3)], axis=0).astype(BF)
        gots[keep] = exchange(passed, along(keep, False, 1))
    for keep in both_ways:
        got = gots[keep].astype(F32)
        last = (pick(keep, 1) + got[block:]).astype(BF)
        done[keep] = (
            pick(keep, 0) + got[:block] + exchange(last, along(keep, False, 0)).astype(F32)
        ).astype(BF)

    low = jnp.where(core == 0, done[True], done[False])
    high = jnp.where(core == 0, done[False], done[True])
    result = jnp.concatenate([low, high], axis=0)
    return (result[:, :width], result[:, width:], grad_in, grad_out)


def solution(mesh):
    placed = (P(("col", "dp"), "row"), P(("col", "dp"), "row"), P("row", "col"), P("col", "row"))
    return jax.shard_map(
        shards,
        mesh=mesh,
        in_specs=placed,
        out_specs=(
            P(("col", "dp"), "row"),
            P(("col", "dp"), "row"),
            P("row", ("col", "dp")),
            P(("col", "dp"), "row"),
        ),
        check_vma=False,
    )
```

```python
import functools
import math

import jax
import jax.numpy as jnp
from jax import lax
from jax.experimental import pallas as pl
from jax.experimental.pallas import tpu as pltpu
from jax.sharding import PartitionSpec as P

AXES = ("row", "col", "dp")
RING = 4
PARTS = 2
BF = jnp.bfloat16
F32 = jnp.float32
NN = (((1,), (0,)), ((), ()))
NT = (((1,), (1,)), ((), ()))
TN = (((0,), (0,)), ((), ()))


def cost(flops, bytes_accessed, transcendentals):
    return pl.CostEstimate(
        flops=flops // 1000, bytes_accessed=bytes_accessed // 1000, transcendentals=transcendentals
    )


def gelu_parts(pre):
    cdf = 0.5 * (1.0 + jax.scipy.special.erf(pre * (1.0 / math.sqrt(2.0))))
    activated = pre * cdf
    slope = cdf + pre * jnp.exp(-0.5 * pre * pre) * (1.0 / math.sqrt(2.0 * math.pi))
    return (activated, slope)


def flat(z, c, x, y):
    return ((z * 2 + c) * RING + x) * RING + y


def exchange(array, partner):
    pairs = []
    for z in range(RING):
        for c in range(2):
            for x in range(RING):
                for y in range(RING):
                    pairs.append((flat(*partner(z, c, x, y)), flat(z, c, x, y)))
    return lax.ppermute(array, AXES, pairs)


NEAR = ((1, 3), (3, 1))
Z_PAIR = ((1, 3), (3, 1))
OWNER_SLOT = ((0, 2, 3, 1), (0, 1, 3, 2))


def along(keep, first, turn):
    def partner(z, c, x, y):
        half = c if keep else 1 - c
        step = NEAR[c][turn]
        if (half == 0) == first:
            return (z, c, x ^ step, y)
        return (z, c, x, y ^ step)

    return partner


def along_z(turn):
    return lambda z, c, x, y: (z ^ Z_PAIR[c][turn], c, x, y)


def other_core(z, c, x, y):
    return (z, 1 - c, x, y)


def slot_of(keep, place_ref, i):
    z, core = place_ref[0], place_ref[1]

    def one(c):
        near = NEAR[c]
        owned = z ^ (0, near[0], near[1], near[0] ^ near[1])[i]
        table = OWNER_SLOT[c if keep else 1 - c]
        slot = jnp.int32(table[0])
        for j in range(1, RING):
            slot = jnp.where(owned == j, table[j], slot)
        return slot

    return jnp.where(core == 0, one(0), one(1))


def arrival_of(keep, place_ref, i):
    z, core = place_ref[0], place_ref[1]

    def one(c):
        near = NEAR[c]
        arrival = (0, near[0], near[1], near[0] ^ near[1])
        owned = z ^ OWNER_SLOT[c if keep else 1 - c].index(i)
        place = jnp.int32(arrival.index(0))
        for j in range(1, RING):
            place = jnp.where(owned == j, arrival.index(j), place)
        return place

    return jnp.where(core == 0, one(0), one(1))


def cut_kernel(place_ref, tokens_ref, grad_ref, kept_ref, passed_ref, sems):
    block, wide = kept_ref.shape[0], tokens_ref.shape[1]
    core = place_ref[1]
    copies = []
    for ref, which in ((kept_ref, core), (passed_ref, 1 - core)):
        rows = pl.ds(pl.multiple_of(which * block, block), block)
        for i, source in enumerate((tokens_ref, grad_ref)):
            copies.append(
                pltpu.make_async_copy(
                    source.at[rows, :],
                    ref.at[:, i * wide:(i + 1) * wide],
                    sems.at[len(copies)],
                )
            )
    for copy in copies:
        copy.start()
    for copy in copies:
        copy.wait()


def whole(kernel, place, arrays, shapes):
    return pl.pallas_call(
        kernel,
        in_specs=[pl.BlockSpec(memory_space=pltpu.SMEM)]
        + [pl.BlockSpec(memory_space=pltpu.VMEM)] * len(arrays),
        out_specs=[pl.BlockSpec(memory_space=pltpu.VMEM)] * len(shapes),
        out_shape=[jax.ShapeDtypeStruct(shape, BF) for shape in shapes],
        compiler_params=pltpu.CompilerParams(vmem_limit_bytes=8 * 2**20),
        cost_estimate=cost(flops=0, bytes_accessed=0, transcendentals=0),
    )(place, *arrays)


def cut(place, tokens, out_grad):
    rows, wide = tokens.shape
    half = jax.ShapeDtypeStruct((rows // 2, 2 * wide), BF)
    return pl.pallas_call(
        cut_kernel,
        in_specs=[pl.BlockSpec(memory_space=pltpu.SMEM)]
        + [pl.BlockSpec(memory_space=pltpu.HBM)] * 2,
        out_specs=[pl.BlockSpec(memory_space=pltpu.VMEM)] * 2,
        out_shape=[half, half],
        scratch_shapes=[pltpu.SemaphoreType.DMA((4,))],
        compiler_params=pltpu.CompilerParams(vmem_limit_bytes=8 * 2**20),
        cost_estimate=cost(flops=0, bytes_accessed=0, transcendentals=0),
    )(place, tokens, out_grad)


def put_back_kernel(place_ref, kept_ref, passed_ref, mixed_ref, grad_ref, sems):
    block, wide = kept_ref.shape[0], mixed_ref.shape[1]
    core = place_ref[1]
    copies = []
    for ref, which in ((kept_ref, core), (passed_ref, 1 - core)):
        rows = pl.ds(pl.multiple_of(which * block, block), block)
        for i, target in enumerate((mixed_ref, grad_ref)):
            copies.append(
                pltpu.make_async_copy(
                    ref.at[:, i * wide:(i + 1) * wide],
                    target.at[rows, :],
                    sems.at[len(copies)],
                )
            )
    for copy in copies:
        copy.start()
    for copy in copies:
        copy.wait()


def put_back(place, kept, passed):
    rows, wide = kept.shape
    out = jax.ShapeDtypeStruct((2 * rows, wide // 2), BF)
    return pl.pallas_call(
        put_back_kernel,
        in_specs=[pl.BlockSpec(memory_space=pltpu.SMEM)]
        + [pl.BlockSpec(memory_space=pltpu.VMEM)] * 2,
        out_specs=[pl.BlockSpec(memory_space=pltpu.HBM)] * 2,
        out_shape=[out, out],
        scratch_shapes=[pltpu.SemaphoreType.DMA((4,))],
        compiler_params=pltpu.CompilerParams(vmem_limit_bytes=8 * 2**20),
        cost_estimate=cost(flops=0, bytes_accessed=0, transcendentals=0),
    )(place, kept, passed)


def join_kernel(place_ref, a_ref, b_ref, out_ref):
    rows = a_ref.shape[0]
    out_ref[:rows, :] = a_ref[...]
    out_ref[rows:, :] = b_ref[...]


def join(place, a, b):
    return whole(join_kernel, place, [a, b], [(2 * a.shape[0], a.shape[1])])[0]


def assemble_kernel(keep, place_ref, a_ref, b_ref, c_ref, *out_refs):
    rows = a_ref.shape[0]
    part = rows // PARTS

    def put(i, ref, first):
        at = pl.multiple_of(slot_of(keep, place_ref, i) * part, part)
        for j, out_ref in enumerate(out_refs):
            out_ref[pl.ds(at, part), :] = ref[first + j * part:first + (j + 1) * part, :]

    put(0, a_ref, 0)
    put(1, b_ref, 0)
    put(2, c_ref, 0)
    put(3, c_ref, rows)


def assemble(keep, place, a, b, c):
    rows, wide = a.shape
    kernel = functools.partial(assemble_kernel, keep)
    return whole(kernel, place, [a, b, c], [(RING * rows // PARTS, wide)] * PARTS)


def order_of(keep):
    return (0, 1, 2, 3) if keep else (0, 2, 1, 3)


def panel_at(piece, slot):
    return piece // 2, (piece % 2) * RING + slot


def hidden_at(keep, piece, slot):
    return slot // 2, (slot % 2) * RING + order_of(keep).index(piece)


def pair_kernel(keep, hidden, added, split, side, block, place_ref, *refs):
    a_refs, (left_ref, right_ref), rest = refs[:2], refs[2:4], refs[4:]
    if added:
        more_ref, rest = rest[0], rest[1:]
    rows_ref = rest[-1]
    out_refs = rest[:-1]

    @pl.when(pl.program_id(1) == 0)
    def _():
        if hidden:
            size = RING * block
            for i in range(RING):
                at = pl.multiple_of(arrival_of(keep, place_ref, i) * size, size)
                first = (i % 2) * size
                rows_ref[pl.ds(at, size), :] = a_refs[i // 2][first:first + size, :]
        else:
            for i in range(RING):
                for j, piece in enumerate(order_of(keep)):
                    which, first = panel_at(piece, i)
                    at = (i * RING + j) * block
                    rows_ref[at:at + block, :] = a_refs[which][first * block:(first + 1) * block, :]

    def rows():
        if side is None:
            return rows_ref[...]
        half = rows_ref.shape[0] // 2
        return rows_ref[side * half:(side + 1) * half, :]

    def finish(total):
        if added:
            total = total + more_ref[...].astype(F32)
        total = total.astype(BF)
        if not split:
            out_refs[0][...] = total
        else:
            half = total.shape[0] // 2
            out_refs[0][...] = total[:half]
            out_refs[1][...] = total[half:]

    @pl.when(pl.program_id(0) == 0)
    def _():
        finish(lax.dot_general(rows(), left_ref[...], NN, preferred_element_type=F32))

    @pl.when(pl.program_id(0) == 1)
    def _():
        finish(lax.dot_general(rows(), right_ref[...], NT, preferred_element_type=F32))


def pair_dot(keep, hidden, pair, left, right, place, more=None, split=True, side=None, tile=512):
    rows = sum(a.shape[0] for a in pair)
    block = rows // RING // RING
    depth, wide = left.shape
    tiles = wide // tile
    in_specs = [pl.BlockSpec((a.shape[0], depth), lambda h, n, place: (0, h)) for a in pair]
    in_specs += [
        pl.BlockSpec((depth, tile), lambda h, n, place: (0, n * (1 - h) + (tiles - 1) * h)),
        pl.BlockSpec((tile, depth), lambda h, n, place: (n * h, 0)),
    ]
    out_of = lambda n_rows: pl.BlockSpec((n_rows, tile), lambda h, n, place: (0, h * tiles + n))
    args = [*pair, left, right]
    if more is not None:
        in_specs.append(out_of(rows))
        args.append(more)
    outs = [rows // 2, rows // 2] if split else [rows if side is None else rows // 2]
    result = pl.pallas_call(
        functools.partial(pair_kernel, keep, hidden, more is not None, split, side, block),
        grid_spec=pltpu.PrefetchScalarGridSpec(
            num_scalar_prefetch=1,
            grid=(2, tiles),
            in_specs=in_specs,
            out_specs=[out_of(n) for n in outs],
            scratch_shapes=[pltpu.VMEM((rows, depth), BF)],
        ),
        out_shape=[jax.ShapeDtypeStruct((n, 2 * wide), BF) for n in outs],
        compiler_params=pltpu.CompilerParams(vmem_limit_bytes=18 * 2**20),
        cost_estimate=cost(
            flops=4 * rows * depth * wide,
            bytes_accessed=4 * depth * wide + 8 * rows * wide,
            transcendentals=0,
        ),
    )(place, *args)
    return result if split else result[0]


def grad_kernel(pairs, block, factor, begun, *refs):
    lefts, rights, out_ref = refs[:4], refs[4:8], refs[-1]
    total = None
    for i, blocks in enumerate(pairs):
        right = jnp.concatenate(
            [rights[j][first * block:(first + 1) * block, :] for j, first in blocks], axis=0
        )
        term = lax.dot_general(lefts[i][...], right, TN, preferred_element_type=F32)
        total = term if total is None else total + term
    total = total * factor
    out_ref[...] = total + refs[8][...] if begun else total


def grad_dot(lefts, left_part, rights, right_part, pairs, factor, begun=None, tile=256):
    wide = lefts[0].shape[1] // 2
    tiles = wide // tile
    tokens = sum(a.shape[0] for a in lefts)
    args = [*lefts, *rights]
    in_specs = [pl.BlockSpec((a.shape[0], wide), lambda n: (0, left_part)) for a in lefts]
    in_specs += [
        pl.BlockSpec((a.shape[0], tile), lambda n: (0, right_part * tiles + n)) for a in rights
    ]
    out_spec = pl.BlockSpec((wide, tile), lambda n: (0, n))
    aliases = {}
    if begun is not None:
        aliases = {len(args): 0}
        args.append(begun)
        in_specs.append(out_spec)
    block = rights[0].shape[0] // (2 * RING)
    return pl.pallas_call(
        functools.partial(grad_kernel, pairs, block, factor, begun is not None),
        grid=(tiles,),
        in_specs=in_specs,
        out_specs=out_spec,
        out_shape=jax.ShapeDtypeStruct((wide, wide), F32),
        input_output_aliases=aliases,
        compiler_params=pltpu.CompilerParams(vmem_limit_bytes=24 * 2**20),
        cost_estimate=cost(
            flops=2 * tokens * wide * wide,
            bytes_accessed=3 * tokens * wide + 2 * wide * wide,
            transcendentals=0,
        ),
    )(*args)


def after(value, *events):
    return lax.optimization_barrier((value, *events))[0]


def shards(tokens, out_grad, weight_in, weight_out):
    core = lax.axis_index("row") % 2
    z = lax.axis_index("row") // 2
    dp = lax.axis_index("dp")
    rows, width = tokens.shape
    block = rows // 2
    inner = weight_in.shape[1] // 2
    factor = 1.0 / math.sqrt(rows * 16)
    both_ways = (True, False)

    place = jnp.stack([z, core]).astype(jnp.int32)
    w_in = lax.dynamic_slice_in_dim(weight_in, dp * inner, inner, 1)
    w_out = lax.dynamic_slice_in_dim(weight_out, dp * inner, inner, 0)

    order = (False, True)
    start, one, two, own_a, own_b = {}, {}, {}, {}, {}
    start[True], start[False] = cut(place, tokens, out_grad)
    for keep in order:
        one[keep] = exchange(start[keep], along(keep, True, 0))
    for keep in order:
        two[keep] = exchange(join(place, start[keep], one[keep]), along(keep, True, 1))
    for keep in order:
        own_a[keep], own_b[keep] = assemble(keep, place, start[keep], one[keep], two[keep])

    def others(near):
        return {keep: exchange(near[keep], along(keep, False, 1)) for keep in order}

    def panel_dot(keep, near, rest, *events, more=None):
        pair = [near[keep], after(rest[keep], *events) if events else rest[keep]]
        return pair_dot(keep, False, pair, w_in, w_out, place, more=more, split=keep)

    def out_dot(keep, pair, *events, side=None):
        pair = list(pair)
        pair[1] = after(pair[1], *events) if events else pair[1]
        return pair_dot(
            keep, True, pair, w_out, w_in, place, split=side is None, side=side
        )

    def halfway(kept, got):
        half = kept.shape[0] // 2
        sums = kept.astype(F32) + got.astype(F32)
        return [sums[:half], sums[half:]]

    def half_sum(kept, got):
        return (kept.astype(F32) + got.astype(F32)).astype(BF)

    def hidden_of(half, got):
        rows = half.shape[0] // 2
        other = jnp.concatenate([got[rows:], got[:rows]], axis=0)
        value = half.astype(F32) + other.astype(F32)
        pre, back = value[:, :width], value[:, width:]
        activated, slope = gelu_parts(pre)
        return jnp.concatenate([activated.astype(BF), (back * slope).astype(BF)], axis=1)

    def neighbours(own):
        return {keep: exchange(own[keep], along(keep, False, 0)) for keep in order}

    def joined(own, near):
        return {keep: join(place, own[keep], near[keep]) for keep in order}

    both = lax.optimization_barrier((own_a[True], own_a[False]))
    own_a = {True: both[0], False: both[1]}
    near_a = joined(own_a, neighbours(own_a))
    rest_a = others(near_a)
    near_of_b = neighbours(own_b)
    sent_a = panel_dot(False, near_a, rest_a, rest_a[True])
    kept_a, send_a = panel_dot(True, near_a, rest_a, more=exchange(sent_a, other_core))
    near_b = joined(own_b, {keep: after(near_of_b[keep], send_a) for keep in order})
    rest_b = others(near_b)
    sent_b = panel_dot(False, near_b, rest_b, rest_b[True], send_a)
    step_a = after(exchange(send_a, along_z(0)), sent_b)
    half_a = half_sum(kept_a, step_a)
    turn_a = exchange(half_a, along_z(1))
    kept_b, send_b = panel_dot(
        True, near_b, rest_b, more=exchange(sent_b, other_core)
    )
    pair_a = hidden_of(half_a, after(turn_a, send_b))
    step_b = exchange(after(send_b, turn_a), along_z(0))
    far_a = exchange(pair_a, along_z(0))
    hid_a = {True: (pair_a, far_a)}
    hid_a[False] = (exchange(pair_a, other_core), exchange(far_a, other_core))

    in_pairs, out_pairs = [], []
    for base, keep in ((0, True), (2, False)):
        for i in range(2):
            in_pairs.append(
                tuple(
                    (base + hidden_at(keep, 2 * i + p, slot)[0], hidden_at(keep, 2 * i + p, slot)[1])
                    for p in range(2)
                    for slot in range(RING)
                )
            )
            out_pairs.append(
                tuple(
                    (base + panel_at(piece, 2 * i + s)[0], panel_at(piece, 2 * i + s)[1])
                    for s in range(2)
                    for piece in order_of(keep)
                )
            )

    def grads(which, near, rest, hid, begun, *events):
        panels = [near[True], rest[True], near[False], rest[False]]
        hiddens = [*hid[True], *hid[False]]
        lefts, rights, pairs = (
            (panels, hiddens, in_pairs) if which == 0 else (hiddens, panels, out_pairs)
        )
        lefts[0] = after(lefts[0], *events)
        return grad_dot(lefts, 0, rights, 1, pairs, factor, begun)

    def second_half(keep, kept, got):
        sums = halfway(kept, got)
        return sums[0], exchange(sums[1].astype(BF), along(keep, True, 0))

    out_a, out_b, got_a, got_b = {}, {}, {}, {}
    sums_a, sums_b, last_a, last_b, total_a, total_b = {}, {}, {}, {}, {}, {}
    out_a[True] = out_dot(True, hid_a[True])
    half_b = half_sum(kept_b, after(step_b, out_a[True][0], *hid_a[False]))
    turn_b = exchange(half_b, along_z(1))
    out_a[False] = out_dot(False, hid_a[False], out_a[True][0], step_b)
    for keep in both_ways:
        got_a[keep] = exchange(out_a[keep][1], along(keep, True, 1))
    grad_in = grads(0, near_a, rest_a, hid_a, None, out_a[False][0])
    pair_b = hidden_of(half_b, after(turn_b, grad_in))
    far_b = exchange(pair_b, along_z(0))
    grad_out = grads(1, near_a, rest_a, hid_a, None, turn_b, got_a[True], got_a[False], grad_in)
    for keep in both_ways:
        got = after(got_a[keep], grad_in, got_a[not keep], pair_b)
        sums_a[keep], last_a[keep] = second_half(keep, out_a[keep][0], got)
    far_b = after(far_b, grad_out, last_a[True], last_a[False])
    hid_b = {True: (pair_b, far_b)}
    hid_b[False] = (exchange(pair_b, other_core), exchange(far_b, other_core))

    leaves, stays = {}, {}
    leaves[True] = out_dot(True, hid_b[True], hid_b[False][0], side=1)
    leaves[False] = out_dot(False, hid_b[False], leaves[True], side=1)
    stays[True] = out_dot(True, hid_b[True], leaves[False], side=0)
    stays[False] = out_dot(False, hid_b[False], stays[True], side=0)
    out_b = {keep: (stays[keep], leaves[keep]) for keep in both_ways}
    for keep in both_ways:
        got_b[keep] = exchange(out_b[keep][1], along(keep, True, 1))
    grad_in = grads(
        0, near_b, rest_b, hid_b, grad_in, out_b[False][0]
    )
    for keep in both_ways:
        got = after(got_b[keep], grad_in, got_b[not keep])
        sums_b[keep], last_b[keep] = second_half(keep, out_b[keep][0], got)
    grad_out = grads(1, near_b, rest_b, hid_b, grad_out, got_b[True], got_b[False], grad_in)
    for keep in both_ways:
        total_a[keep] = sums_a[keep] + last_a[keep].astype(F32)
        total_b[keep] = sums_b[keep] + after(last_b[keep], grad_out).astype(F32)

    part = block // PARTS
    pick = lambda keep, piece: jnp.concatenate(
        [
            total[keep][order_of(keep).index(piece) * part:(order_of(keep).index(piece) + 1) * part]
            for total in (total_a, total_b)
        ],
        axis=0,
    )
    gots, done = {}, {}
    for keep in both_ways:
        passed = jnp.concatenate([pick(keep, 2), pick(keep, 3)], axis=0).astype(BF)
        gots[keep] = exchange(passed, along(keep, False, 1))
    for keep in both_ways:
        got = gots[keep].astype(F32)
        last = (pick(keep, 1) + got[block:]).astype(BF)
        done[keep] = (
            pick(keep, 0) + got[:block] + exchange(last, along(keep, False, 0)).astype(F32)
        ).astype(BF)

    mixed, token_grad = put_back(place, done[True], done[False])
    return (mixed, token_grad, grad_in, grad_out)


def solution(mesh):
    placed = (P(("col", "dp"), "row"), P(("col", "dp"), "row"), P("row", "col"), P("col", "row"))
    return jax.shard_map(
        shards,
        mesh=mesh,
        in_specs=placed,
        out_specs=(
            P(("col", "dp"), "row"),
            P(("col", "dp"), "row"),
            P("row", ("col", "dp")),
            P(("col", "dp"), "row"),
        ),
        check_vma=False,
    )
```

```python
import functools
import math

import jax
import jax.numpy as jnp
from jax import lax
from jax.experimental import pallas as pl
from jax.experimental.pallas import tpu as pltpu
from jax.sharding import PartitionSpec as P

AXES = ("row", "col", "dp")
RING = 4
PARTS = 2
BF = jnp.bfloat16
F32 = jnp.float32
NN = (((1,), (0,)), ((), ()))
NT = (((1,), (1,)), ((), ()))
TN = (((0,), (0,)), ((), ()))


def cost(flops, bytes_accessed, transcendentals):
    return pl.CostEstimate(
        flops=flops // 1000, bytes_accessed=bytes_accessed // 1000, transcendentals=transcendentals
    )


def gelu_parts(pre):
    cdf = 0.5 * (1.0 + jax.scipy.special.erf(pre * (1.0 / math.sqrt(2.0))))
    activated = pre * cdf
    slope = cdf + pre * jnp.exp(-0.5 * pre * pre) * (1.0 / math.sqrt(2.0 * math.pi))
    return (activated, slope)


def flat(z, c, x, y):
    return ((z * 2 + c) * RING + x) * RING + y


def exchange(array, partner):
    pairs = []
    for z in range(RING):
        for c in range(2):
            for x in range(RING):
                for y in range(RING):
                    pairs.append((flat(*partner(z, c, x, y)), flat(z, c, x, y)))
    return lax.ppermute(array, AXES, pairs)


NEAR = ((1, 3), (3, 1))
Z_PAIR = ((1, 3), (3, 1))
OWNER_SLOT = ((0, 2, 3, 1), (0, 1, 3, 2))


def along(keep, first, turn):
    def partner(z, c, x, y):
        half = c if keep else 1 - c
        step = NEAR[c][turn]
        if (half == 0) == first:
            return (z, c, x ^ step, y)
        return (z, c, x, y ^ step)

    return partner


def along_z(turn):
    return lambda z, c, x, y: (z ^ Z_PAIR[c][turn], c, x, y)


def other_core(z, c, x, y):
    return (z, 1 - c, x, y)


def slot_of(keep, place_ref, i):
    z, core = place_ref[0], place_ref[1]

    def one(c):
        near = NEAR[c]
        owned = z ^ (0, near[0], near[1], near[0] ^ near[1])[i]
        table = OWNER_SLOT[c if keep else 1 - c]
        slot = jnp.int32(table[0])
        for j in range(1, RING):
            slot = jnp.where(owned == j, table[j], slot)
        return slot

    return jnp.where(core == 0, one(0), one(1))


def arrival_of(keep, place_ref, i):
    z, core = place_ref[0], place_ref[1]

    def one(c):
        near = NEAR[c]
        arrival = (0, near[0], near[1], near[0] ^ near[1])
        owned = z ^ OWNER_SLOT[c if keep else 1 - c].index(i)
        place = jnp.int32(arrival.index(0))
        for j in range(1, RING):
            place = jnp.where(owned == j, arrival.index(j), place)
        return place

    return jnp.where(core == 0, one(0), one(1))


def cut_kernel(place_ref, tokens_ref, grad_ref, kept_ref, passed_ref, sems):
    block, wide = kept_ref.shape[0], tokens_ref.shape[1]
    core = place_ref[1]
    copies = []
    for ref, which in ((kept_ref, core), (passed_ref, 1 - core)):
        rows = pl.ds(pl.multiple_of(which * block, block), block)
        for i, source in enumerate((tokens_ref, grad_ref)):
            copies.append(
                pltpu.make_async_copy(
                    source.at[rows, :],
                    ref.at[:, i * wide:(i + 1) * wide],
                    sems.at[len(copies)],
                )
            )
    for copy in copies:
        copy.start()
    for copy in copies:
        copy.wait()


def whole(kernel, place, arrays, shapes):
    return pl.pallas_call(
        kernel,
        in_specs=[pl.BlockSpec(memory_space=pltpu.SMEM)]
        + [pl.BlockSpec(memory_space=pltpu.VMEM)] * len(arrays),
        out_specs=[pl.BlockSpec(memory_space=pltpu.VMEM)] * len(shapes),
        out_shape=[jax.ShapeDtypeStruct(shape, BF) for shape in shapes],
        compiler_params=pltpu.CompilerParams(vmem_limit_bytes=8 * 2**20),
        cost_estimate=cost(flops=0, bytes_accessed=0, transcendentals=0),
    )(place, *arrays)


def cut(place, tokens, out_grad):
    rows, wide = tokens.shape
    half = jax.ShapeDtypeStruct((rows // 2, 2 * wide), BF)
    return pl.pallas_call(
        cut_kernel,
        in_specs=[pl.BlockSpec(memory_space=pltpu.SMEM)]
        + [pl.BlockSpec(memory_space=pltpu.HBM)] * 2,
        out_specs=[pl.BlockSpec(memory_space=pltpu.VMEM)] * 2,
        out_shape=[half, half],
        scratch_shapes=[pltpu.SemaphoreType.DMA((4,))],
        compiler_params=pltpu.CompilerParams(vmem_limit_bytes=8 * 2**20),
        cost_estimate=cost(flops=0, bytes_accessed=0, transcendentals=0),
    )(place, tokens, out_grad)


def put_back_kernel(place_ref, kept_ref, passed_ref, mixed_ref, grad_ref, sems):
    block, wide = kept_ref.shape[0], mixed_ref.shape[1]
    core = place_ref[1]
    copies = []
    for ref, which in ((kept_ref, core), (passed_ref, 1 - core)):
        rows = pl.ds(pl.multiple_of(which * block, block), block)
        for i, target in enumerate((mixed_ref, grad_ref)):
            copies.append(
                pltpu.make_async_copy(
                    ref.at[:, i * wide:(i + 1) * wide],
                    target.at[rows, :],
                    sems.at[len(copies)],
                )
            )
    for copy in copies:
        copy.start()
    for copy in copies:
        copy.wait()


def put_back(place, kept, passed):
    rows, wide = kept.shape
    out = jax.ShapeDtypeStruct((2 * rows, wide // 2), BF)
    return pl.pallas_call(
        put_back_kernel,
        in_specs=[pl.BlockSpec(memory_space=pltpu.SMEM)]
        + [pl.BlockSpec(memory_space=pltpu.VMEM)] * 2,
        out_specs=[pl.BlockSpec(memory_space=pltpu.HBM)] * 2,
        out_shape=[out, out],
        scratch_shapes=[pltpu.SemaphoreType.DMA((4,))],
        compiler_params=pltpu.CompilerParams(vmem_limit_bytes=8 * 2**20),
        cost_estimate=cost(flops=0, bytes_accessed=0, transcendentals=0),
    )(place, kept, passed)


def join_kernel(place_ref, a_ref, b_ref, out_ref):
    rows = a_ref.shape[0]
    out_ref[:rows, :] = a_ref[...]
    out_ref[rows:, :] = b_ref[...]


def join(place, a, b):
    return whole(join_kernel, place, [a, b], [(2 * a.shape[0], a.shape[1])])[0]


def assemble_kernel(keep, place_ref, a_ref, b_ref, c_ref, *out_refs):
    rows = a_ref.shape[0]
    part = rows // PARTS

    def put(i, ref, first):
        at = pl.multiple_of(slot_of(keep, place_ref, i) * part, part)
        for j, out_ref in enumerate(out_refs):
            out_ref[pl.ds(at, part), :] = ref[first + j * part:first + (j + 1) * part, :]

    put(0, a_ref, 0)
    put(1, b_ref, 0)
    put(2, c_ref, 0)
    put(3, c_ref, rows)


def assemble(keep, place, a, b, c):
    rows, wide = a.shape
    kernel = functools.partial(assemble_kernel, keep)
    return whole(kernel, place, [a, b, c], [(RING * rows // PARTS, wide)] * PARTS)


def order_of(keep):
    return (0, 1, 2, 3) if keep else (0, 2, 1, 3)


def panel_at(piece, slot):
    return piece // 2, (piece % 2) * RING + slot


def hidden_at(keep, piece, slot):
    return slot // 2, (slot % 2) * RING + order_of(keep).index(piece)


def pair_kernel(keep, hidden, added, split, side, block, place_ref, *refs):
    a_refs, (left_ref, right_ref), rest = refs[:2], refs[2:4], refs[4:]
    if added:
        more_ref, rest = rest[0], rest[1:]
    rows_ref = rest[-1]
    out_refs = rest[:-1]

    @pl.when(pl.program_id(1) == 0)
    def _():
        if hidden:
            size = RING * block
            for i in range(RING):
                at = pl.multiple_of(arrival_of(keep, place_ref, i) * size, size)
                first = (i % 2) * size
                rows_ref[pl.ds(at, size), :] = a_refs[i // 2][first:first + size, :]
        else:
            for i in range(RING):
                for j, piece in enumerate(order_of(keep)):
                    which, first = panel_at(piece, i)
                    at = (i * RING + j) * block
                    rows_ref[at:at + block, :] = a_refs[which][first * block:(first + 1) * block, :]

    def rows():
        if side is None:
            return rows_ref[...]
        half = rows_ref.shape[0] // 2
        return rows_ref[side * half:(side + 1) * half, :]

    def finish(total):
        if added:
            total = total + more_ref[...].astype(F32)
        total = total.astype(BF)
        if not split:
            out_refs[0][...] = total
        else:
            half = total.shape[0] // 2
            out_refs[0][...] = total[:half]
            out_refs[1][...] = total[half:]

    @pl.when(pl.program_id(0) == 0)
    def _():
        finish(lax.dot_general(rows(), left_ref[...], NN, preferred_element_type=F32))

    @pl.when(pl.program_id(0) == 1)
    def _():
        finish(lax.dot_general(rows(), right_ref[...], NT, preferred_element_type=F32))


def pair_dot(keep, hidden, pair, left, right, place, more=None, split=True, side=None, tile=512):
    rows = sum(a.shape[0] for a in pair)
    block = rows // RING // RING
    depth, wide = left.shape
    tiles = wide // tile
    in_specs = [pl.BlockSpec((a.shape[0], depth), lambda h, n, place: (0, h)) for a in pair]
    in_specs += [
        pl.BlockSpec((depth, tile), lambda h, n, place: (0, n * (1 - h) + (tiles - 1) * h)),
        pl.BlockSpec((tile, depth), lambda h, n, place: (n * h, 0)),
    ]
    out_of = lambda n_rows: pl.BlockSpec((n_rows, tile), lambda h, n, place: (0, h * tiles + n))
    args = [*pair, left, right]
    if more is not None:
        in_specs.append(out_of(rows))
        args.append(more)
    outs = [rows // 2, rows // 2] if split else [rows if side is None else rows // 2]
    result = pl.pallas_call(
        functools.partial(pair_kernel, keep, hidden, more is not None, split, side, block),
        grid_spec=pltpu.PrefetchScalarGridSpec(
            num_scalar_prefetch=1,
            grid=(2, tiles),
            in_specs=in_specs,
            out_specs=[out_of(n) for n in outs],
            scratch_shapes=[pltpu.VMEM((rows, depth), BF)],
        ),
        out_shape=[jax.ShapeDtypeStruct((n, 2 * wide), BF) for n in outs],
        compiler_params=pltpu.CompilerParams(vmem_limit_bytes=18 * 2**20),
        cost_estimate=cost(
            flops=4 * rows * depth * wide,
            bytes_accessed=4 * depth * wide + 8 * rows * wide,
            transcendentals=0,
        ),
    )(place, *args)
    return result if split else result[0]


def grad_kernel(pairs, block, factor, begun, *refs):
    lefts, rights, out_ref = refs[:4], refs[4:8], refs[-1]
    total = None
    for i, blocks in enumerate(pairs):
        right = jnp.concatenate(
            [rights[j][first * block:(first + 1) * block, :] for j, first in blocks], axis=0
        )
        term = lax.dot_general(lefts[i][...], right, TN, preferred_element_type=F32)
        total = term if total is None else total + term
    total = total * factor
    out_ref[...] = total + refs[8][...] if begun else total


def grad_dot(lefts, left_part, rights, right_part, pairs, factor, begun=None, tile=512):
    wide = lefts[0].shape[1] // 2
    tiles = wide // tile
    tokens = sum(a.shape[0] for a in lefts)
    args = [*lefts, *rights]
    in_specs = [pl.BlockSpec((a.shape[0], wide), lambda n: (0, left_part)) for a in lefts]
    in_specs += [
        pl.BlockSpec((a.shape[0], tile), lambda n: (0, right_part * tiles + n)) for a in rights
    ]
    out_spec = pl.BlockSpec((wide, tile), lambda n: (0, n))
    aliases = {}
    if begun is not None:
        aliases = {len(args): 0}
        args.append(begun)
        in_specs.append(out_spec)
    block = rights[0].shape[0] // (2 * RING)
    return pl.pallas_call(
        functools.partial(grad_kernel, pairs, block, factor, begun is not None),
        grid=(tiles,),
        in_specs=in_specs,
        out_specs=out_spec,
        out_shape=jax.ShapeDtypeStruct((wide, wide), F32),
        input_output_aliases=aliases,
        compiler_params=pltpu.CompilerParams(vmem_limit_bytes=30 * 2**20),
        cost_estimate=cost(
            flops=2 * tokens * wide * wide,
            bytes_accessed=3 * tokens * wide + 2 * wide * wide,
            transcendentals=0,
        ),
    )(*args)


def after(value, *events):
    return lax.optimization_barrier((value, *events))[0]


def shards(tokens, out_grad, weight_in, weight_out):
    core = lax.axis_index("row") % 2
    z = lax.axis_index("row") // 2
    dp = lax.axis_index("dp")
    rows, width = tokens.shape
    block = rows // 2
    inner = weight_in.shape[1] // 2
    factor = 1.0 / math.sqrt(rows * 16)
    both_ways = (True, False)

    place = jnp.stack([z, core]).astype(jnp.int32)
    w_in = lax.dynamic_slice_in_dim(weight_in, dp * inner, inner, 1)
    w_out = lax.dynamic_slice_in_dim(weight_out, dp * inner, inner, 0)

    order = (False, True)
    start, one, two, own_a, own_b = {}, {}, {}, {}, {}
    start[True], start[False] = cut(place, tokens, out_grad)
    for keep in order:
        one[keep] = exchange(start[keep], along(keep, True, 0))
    for keep in order:
        two[keep] = exchange(join(place, start[keep], one[keep]), along(keep, True, 1))
    for keep in order:
        own_a[keep], own_b[keep] = assemble(keep, place, start[keep], one[keep], two[keep])

    def others(near):
        return {keep: exchange(near[keep], along(keep, False, 1)) for keep in order}

    def panel_dot(keep, near, rest, *events, more=None):
        pair = [near[keep], after(rest[keep], *events) if events else rest[keep]]
        return pair_dot(keep, False, pair, w_in, w_out, place, more=more, split=keep)

    def out_dot(keep, pair, *events, side=None):
        pair = list(pair)
        pair[1] = after(pair[1], *events) if events else pair[1]
        return pair_dot(
            keep, True, pair, w_out, w_in, place, split=side is None, side=side
        )

    def halfway(kept, got):
        half = kept.shape[0] // 2
        sums = kept.astype(F32) + got.astype(F32)
        return [sums[:half], sums[half:]]

    def half_sum(kept, got):
        return (kept.astype(F32) + got.astype(F32)).astype(BF)

    def hidden_of(half, got):
        rows = half.shape[0] // 2
        other = jnp.concatenate([got[rows:], got[:rows]], axis=0)
        value = half.astype(F32) + other.astype(F32)
        pre, back = value[:, :width], value[:, width:]
        activated, slope = gelu_parts(pre)
        return jnp.concatenate([activated.astype(BF), (back * slope).astype(BF)], axis=1)

    def neighbours(own):
        return {keep: exchange(own[keep], along(keep, False, 0)) for keep in order}

    def joined(own, near):
        return {keep: join(place, own[keep], near[keep]) for keep in order}

    both = lax.optimization_barrier((own_a[True], own_a[False]))
    own_a = {True: both[0], False: both[1]}
    near_a = joined(own_a, neighbours(own_a))
    rest_a = others(near_a)
    near_of_b = neighbours(own_b)
    sent_a = panel_dot(False, near_a, rest_a, rest_a[True])
    kept_a, send_a = panel_dot(True, near_a, rest_a, more=exchange(sent_a, other_core))
    near_b = joined(own_b, {keep: after(near_of_b[keep], send_a) for keep in order})
    rest_b = others(near_b)
    sent_b = panel_dot(False, near_b, rest_b, rest_b[True], send_a)
    step_a = after(exchange(send_a, along_z(0)), sent_b)
    half_a = half_sum(kept_a, step_a)
    turn_a = exchange(half_a, along_z(1))
    kept_b, send_b = panel_dot(
        True, near_b, rest_b, more=exchange(sent_b, other_core)
    )
    pair_a = hidden_of(half_a, after(turn_a, send_b))
    step_b = exchange(after(send_b, turn_a), along_z(0))
    far_a = exchange(pair_a, along_z(0))
    hid_a = {True: (pair_a, far_a)}
    hid_a[False] = (exchange(pair_a, other_core), exchange(far_a, other_core))

    in_pairs, out_pairs = [], []
    for base, keep in ((0, True), (2, False)):
        for i in range(2):
            in_pairs.append(
                tuple(
                    (base + hidden_at(keep, 2 * i + p, slot)[0], hidden_at(keep, 2 * i + p, slot)[1])
                    for p in range(2)
                    for slot in range(RING)
                )
            )
            out_pairs.append(
                tuple(
                    (base + panel_at(piece, 2 * i + s)[0], panel_at(piece, 2 * i + s)[1])
                    for s in range(2)
                    for piece in order_of(keep)
                )
            )

    def grads(which, near, rest, hid, begun, *events):
        panels = [near[True], rest[True], near[False], rest[False]]
        hiddens = [*hid[True], *hid[False]]
        lefts, rights, pairs = (
            (panels, hiddens, in_pairs) if which == 0 else (hiddens, panels, out_pairs)
        )
        lefts[0] = after(lefts[0], *events)
        return grad_dot(lefts, 0, rights, 1, pairs, factor, begun)

    def second_half(keep, kept, got):
        sums = halfway(kept, got)
        return sums[0], exchange(sums[1].astype(BF), along(keep, True, 0))

    out_a, out_b, got_a, got_b = {}, {}, {}, {}
    sums_a, sums_b, last_a, last_b, total_a, total_b = {}, {}, {}, {}, {}, {}
    out_a[True] = out_dot(True, hid_a[True])
    half_b = half_sum(kept_b, after(step_b, out_a[True][0], *hid_a[False]))
    turn_b = exchange(half_b, along_z(1))
    out_a[False] = out_dot(False, hid_a[False], out_a[True][0], step_b)
    for keep in both_ways:
        got_a[keep] = exchange(out_a[keep][1], along(keep, True, 1))
    grad_in = grads(0, near_a, rest_a, hid_a, None, out_a[False][0])
    pair_b = hidden_of(half_b, after(turn_b, grad_in))
    far_b = exchange(pair_b, along_z(0))
    grad_out = grads(1, near_a, rest_a, hid_a, None, turn_b, got_a[True], got_a[False], grad_in)
    for keep in both_ways:
        got = after(got_a[keep], grad_in, got_a[not keep], pair_b)
        sums_a[keep], last_a[keep] = second_half(keep, out_a[keep][0], got)
    far_b = after(far_b, grad_out, last_a[True], last_a[False])
    hid_b = {True: (pair_b, far_b)}
    hid_b[False] = (exchange(pair_b, other_core), exchange(far_b, other_core))

    leaves, stays = {}, {}
    leaves[True] = out_dot(True, hid_b[True], hid_b[False][0], side=1)
    leaves[False] = out_dot(False, hid_b[False], leaves[True], side=1)
    stays[True] = out_dot(True, hid_b[True], leaves[False], side=0)
    stays[False] = out_dot(False, hid_b[False], stays[True], side=0)
    out_b = {keep: (stays[keep], leaves[keep]) for keep in both_ways}
    for keep in both_ways:
        got_b[keep] = exchange(out_b[keep][1], along(keep, True, 1))
    grad_in = grads(
        0, near_b, rest_b, hid_b, grad_in, out_b[False][0]
    )
    for keep in both_ways:
        got = after(got_b[keep], grad_in, got_b[not keep])
        sums_b[keep], last_b[keep] = second_half(keep, out_b[keep][0], got)
    grad_out = grads(1, near_b, rest_b, hid_b, grad_out, got_b[True], got_b[False], grad_in)
    for keep in both_ways:
        total_a[keep] = sums_a[keep] + last_a[keep].astype(F32)
        total_b[keep] = sums_b[keep] + after(last_b[keep], grad_out).astype(F32)

    part = block // PARTS
    pick = lambda keep, piece: jnp.concatenate(
        [
            total[keep][order_of(keep).index(piece) * part:(order_of(keep).index(piece) + 1) * part]
            for total in (total_a, total_b)
        ],
        axis=0,
    )
    gots, done = {}, {}
    for keep in both_ways:
        passed = jnp.concatenate([pick(keep, 2), pick(keep, 3)], axis=0).astype(BF)
        gots[keep] = exchange(passed, along(keep, False, 1))
    for keep in both_ways:
        got = gots[keep].astype(F32)
        last = (pick(keep, 1) + got[block:]).astype(BF)
        done[keep] = (
            pick(keep, 0) + got[:block] + exchange(last, along(keep, False, 0)).astype(F32)
        ).astype(BF)

    mixed, token_grad = put_back(place, done[True], done[False])
    return (mixed, token_grad, grad_in, grad_out)


def solution(mesh):
    placed = (P(("col", "dp"), "row"), P(("col", "dp"), "row"), P("row", "col"), P("col", "row"))
    return jax.shard_map(
        shards,
        mesh=mesh,
        in_specs=placed,
        out_specs=(
            P(("col", "dp"), "row"),
            P(("col", "dp"), "row"),
            P("row", ("col", "dp")),
            P(("col", "dp"), "row"),
        ),
        check_vma=False,
    )
```
